256 devices in a mesh: band: 32 (over z_hi, x, core), grid: 8 (over y, z_lo).
Axes of the slice: x: 4, y: 4, z: 8 (z_hi: 4, z_lo: 2; z = z_hi * 2 + z_lo), core: 2. Of those that a mesh axis runs over, the one named last changes fastest.
Arguments:
- orbitals: bfloat16 [64, 192, 36864], P('band', 'grid'), may hold values from -6 to 6
Outputs:
- exchange_applied: float32 [32, 192, 36864], P('band', 'grid')
The draws below stay inside these ranges and needn't reach their ends.
All inputs are finite; a program needn't handle non-finite values.
Results may differ from the reference program's by a relative error of at most 0.0062.
Values may be sent and summed in bfloat16 or wider, within the bound.
No kernel may reach another device: no remote copies, remote signals or barrier semaphores. Data moves between devices by JAX's collectives and lax.ppermute only.
A program may use at most 128 MiB of HBM per device.

```python
import jax
import jax.numpy as jnp
from jax import lax

SIDE = 192
BLOCK = 2
STEPS = 2
TGT_DEV = 1
ORBS = 64
TARGETS = 32
N_BAND = 32


def level_of(rng, dims, cuts, smallest, top_value):
    def one(position, parts):
        heights = jax.random.uniform(jax.random.fold_in(jax.random.fold_in(rng, 6), position), (parts,), jnp.float32, smallest / len(cuts), top_value / len(cuts))
        return jnp.repeat(jnp.exp(heights), dims[position] // parts).reshape((-1,) + (1,) * (len(dims) - position - 1))

    loudness = one(*cuts[0])
    for cut in cuts[1:]:
        loudness = loudness * one(*cut)
    return loudness


def bell_draw(key, shape, scale, limit, split=(), kind=jnp.bfloat16):
    factor_of = level_of(key, shape, split, -0.22, 0.18) if split else 1.0
    array = jax.random.normal(key, shape, jnp.float32) * scale * factor_of
    return jnp.minimum(jnp.maximum(array, -limit), limit).astype(kind)


def setup_inputs(seed: int = 0) -> dict:
    streams_of = jax.random.split(jax.random.key(seed), 2)
    return {
        "orbitals": bell_draw(streams_of[0], (ORBS, SIDE, SIDE * SIDE), 1.0, 6.0, ((0, 32), (1, 8))),
    }


COUL = 160.0


def cas_matrix(count):
    indices = jnp.arange(count, dtype=jnp.int32)
    products = (indices[:, None] * indices[None, :]) % count
    phases = products.astype(jnp.float32) * (2.0 * jnp.pi / count)
    return (jnp.cos(phases) + jnp.sin(phases)).astype(jnp.bfloat16)


def coulomb_kernel(count):
    indices = jnp.arange(count, dtype=jnp.int32)
    wave_num = jnp.where(indices < count // 2, indices, indices - count).astype(jnp.float32)
    squared = wave_num * wave_num
    norm_sq = squared[:, None, None] + squared[None, :, None] + squared[None, None, :]
    bounded = jnp.maximum(norm_sq, 1.0)
    return jnp.where(norm_sq > 0.5, COUL / bounded, 0.0) / float(count) ** 3


def contract(pattern, values, cas_table):
    return jnp.einsum(pattern, values.astype(jnp.float32), cas_table.astype(jnp.float32), precision=lax.Precision.HIGHEST)


def convolve(density, cas_table, kernel):
    along_z = contract('pxyz,kz->pxyk', density, cas_table).astype(jnp.bfloat16)
    along_y = contract('pxyz,ky->pxkz', along_z, cas_table).astype(jnp.bfloat16)
    spectrum = (kernel[None] * contract('pxyz,kx->pkyz', along_y, cas_table)).astype(jnp.bfloat16)
    back_x = contract('pkyz,xk->pxyz', spectrum, cas_table).astype(jnp.bfloat16)
    back_y = contract('pxkz,yk->pxyz', back_x, cas_table).astype(jnp.bfloat16)
    return contract('pxyk,zk->pxyz', back_y, cas_table)


def reference(orbitals):
    cas_table = cas_matrix(SIDE)
    kernel = coulomb_kernel(SIDE)
    fields = orbitals.reshape(N_BAND, BLOCK, SIDE, SIDE, SIDE)
    targets = fields[:, :TGT_DEV].reshape(TARGETS, SIDE, SIDE, SIDE)
    blocks = [fields[(step_no * N_BAND) // STEPS] for step_no in range(STEPS)]

    def apply_one(target):
        result = jnp.zeros((SIDE, SIDE, SIDE), jnp.float32)
        target_wide = target.astype(jnp.float32)
        for sources in blocks:
            sources_wide = sources.astype(jnp.float32)
            density = (target_wide[None] * sources_wide).astype(jnp.bfloat16)
            potential = convolve(density, cas_table, kernel)
            result = result - jnp.sum(potential * sources_wide, axis=0)
        return result

    applied = lax.map(apply_one, targets)
    return applied.reshape(TARGETS, SIDE, SIDE * SIDE)
```

```python
import jax
import jax.numpy as jnp
from jax import lax
from jax.experimental import pallas as pl
from jax.experimental.pallas import tpu as pltpu
from jax.sharding import PartitionSpec as P

SIDE = 192
PARTS = 8
ROWS = SIDE // PARTS
QUADS = ROWS // 4
COUL = 160.0
F32 = jnp.float32
BF16 = jnp.bfloat16


def cas_of(left, right):
    products = left[:, None] * right[None, :] % SIDE
    phases = products.astype(F32) * (2.0 * jnp.pi / SIDE)
    return (jnp.cos(phases) + jnp.sin(phases)).astype(BF16)


def wave(index):
    return jnp.where(index < SIDE // 2, index, index - SIDE).astype(F32)


def tables(me):
    natural = jnp.arange(SIDE, dtype=jnp.int32)
    partner = me ^ jnp.arange(PARTS, dtype=jnp.int32)
    by_partner = (partner[:, None] * ROWS + jnp.arange(ROWS, dtype=jnp.int32)[None]).reshape(-1)
    stacked = by_partner.reshape(SIDE // 2, 2).T.reshape(-1)
    return cas_of(by_partner, natural), cas_of(natural, by_partner), cas_of(natural, stacked), cas_of(stacked, natural)


def z_tables():
    natural = jnp.arange(SIDE, dtype=jnp.int32)
    cas = cas_of(natural, natural)
    gap = jnp.zeros((SIDE, 64), BF16)
    first = jnp.concatenate([cas, gap], axis=1)
    second = jnp.concatenate([cas[:, :128], gap, cas[:, 128:]], axis=1)
    return first, second, first.T, second.T


def coulomb(me):
    shape = (ROWS // 2, SIDE, 384)
    pair = lax.broadcasted_iota(jnp.int32, shape, 0)
    row = lax.broadcasted_iota(jnp.int32, shape, 1)
    col = lax.broadcasted_iota(jnp.int32, shape, 2)
    late = jnp.where(col < 256, col >= 128, col >= 320)
    kz = jnp.where(col < 256, col % 128, 128 + col % 64)
    ky = me * ROWS + pair + jnp.where(late, ROWS // 2, 0)
    mx, my, mz = wave(row), wave(ky), wave(kz)
    norm_sq = mx * mx + my * my + mz * mz
    bounded = jnp.maximum(norm_sq, 1.0)
    return jnp.where(norm_sq > 0.5, COUL / bounded, 0.0) / float(SIDE) ** 3


def dot(left, right):
    return jnp.dot(left, right, preferred_element_type=F32)


def forward_body(target, source, z_first, z_second, y_table, *outs):
    lanes = []
    for pair in range(2):
        halves = []
        for plane, table in ((2 * pair, z_first), (2 * pair + 1, z_second)):
            density = (target[plane].astype(F32) * source[0, plane].astype(F32)).astype(BF16)
            halves.append(dot(density, table[...]))
        low, high = halves
        packed = jnp.concatenate([low[:, :128], high[:, :128], low[:, 128:] + high[:, 128:]], axis=1)
        lanes.append(dot(y_table[...], packed.astype(BF16)))
    for part, out in enumerate(outs):
        rows = slice(part * ROWS, (part + 1) * ROWS)
        out[0, 0] = jnp.concatenate([lanes[0][rows], lanes[1][rows]], axis=0).astype(BF16)


def whole(shape):
    return pl.BlockSpec(shape, lambda *_: (0,) * len(shape))


def forward(target, sources, z_first, z_second, y_table):
    pairs = sources.shape[0]
    piece = jax.ShapeDtypeStruct((pairs, QUADS, 2 * ROWS, 384), BF16)
    return pl.pallas_call(
        forward_body,
        grid=(pairs, QUADS),
        in_specs=[
            pl.BlockSpec((4, SIDE, SIDE), lambda p, q: (q, 0, 0)),
            pl.BlockSpec((1, 4, SIDE, SIDE), lambda p, q: (p, q, 0, 0)),
            whole((SIDE, 256)),
            whole((SIDE, 256)),
            whole((SIDE, SIDE)),
        ],
        out_specs=[pl.BlockSpec((1, 1, 2 * ROWS, 384), lambda p, q: (p, q, 0, 0))] * PARTS,
        out_shape=[piece] * PARTS,
        compiler_params=pltpu.CompilerParams(vmem_limit_bytes=32 * 2**20),
        cost_estimate=pl.CostEstimate(flops=pairs * 1400 * 10**6, bytes_accessed=pairs * 7 * 10**6, transcendentals=0),
        name="forward_zy",
    )(target, sources, z_first, z_second, y_table)


def middle_body(*refs):
    ins, (kernel, x_table, x_back), outs, (head0, head1, tail) = refs[:8], refs[8:11], refs[11:19], refs[19:]
    lots = (head0, head1, tail)
    block = QUADS * 2 * ROWS
    for part, ref in enumerate(ins):
        for tile, lot in enumerate(lots):
            lot[part * block : (part + 1) * block] = (
                ref[0, :, :, tile * 128 : (tile + 1) * 128].astype(F32).reshape(block, 128)
            )
    low = lax.broadcasted_iota(jnp.int32, (96, 128), 1) < 64

    def step(i, carry):
        here = pl.ds(i, 96, stride=ROWS)
        there = pl.ds(i + ROWS // 2, 96, stride=ROWS)
        tail_a, tail_b = tail[here, :], tail[there, :]
        tail_first = jnp.where(low, tail_a, pltpu.roll(tail_b, 64, 1))
        tail_second = jnp.where(low, pltpu.roll(tail_a, 64, 1), tail_b)
        columns = jnp.concatenate(
            [
                jnp.concatenate([head0[here, :], head0[there, :], tail_first], axis=1),
                jnp.concatenate([head1[here, :], head1[there, :], tail_second], axis=1),
            ],
            axis=0,
        ).astype(BF16)
        spectrum = (kernel[i] * dot(x_table[...], columns)).astype(BF16)
        back = dot(x_back[...], spectrum)
        head0[here, :] = back[:96, :128]
        head1[here, :] = back[96:, :128]
        head0[there, :] = back[:96, 128:256]
        head1[there, :] = back[96:, 128:256]
        first, second = back[:96, 256:], back[96:, 256:]
        tail[here, :] = jnp.where(low, first, pltpu.roll(second, 64, 1))
        tail[there, :] = jnp.where(low, pltpu.roll(first, 64, 1), second)
        return carry

    lax.fori_loop(0, ROWS // 2, step, 0)
    for part, ref in enumerate(outs):
        for tile, lot in enumerate(lots):
            ref[0, :, :, tile * 128 : (tile + 1) * 128] = (
                lot[part * block : (part + 1) * block].astype(BF16).reshape(QUADS, 2 * ROWS, 128)
            )


def middle(pieces, kernel, x_table, x_back):
    pairs = pieces[0].shape[0]
    spec = pl.BlockSpec((1, QUADS, 2 * ROWS, 384), lambda p: (p, 0, 0, 0))
    return pl.pallas_call(
        middle_body,
        grid=(pairs,),
        in_specs=[spec] * PARTS + [whole(kernel.shape), whole((SIDE, SIDE)), whole((SIDE, SIDE))],
        out_specs=[spec] * PARTS,
        out_shape=[jax.ShapeDtypeStruct(pieces[0].shape, BF16)] * PARTS,
        scratch_shapes=[pltpu.VMEM((SIDE // 2 * ROWS, 128), F32)] * 3,
        compiler_params=pltpu.CompilerParams(vmem_limit_bytes=40 * 2**20),
        cost_estimate=pl.CostEstimate(flops=pairs * 1400 * 10**6, bytes_accessed=pairs * 7 * 10**6, transcendentals=0),
        name="middle_x",
    )(*pieces, kernel, x_table, x_back)


def backward_body(*refs):
    ins, (sources, total, y_table, z_first, z_second), out = refs[:8], refs[8:13], refs[13]
    pairs = sources.shape[0]
    for pair in range(2):
        sums = [total[2 * pair], total[2 * pair + 1]]
        for which in range(pairs):
            rows = slice(pair * ROWS, (pair + 1) * ROWS)
            stack = jnp.concatenate([ref[which, 0].astype(F32)[rows] for ref in ins], axis=0).astype(BF16)
            planes = dot(y_table[...], stack).astype(BF16)
            first = dot(jnp.concatenate([planes[:, :128], planes[:, 256:]], axis=1), z_first[...])
            second = dot(planes[:, 128:], z_second[...])
            sums[0] = sums[0] - first * sources[which, 2 * pair].astype(F32)
            sums[1] = sums[1] - second * sources[which, 2 * pair + 1].astype(F32)
        out[2 * pair] = sums[0]
        out[2 * pair + 1] = sums[1]


def backward(pieces, sources, total, y_table, z_first, z_second):
    pairs = sources.shape[0]
    piece = pl.BlockSpec((pairs, 1, 2 * ROWS, 384), lambda q: (0, q, 0, 0))
    wide = pl.BlockSpec((4, SIDE, SIDE), lambda q: (q, 0, 0))
    return pl.pallas_call(
        backward_body,
        grid=(QUADS,),
        in_specs=[piece] * PARTS
        + [
            pl.BlockSpec((pairs, 4, SIDE, SIDE), lambda q: (0, q, 0, 0)),
            wide,
            whole((SIDE, SIDE)),
            whole((256, SIDE)),
            whole((256, SIDE)),
        ],
        out_specs=wide,
        out_shape=jax.ShapeDtypeStruct((ROWS, SIDE, SIDE), F32),
        compiler_params=pltpu.CompilerParams(vmem_limit_bytes=40 * 2**20),
        cost_estimate=pl.CostEstimate(flops=pairs * 1400 * 10**6, bytes_accessed=pairs * 7 * 10**6, transcendentals=0),
        name="backward_yz",
    )(*pieces, sources, total, y_table, z_first, z_second)


def exchange(pieces):
    return [pieces[0]] + [
        lax.ppermute(pieces[d], "grid", [(i, i ^ d) for i in range(PARTS)]) for d in range(1, PARTS)
    ]


def band_of(z_hi, x, core):
    return z_hi * 8 + x * 2 + core


def spread(orbitals):
    band = lax.axis_index("band")
    z_hi, x = band // 8, (band // 2) % 4
    core = band % 2
    cut = orbitals.shape[2] // 4
    chunks = orbitals.reshape(2, ROWS, 4, cut)
    mine = jnp.where(x == 0, chunks[:, :, 0], jnp.zeros((), BF16))
    for step in range(1, 4):
        pairs = [(band_of(z, 0, 0), band_of(z, step, 0)) for z in (0, 2)]
        mine = mine + lax.ppermute(chunks[:, :, step], "band", pairs)
    swap = [(band_of(z, i, 0), band_of(z, i, 1)) for z in (0, 2) for i in range(4)]
    other = lax.ppermute(mine[..., cut // 2 :], "band", swap)
    mine = jnp.where(core == 0, mine[..., : cut // 2], other)
    got = []
    for moves in (((0, 1), (2, 3)), ((0, 3), (2, 1)), ((0, 2), (2, 0))):
        pairs = [(band_of(a, i, c), band_of(b, i, c)) for a, b in moves for i in range(4) for c in range(2)]
        got.append(lax.ppermute(mine, "band", pairs))
    near, far, cross = got
    from_first = jnp.where(z_hi == 0, mine, jnp.where(z_hi == 1, near, jnp.where(z_hi == 2, cross, far)))
    from_second = jnp.where(z_hi == 2, mine, jnp.where(z_hi == 3, near, jnp.where(z_hi == 0, cross, far)))
    both = jnp.stack([from_first, from_second], axis=1)
    groups = [[8 * k + i for i in range(8)] for k in range(4)]
    gathered = [
        lax.all_gather(both[p], "band", axis=0, axis_index_groups=groups)
        for p in range(2)
    ]
    return [
        jnp.moveaxis(g.reshape(8, 2, ROWS, ROWS, SIDE), 0, 2).reshape(2, ROWS, SIDE, SIDE) for g in gathered
    ]


def local(orbitals):
    me = lax.axis_index("grid")
    y_table, y_back, x_table, x_back = tables(me)
    z_first, z_second, z_first_back, z_second_back = z_tables()
    kernel = coulomb(me)
    target = orbitals[0].reshape(ROWS, SIDE, SIDE)
    total = jnp.zeros((ROWS, SIDE, SIDE), F32)
    batches = spread(orbitals)
    backs = []
    for sources in batches:
        pieces = exchange(forward(target, sources, z_first, z_second, y_table))
        backs.append(exchange(middle(pieces, kernel, x_table, x_back)))
    for pieces, sources in zip(backs, batches):
        total = backward(pieces, sources, total, y_back, z_first_back, z_second_back)
    return total.reshape(1, ROWS, SIDE * SIDE)


def solution(mesh):
    return jax.shard_map(
        local,
        mesh=mesh,
        in_specs=(P("band", "grid", None),),
        out_specs=P("band", "grid", None),
        check_vma=False,
    )
```

```python
import jax
import jax.numpy as jnp
import numpy as np
from jax import lax
from jax.experimental import pallas as pl
from jax.experimental.pallas import tpu as pltpu
from jax.sharding import PartitionSpec as P

SIDE = 192
PARTS = 8
ROWS = SIDE // PARTS
QUADS = ROWS // 4
DUOS = SIDE // 2
CELLS = SIDE * SIDE
COUL = 160.0
F32 = jnp.float32
BF16 = jnp.bfloat16


def cas_matrix():
    index = np.arange(SIDE, dtype=np.int32)
    phases = (index[:, None] * index[None, :] % SIDE).astype(np.float32) * np.float32(2.0 * np.pi / SIDE)
    return np.cos(phases) + np.sin(phases)


CAS = cas_matrix()
BY_PARITY = np.concatenate([np.arange(0, SIDE, 2), np.arange(1, SIDE, 2)])
Y_TABLE = CAS[:, BY_PARITY]
Y_BACK = CAS[BY_PARITY, :]
X_TABLE = CAS[:, BY_PARITY]
X_BACK = CAS[BY_PARITY, :]


def z_tables():
    gap = np.zeros((64, 256), np.float32)
    space = np.zeros((SIDE, 64), np.float32)
    first = np.concatenate([CAS, space], axis=1)
    second = np.concatenate([CAS[:, :128], space, CAS[:, 128:]], axis=1)
    return np.stack([np.concatenate(part, axis=0) for table in (first, second) for part in ((table, gap), (gap, table))])


Z_TABLES = z_tables()
Z_BACKS = np.swapaxes(Z_TABLES, 1, 2)


def wave(index):
    return jnp.where(index < SIDE // 2, index, index - SIDE).astype(F32)


def coulomb(me):
    shape = (ROWS // 2, SIDE, 384)
    pair = lax.broadcasted_iota(jnp.int32, shape, 0)
    row = lax.broadcasted_iota(jnp.int32, shape, 1)
    col = lax.broadcasted_iota(jnp.int32, shape, 2)
    late = jnp.where(col < 256, col >= 128, col >= 320)
    kz = jnp.where(col < 256, col % 128, 128 + col % 64)
    ky = me * ROWS + pair + jnp.where(late, ROWS // 2, 0)
    mx, my, mz = wave(row), wave(ky), wave(kz)
    norm_sq = mx * mx + my * my + mz * mz
    bounded = jnp.maximum(norm_sq, 1.0)
    return jnp.where(norm_sq > 0.5, COUL / bounded, 0.0) / float(SIDE) ** 3


def dot(left, right):
    return jnp.dot(left, right, preferred_element_type=F32)


def whole(shape):
    return pl.BlockSpec(shape, lambda *_: (0,) * len(shape))


def tiles(lots, rows):
    return jnp.concatenate([lot[rows, :] for lot in lots], axis=1)


def forward_body(target, source, z_tables, y_table, out, *lots):
    chunks = source.shape[0]
    per_chunk = DUOS // chunks

    def form(duo, carry):
        chunk, part = duo // per_chunk, duo % per_chunk
        left = target[:, pl.ds(pl.multiple_of(duo * 384, 128), 384)].astype(F32)
        right = source[chunk, 0, :, pl.ds(pl.multiple_of(part * 384, 128), 384)].astype(F32)
        density = left * right
        for tile, lot in enumerate(lots):
            lot[pl.ds(duo, ROWS, stride=DUOS), :] = density[:, tile * 128 : (tile + 1) * 128]
        return carry

    lax.fori_loop(0, DUOS, form, 0, unroll=4)

    def planes(quad, carry):
        along_y = []
        for pair in range(2):
            halves = []
            for plane in range(2):
                rows = pl.ds(pl.multiple_of((quad * 4 + pair * 2 + plane) * DUOS, DUOS), DUOS)
                density = tiles(lots, rows).astype(BF16)
                even = dot(density[:, :256], z_tables[2 * plane])
                odd = dot(density[:, 128:], z_tables[2 * plane + 1])
                halves.append(jnp.concatenate([even, odd], axis=0))
            low, high = halves
            packed = jnp.concatenate([low[:, :128], high[:, :128], low[:, 128:] + high[:, 128:]], axis=1)
            along_y.append(dot(y_table[...], packed.astype(BF16)))
        for part in range(PARTS):
            rows = slice(part * ROWS, (part + 1) * ROWS)
            out[part, 0, quad] = jnp.concatenate([along_y[0][rows], along_y[1][rows]], axis=0).astype(BF16)
        return carry

    lax.fori_loop(0, QUADS, planes, 0)


def forward(target, sources):
    chunks, pairs = sources.shape[:2]
    return pl.pallas_call(
        forward_body,
        grid=(pairs,),
        in_specs=[
            whole((ROWS, CELLS)),
            pl.BlockSpec((chunks, 1, ROWS, CELLS // chunks), lambda p: (0, p, 0, 0)),
            whole((4, 256, 256)),
            whole((SIDE, SIDE)),
        ],
        out_specs=pl.BlockSpec((PARTS, 1, QUADS, 2 * ROWS, 384), lambda p: (0, p, 0, 0, 0)),
        out_shape=jax.ShapeDtypeStruct((PARTS, pairs, QUADS, 2 * ROWS, 384), BF16),
        scratch_shapes=[pltpu.VMEM((ROWS * DUOS, 128), F32)] * 3,
        compiler_params=pltpu.CompilerParams(vmem_limit_bytes=40 * 2**20),
        cost_estimate=pl.CostEstimate(flops=pairs * 1400 * 10**6, bytes_accessed=pairs * 7 * 10**6, transcendentals=0),
        name="forward_zy",
    )(target, sources, jnp.asarray(Z_TABLES, BF16), jnp.asarray(Y_TABLE, BF16))


def middle_body(pieces, kernel, x_table, x_back, out, head0, head1, tail):
    lots = (head0, head1, tail)
    block = QUADS * 2 * ROWS
    for part in range(PARTS):
        for tile, lot in enumerate(lots):
            lot[part * block : (part + 1) * block] = (
                pieces[part, 0, :, :, tile * 128 : (tile + 1) * 128].astype(F32).reshape(block, 128)
            )
    low = lax.broadcasted_iota(jnp.int32, (DUOS, 128), 1) < 64

    def step(i, carry):
        here = pl.ds(i, DUOS, stride=ROWS)
        there = pl.ds(i + ROWS // 2, DUOS, stride=ROWS)
        tail_a, tail_b = tail[here, :], tail[there, :]
        tail_first = jnp.where(low, tail_a, pltpu.roll(tail_b, 64, 1))
        tail_second = jnp.where(low, pltpu.roll(tail_a, 64, 1), tail_b)
        columns = jnp.concatenate(
            [
                jnp.concatenate([head0[here, :], head0[there, :], tail_first], axis=1),
                jnp.concatenate([head1[here, :], head1[there, :], tail_second], axis=1),
            ],
            axis=0,
        ).astype(BF16)
        spectrum = (kernel[i] * dot(x_table[...], columns)).astype(BF16)
        back = dot(x_back[...], spectrum)
        head0[here, :] = back[:DUOS, :128]
        head1[here, :] = back[DUOS:, :128]
        head0[there, :] = back[:DUOS, 128:256]
        head1[there, :] = back[DUOS:, 128:256]
        first, second = back[:DUOS, 256:], back[DUOS:, 256:]
        tail[here, :] = jnp.where(low, first, pltpu.roll(second, 64, 1))
        tail[there, :] = jnp.where(low, pltpu.roll(first, 64, 1), second)
        return carry

    lax.fori_loop(0, ROWS // 2, step, 0)
    for part in range(PARTS):
        for tile, lot in enumerate(lots):
            out[part, 0, :, :, tile * 128 : (tile + 1) * 128] = (
                lot[part * block : (part + 1) * block].astype(BF16).reshape(QUADS, 2 * ROWS, 128)
            )


def middle(pieces, kernel):
    pairs = pieces.shape[1]
    spec = pl.BlockSpec((PARTS, 1, QUADS, 2 * ROWS, 384), lambda p: (0, p, 0, 0, 0))
    return pl.pallas_call(
        middle_body,
        grid=(pairs,),
        in_specs=[spec, whole(kernel.shape), whole((SIDE, SIDE)), whole((SIDE, SIDE))],
        out_specs=spec,
        out_shape=jax.ShapeDtypeStruct(pieces.shape, BF16),
        scratch_shapes=[pltpu.VMEM((DUOS * ROWS, 128), F32)] * 3,
        compiler_params=pltpu.CompilerParams(vmem_limit_bytes=40 * 2**20),
        cost_estimate=pl.CostEstimate(flops=pairs * 1400 * 10**6, bytes_accessed=pairs * 7 * 10**6, transcendentals=0),
        name="middle_x",
    )(pieces, kernel, jnp.asarray(X_TABLE, BF16), jnp.asarray(X_BACK, BF16))


def backward_body(pieces, source, *refs):
    (total, y_table, z_tables, out), lots = ((None,) + refs[:3], refs[3:]) if len(refs) == 6 else (refs[:4], refs[4:])
    chunks = source.shape[0]
    per_chunk = DUOS // chunks

    @pl.when(pl.program_id(0) == 0)
    def _():
        if total is None:
            out[...] = jnp.zeros(out.shape, F32)
        else:
            out[...] = total[...]

    def planes(quad, carry):
        parts = [pieces[part, 0, quad].astype(F32) for part in range(PARTS)]
        for pair in range(2):
            stack = jnp.concatenate([part[pair * ROWS : (pair + 1) * ROWS] for part in parts], axis=0)
            fields = dot(y_table[...], stack.astype(BF16)).astype(BF16)
            for plane in range(2):
                lanes = fields[:, 128:] if plane else jnp.concatenate([fields[:, :128], fields[:, 256:]], axis=1)
                even = dot(lanes[:DUOS], z_tables[2 * plane])
                odd = dot(lanes[DUOS:], z_tables[2 * plane + 1])
                rows = pl.ds(pl.multiple_of((quad * 4 + pair * 2 + plane) * DUOS, DUOS), DUOS)
                lots[0][rows, :] = even[:, :128]
                lots[1][rows, :] = even[:, 128:] + odd[:, :128]
                lots[2][rows, :] = odd[:, 128:]
        return carry

    lax.fori_loop(0, QUADS, planes, 0)

    def gather(duo, carry):
        chunk, part = duo // per_chunk, duo % per_chunk
        potential = tiles(lots, pl.ds(duo, ROWS, stride=DUOS))
        here = pl.ds(pl.multiple_of(duo * 384, 128), 384)
        right = source[chunk, 0, :, pl.ds(pl.multiple_of(part * 384, 128), 384)].astype(F32)
        out[:, here] = out[:, here] - potential * right
        return carry

    lax.fori_loop(0, DUOS, gather, 0, unroll=4)


def backward(pieces, sources, total):
    chunks, pairs = sources.shape[:2]
    return pl.pallas_call(
        backward_body,
        grid=(pairs,),
        in_specs=[
            pl.BlockSpec((PARTS, 1, QUADS, 2 * ROWS, 384), lambda p: (0, p, 0, 0, 0)),
            pl.BlockSpec((chunks, 1, ROWS, CELLS // chunks), lambda p: (0, p, 0, 0)),
        ]
        + [whole((ROWS, CELLS))] * (total is not None)
        + [whole((SIDE, SIDE)), whole((4, 256, 256))],
        out_specs=whole((ROWS, CELLS)),
        out_shape=jax.ShapeDtypeStruct((ROWS, CELLS), F32),
        scratch_shapes=[pltpu.VMEM((ROWS * DUOS, 128), F32)] * 3,
        compiler_params=pltpu.CompilerParams(vmem_limit_bytes=48 * 2**20),
        cost_estimate=pl.CostEstimate(flops=pairs * 1400 * 10**6, bytes_accessed=pairs * 7 * 10**6, transcendentals=0),
        name="backward_yz",
    )(pieces, sources, *([] if total is None else [total]), jnp.asarray(Y_BACK, BF16), jnp.asarray(Z_BACKS, BF16))


def exchange(pieces):
    return lax.all_to_all(pieces, "grid", 0, 0, tiled=True)


def band_of(z_hi, x, core):
    return z_hi * 8 + x * 2 + core


def spread(orbitals):
    band = lax.axis_index("band")
    z_hi, x = band // 8, (band // 2) % 4
    core = band % 2
    cut = CELLS // 4
    mine = jnp.where(x == 0, orbitals[:, :cut], jnp.zeros((), BF16))
    for step in range(1, 4):
        pairs = [(band_of(z, 0, 0), band_of(z, step, 0)) for z in (0, 2)]
        mine = mine + lax.ppermute(orbitals[:, step * cut : (step + 1) * cut], "band", pairs)
    swap = [(band_of(z, i, 0), band_of(z, i, 1)) for z in (0, 2) for i in range(4)]
    other = lax.ppermute(mine[:, cut // 2 :], "band", swap)
    mine = jnp.where(core == 0, mine[:, : cut // 2], other)
    got = []
    for moves in (((0, 1), (2, 3)), ((0, 3), (2, 1)), ((0, 2), (2, 0))):
        pairs = [(band_of(a, i, c), band_of(b, i, c)) for a, b in moves for i in range(4) for c in range(2)]
        got.append(lax.ppermute(mine, "band", pairs))
    near, far, cross = got
    from_first = jnp.where(z_hi == 0, mine, jnp.where(z_hi == 1, near, jnp.where(z_hi == 2, cross, far)))
    from_second = jnp.where(z_hi == 2, mine, jnp.where(z_hi == 3, near, jnp.where(z_hi == 0, cross, far)))
    groups = [[8 * k + i for i in range(8)] for k in range(4)]
    return lax.all_gather(jnp.stack([from_first, from_second]), "band", axis=0, axis_index_groups=groups)


def local(orbitals):
    kernel = coulomb(lax.axis_index("grid"))
    batches = [spread(orbitals[p]) for p in range(2)]
    backs = []
    for sources in batches:
        pieces = exchange(forward(orbitals[0], sources))
        backs.append(exchange(middle(pieces, kernel)))
    total = None
    for pieces, sources in zip(backs, batches):
        total = backward(pieces, sources, total)
    return total[None]


def solution(mesh):
    return jax.shard_map(
        local,
        mesh=mesh,
        in_specs=(P("band", "grid", None),),
        out_specs=P("band", "grid", None),
        check_vma=False,
    )
```

```python
import jax
import jax.numpy as jnp
import numpy as np
from jax import lax
from jax.experimental import pallas as pl
from jax.experimental.pallas import tpu as pltpu
from jax.sharding import PartitionSpec as P

SIDE = 192
PARTS = 8
ROWS = SIDE // PARTS
QUADS = ROWS // 4
DUOS = SIDE // 2
CELLS = SIDE * SIDE
COUL = 160.0
PER_CUT = DUOS // 4
PIECES = (PARTS, QUADS, 2 * ROWS, 384)
VECTOR = pl.BlockSpec(memory_space=pltpu.VMEM)
SCALAR = pl.BlockSpec(memory_space=pltpu.SMEM)
F32 = jnp.float32
BF16 = jnp.bfloat16


def cas_matrix():
    index = np.arange(SIDE, dtype=np.int32)
    phases = (index[:, None] * index[None, :] % SIDE).astype(np.float32) * np.float32(2.0 * np.pi / SIDE)
    return np.cos(phases) + np.sin(phases)


CAS = cas_matrix()
BY_PARITY = np.concatenate([np.arange(0, SIDE, 2), np.arange(1, SIDE, 2)])
Y_TABLE = CAS[:, BY_PARITY]
Y_BACK = CAS[BY_PARITY, :]
X_TABLE = CAS[:, BY_PARITY]
X_BACK = CAS[BY_PARITY, :]


def z_tables():
    gap = np.zeros((64, 256), np.float32)
    space = np.zeros((SIDE, 64), np.float32)
    first = np.concatenate([CAS, space], axis=1)
    second = np.concatenate([CAS[:, :128], space, CAS[:, 128:]], axis=1)
    return np.stack([np.concatenate(part, axis=0) for table in (first, second) for part in ((table, gap), (gap, table))])


Z_TABLES = z_tables()
Z_BACKS = np.swapaxes(Z_TABLES, 1, 2)


def wave(index):
    return jnp.where(index < SIDE // 2, index, index - SIDE).astype(F32)


def coulomb(me):
    shape = (ROWS // 2, SIDE, 384)
    pair = lax.broadcasted_iota(jnp.int32, shape, 0)
    row = lax.broadcasted_iota(jnp.int32, shape, 1)
    col = lax.broadcasted_iota(jnp.int32, shape, 2)
    late = jnp.where(col < 256, col >= 128, col >= 320)
    kz = jnp.where(col < 256, col % 128, 128 + col % 64)
    ky = me * ROWS + pair + jnp.where(late, ROWS // 2, 0)
    mx, my, mz = wave(row), wave(ky), wave(kz)
    norm_sq = mx * mx + my * my + mz * mz
    bounded = jnp.maximum(norm_sq, 1.0)
    return jnp.where(norm_sq > 0.5, COUL / bounded, 0.0) / float(SIDE) ** 3


def dot(left, right):
    return jnp.dot(left, right, preferred_element_type=F32)


def tiles(lots, rows):
    return jnp.concatenate([lot[rows, :] for lot in lots], axis=1)


def forward_body(column, target, source, z_tables, y_table, out, *lots):
    def form(duo, carry):
        chunk, part = (duo // PER_CUT) ^ column[0], duo % PER_CUT
        left = target[:, pl.ds(pl.multiple_of(duo * 384, 128), 384)].astype(F32)
        right = source[chunk, :, pl.ds(pl.multiple_of(part * 384, 128), 384)].astype(F32)
        density = left * right
        for tile, lot in enumerate(lots):
            lot[pl.ds(duo, ROWS, stride=DUOS), :] = density[:, tile * 128 : (tile + 1) * 128]
        return carry

    lax.fori_loop(0, DUOS, form, 0, unroll=4)

    def planes(quad, carry):
        along_y = []
        for pair in range(2):
            halves = []
            for plane in range(2):
                rows = pl.ds(pl.multiple_of((quad * 4 + pair * 2 + plane) * DUOS, DUOS), DUOS)
                density = tiles(lots, rows).astype(BF16)
                even = dot(density[:, :256], z_tables[2 * plane])
                odd = dot(density[:, 128:], z_tables[2 * plane + 1])
                halves.append(jnp.concatenate([even, odd], axis=0))
            low, high = halves
            packed = jnp.concatenate([low[:, :128], high[:, :128], low[:, 128:] + high[:, 128:]], axis=1)
            along_y.append(dot(y_table[...], packed.astype(BF16)))
        for part in range(PARTS):
            rows = slice(part * ROWS, (part + 1) * ROWS)
            out[part, quad] = jnp.concatenate([along_y[0][rows], along_y[1][rows]], axis=0).astype(BF16)
        return carry

    lax.fori_loop(0, QUADS, planes, 0)


def forward(column, target, source):
    return pl.pallas_call(
        forward_body,
        in_specs=[SCALAR] + [VECTOR] * 4,
        out_specs=VECTOR,
        out_shape=jax.ShapeDtypeStruct(PIECES, BF16),
        scratch_shapes=[pltpu.VMEM((ROWS * DUOS, 128), F32)] * 3,
        compiler_params=pltpu.CompilerParams(vmem_limit_bytes=32 * 2**20),
        cost_estimate=pl.CostEstimate(flops=1400 * 10**6, bytes_accessed=7 * 10**6, transcendentals=0),
        name="forward_zy",
    )(column, target, source, jnp.asarray(Z_TABLES, BF16), jnp.asarray(Y_TABLE, BF16))


def middle_body(pieces, kernel, x_table, x_back, out, head0, head1, tail):
    lots = (head0, head1, tail)
    block = QUADS * 2 * ROWS
    for part in range(PARTS):
        for tile, lot in enumerate(lots):
            lot[part * block : (part + 1) * block] = (
                pieces[part, :, :, tile * 128 : (tile + 1) * 128].astype(F32).reshape(block, 128)
            )
    low = lax.broadcasted_iota(jnp.int32, (DUOS, 128), 1) < 64

    def step(i, carry):
        here = pl.ds(i, DUOS, stride=ROWS)
        there = pl.ds(i + ROWS // 2, DUOS, stride=ROWS)
        tail_a, tail_b = tail[here, :], tail[there, :]
        tail_first = jnp.where(low, tail_a, pltpu.roll(tail_b, 64, 1))
        tail_second = jnp.where(low, pltpu.roll(tail_a, 64, 1), tail_b)
        columns = jnp.concatenate(
            [
                jnp.concatenate([head0[here, :], head0[there, :], tail_first], axis=1),
                jnp.concatenate([head1[here, :], head1[there, :], tail_second], axis=1),
            ],
            axis=0,
        ).astype(BF16)
        spectrum = (kernel[i] * dot(x_table[...], columns)).astype(BF16)
        back = dot(x_back[...], spectrum)
        head0[here, :] = back[:DUOS, :128]
        head1[here, :] = back[DUOS:, :128]
        head0[there, :] = back[:DUOS, 128:256]
        head1[there, :] = back[DUOS:, 128:256]
        first, second = back[:DUOS, 256:], back[DUOS:, 256:]
        tail[here, :] = jnp.where(low, first, pltpu.roll(second, 64, 1))
        tail[there, :] = jnp.where(low, pltpu.roll(first, 64, 1), second)
        return carry

    lax.fori_loop(0, ROWS // 2, step, 0)
    for part in range(PARTS):
        for tile, lot in enumerate(lots):
            out[part, :, :, tile * 128 : (tile + 1) * 128] = (
                lot[part * block : (part + 1) * block].astype(BF16).reshape(QUADS, 2 * ROWS, 128)
            )


def middle(pieces, kernel):
    return pl.pallas_call(
        middle_body,
        in_specs=[VECTOR] * 4,
        out_specs=VECTOR,
        out_shape=jax.ShapeDtypeStruct(PIECES, BF16),
        scratch_shapes=[pltpu.VMEM((DUOS * ROWS, 128), F32)] * 3,
        compiler_params=pltpu.CompilerParams(vmem_limit_bytes=32 * 2**20),
        cost_estimate=pl.CostEstimate(flops=1400 * 10**6, bytes_accessed=7 * 10**6, transcendentals=0),
        name="middle_x",
    )(pieces, kernel, jnp.asarray(X_TABLE, BF16), jnp.asarray(X_BACK, BF16))


def backward_body(column, pieces, source, *refs):
    (total, y_table, z_tables, out), lots = ((None,) + refs[:3], refs[3:]) if len(refs) == 6 else (refs[:4], refs[4:])

    def planes(quad, carry):
        parts = [pieces[part, quad].astype(F32) for part in range(PARTS)]
        for pair in range(2):
            stack = jnp.concatenate([part[pair * ROWS : (pair + 1) * ROWS] for part in parts], axis=0)
            fields = dot(y_table[...], stack.astype(BF16)).astype(BF16)
            for plane in range(2):
                lanes = fields[:, 128:] if plane else jnp.concatenate([fields[:, :128], fields[:, 256:]], axis=1)
                even = dot(lanes[:DUOS], z_tables[2 * plane])
                odd = dot(lanes[DUOS:], z_tables[2 * plane + 1])
                rows = pl.ds(pl.multiple_of((quad * 4 + pair * 2 + plane) * DUOS, DUOS), DUOS)
                lots[0][rows, :] = even[:, :128]
                lots[1][rows, :] = even[:, 128:] + odd[:, :128]
                lots[2][rows, :] = odd[:, 128:]
        return carry

    lax.fori_loop(0, QUADS, planes, 0)

    def gather(duo, carry):
        chunk, part = (duo // PER_CUT) ^ column[0], duo % PER_CUT
        potential = tiles(lots, pl.ds(duo, ROWS, stride=DUOS))
        here = pl.ds(pl.multiple_of(duo * 384, 128), 384)
        right = source[chunk, :, pl.ds(pl.multiple_of(part * 384, 128), 384)].astype(F32)
        term = potential * right
        out[:, here] = -term if total is None else total[:, here] - term
        return carry

    lax.fori_loop(0, DUOS, gather, 0, unroll=4)


def backward(column, pieces, source, total):
    return pl.pallas_call(
        backward_body,
        in_specs=[SCALAR] + [VECTOR] * (4 + (total is not None)),
        out_specs=VECTOR,
        out_shape=jax.ShapeDtypeStruct((ROWS, CELLS), F32),
        scratch_shapes=[pltpu.VMEM((ROWS * DUOS, 128), F32)] * 3,
        compiler_params=pltpu.CompilerParams(vmem_limit_bytes=32 * 2**20),
        cost_estimate=pl.CostEstimate(flops=1400 * 10**6, bytes_accessed=7 * 10**6, transcendentals=0),
        name="backward_yz",
    )(column, pieces, source, *([] if total is None else [total]), jnp.asarray(Y_BACK, BF16), jnp.asarray(Z_BACKS, BF16))


BOTH = ("band", "grid")
CHIPS = [(x, y, z) for x in range(4) for y in range(4) for z in range(8)]


def place(x, y, z, core):
    return ((z % 8 // 2) * 8 + x * 2 + core) * PARTS + y * 2 + z % 2


def exchange_groups():
    groups = [[place(x, y, 2 * k + low, 0) for y in range(4) for low in range(2)] for x in range(4) for k in range(4)]
    for y in range(4):
        for k in range(4):
            groups.append([place(slab ^ y, y, 2 * k + 2 - low, 1) for slab in range(4) for low in range(2)])
    return groups


def exchange(pieces):
    return lax.all_to_all(pieces, BOTH, 0, 0, axis_index_groups=exchange_groups(), tiled=True)


def turned(x, y, z, which):
    step = (2 if z % 2 == 0 else 0) if which == 0 else (-2 if z % 2 else 0)
    return x ^ y, x, (z + step) % 8


def move(array, pairs):
    return lax.ppermute(array, BOTH, pairs)


def spread(orbital, is_root):
    cut = CELLS // 4
    cuts = [orbital[:, step * cut : (step + 1) * cut] for step in range(4)]
    slabs = [(y, low) for y in range(4) for low in range(2)]
    mine = sum(
        move(cuts[step], [(place(0, y, z + low, 0), place(step, y, z + low, z // 4)) for z in (0, 4) for y, low in slabs])
        for step in range(4)
    )
    away = sum(
        move(
            mine,
            [(place(x, y, 4 * c + low, c), place(x, y, 4 * c + low + up, c)) for c in range(2) for x in range(4) for y, low in slabs],
        )
        for up in (2, 6, 4)
    )
    mine = jnp.where(is_root, mine, away)
    got = []
    for step in range(4):
        pairs = [(place(x, y, z, 0), place(x ^ step, y, z, 0)) for x, y, z in CHIPS]
        pairs += [(place(x, y, z, 1), place(x ^ step, y ^ x ^ step, z, 1)) for x, y, z in CHIPS]
        got.append(move(mine, pairs))
    return jnp.stack(got)


def local(orbitals):
    band, grid = lax.axis_index("band"), lax.axis_index("grid")
    z_hi, x, core = band // 8, (band // 2) % 4, band % 2
    y, low = grid // 2, grid % 2
    column = x[None].astype(jnp.int32)
    kernel = coulomb(2 * jnp.where(core == 0, y, x ^ y) + low)
    own = orbitals[0]

    sources = [spread(orbitals[p], z_hi == 2 * core) for p in range(2)]
    out_a = [(place(x, y, z, 0), place(*turned(x, y, z, 0), 1)) for x, y, z in CHIPS]
    out_b = [(place(x, y, z, 1), place(*turned(x, y, z, 1), 1)) for x, y, z in CHIPS]
    target_a = jnp.where(core == 0, own, move(own, out_a))
    swap = [(place(x, y, z, 1), place(x, y, z, 0)) for x, y, z in CHIPS]
    target_b = move(own, swap) + move(own, out_b)
    targets = [target_a, target_b]

    there = {}
    for p in range(2):
        for t in range(2):
            there[p, t] = exchange(forward(column, targets[t], sources[p]))
    sums = []
    for t in range(2):
        total = None
        for p in range(2):
            total = backward(column, exchange(middle(there[p, t], kernel)), sources[p], total)
        sums.append(total)
    sum_a, sum_b = sums
    back_a = move(sum_a.astype(BF16), [(b, a) for a, b in out_a])
    back_b = move(sum_b.astype(BF16), [(b, a) for a, b in out_b])
    swapped = move(sum_b, [(b, a) for a, b in swap])
    result = jnp.where(core == 0, sum_a, swapped) + jnp.where(core == 0, back_a, back_b).astype(F32)
    return result[None]


def solution(mesh):
    return jax.shard_map(
        local,
        mesh=mesh,
        in_specs=(P("band", "grid", None),),
        out_specs=P("band", "grid", None),
        check_vma=False,
    )
```

```python
import jax
import jax.numpy as jnp
import numpy as np
from jax import lax
from jax.experimental import pallas as pl
from jax.experimental.pallas import tpu as pltpu
from jax.sharding import PartitionSpec as P

SIDE = 192
PARTS = 8
ROWS = SIDE // PARTS
QUADS = ROWS // 4
DUOS = SIDE // 2
CELLS = SIDE * SIDE
COUL = 160.0
PITCH = 104
PER_CUT = DUOS // 4
PIECES = (PARTS, QUADS, 2 * ROWS, 384)
VECTOR = pl.BlockSpec(memory_space=pltpu.VMEM)
SCALAR = pl.BlockSpec(memory_space=pltpu.SMEM)
F32 = jnp.float32
BF16 = jnp.bfloat16


def cas_matrix():
    index = np.arange(SIDE, dtype=np.int32)
    phases = (index[:, None] * index[None, :] % SIDE).astype(np.float32) * np.float32(2.0 * np.pi / SIDE)
    return np.cos(phases) + np.sin(phases)


CAS = cas_matrix()
BY_PARITY = np.concatenate([np.arange(0, SIDE, 2), np.arange(1, SIDE, 2)])
Y_TABLE = CAS[:, BY_PARITY]
Y_BACK = CAS[BY_PARITY, :]
X_TABLE = CAS[:, BY_PARITY]
X_BACK = CAS[BY_PARITY, :]


def z_tables():
    gap = np.zeros((64, 256), np.float32)
    space = np.zeros((SIDE, 64), np.float32)
    first = np.concatenate([CAS, space], axis=1)
    second = np.concatenate([CAS[:, :128], space, CAS[:, 128:]], axis=1)
    return np.stack([np.concatenate(part, axis=0) for table in (first, second) for part in ((table, gap), (gap, table))])


Z_TABLES = z_tables()
Z_BACKS = np.swapaxes(Z_TABLES, 1, 2)


def wave(index):
    return jnp.where(index < SIDE // 2, index, index - SIDE).astype(F32)


def coulomb(me):
    shape = (ROWS // 2, SIDE, 384)
    pair = lax.broadcasted_iota(jnp.int32, shape, 0)
    row = lax.broadcasted_iota(jnp.int32, shape, 1)
    col = lax.broadcasted_iota(jnp.int32, shape, 2)
    late = jnp.where(col < 256, col >= 128, col >= 320)
    kz = jnp.where(col < 256, col % 128, 128 + col % 64)
    ky = me * ROWS + pair + jnp.where(late, ROWS // 2, 0)
    mx, my, mz = wave(row), wave(ky), wave(kz)
    norm_sq = mx * mx + my * my + mz * mz
    bounded = jnp.maximum(norm_sq, 1.0)
    return jnp.where(norm_sq > 0.5, COUL / bounded, 0.0) / float(SIDE) ** 3


def dot(left, right):
    return jnp.dot(left, right, preferred_element_type=F32)


def tiles(lots, rows):
    return jnp.concatenate([lot[rows, :] for lot in lots], axis=1)


def forward_body(column, target, *refs):
    sources, (z_tables, y_table, out), lots = refs[:4], refs[4:7], refs[7:]

    for slot, source in enumerate(sources):

        def form(part, carry, source=source, slot=slot):
            duo = (column[0] ^ slot) * PER_CUT + part
            left = target[:, pl.ds(pl.multiple_of(duo * 384, 128), 384)].astype(F32)
            right = source[:, pl.ds(pl.multiple_of(part * 384, 128), 384)].astype(F32)
            density = left * right
            for tile, lot in enumerate(lots):
                lot[pl.ds(duo, ROWS, stride=PITCH), :] = density[:, tile * 128 : (tile + 1) * 128]
            return carry

        lax.fori_loop(0, PER_CUT, form, 0, unroll=12)

    def planes(quad, carry):
        along_z = []
        for pair in range(2):
            halves = []
            for plane in range(2):
                rows = pl.ds(pl.multiple_of((quad * 4 + pair * 2 + plane) * PITCH, 8), DUOS)
                density = tiles(lots, rows).astype(BF16)
                even = dot(density[:, :256], z_tables[2 * plane])
                odd = dot(density[:, 128:], z_tables[2 * plane + 1])
                halves.append(jnp.concatenate([even, odd], axis=0))
            low, high = halves
            along_z += [low[:, :128], high[:, :128], low[:, 128:] + high[:, 128:]]
        along_y = dot(y_table[...], jnp.concatenate(along_z, axis=1).astype(BF16))
        for part in range(PARTS):
            rows = slice(part * ROWS, (part + 1) * ROWS)
            out[part, quad] = jnp.concatenate([along_y[rows, :384], along_y[rows, 384:]], axis=0).astype(BF16)
        return carry

    lax.fori_loop(0, QUADS, planes, 0, unroll=6)


def forward(column, target, sources):
    return pl.pallas_call(
        forward_body,
        in_specs=[SCALAR] + [VECTOR] * 7,
        out_specs=VECTOR,
        out_shape=jax.ShapeDtypeStruct(PIECES, BF16),
        scratch_shapes=[pltpu.VMEM((ROWS * PITCH, 128), F32)] * 3,
        compiler_params=pltpu.CompilerParams(vmem_limit_bytes=32 * 2**20),
        cost_estimate=pl.CostEstimate(flops=1400 * 10**6, bytes_accessed=7 * 10**6, transcendentals=0),
        name="forward_zy",
    )(column, target, *sources, jnp.asarray(Z_TABLES, BF16), jnp.asarray(Y_TABLE, BF16))


def middle_body(pieces, kernel, x_table, x_back, out, head0, head1, tail):
    lots = (head0, head1, tail)
    block = QUADS * 2 * ROWS
    for part in range(PARTS):
        for tile, lot in enumerate(lots):
            lot[part * block : (part + 1) * block] = (
                pieces[part, :, :, tile * 128 : (tile + 1) * 128].astype(F32).reshape(block, 128)
            )
    low = lax.broadcasted_iota(jnp.int32, (DUOS, 128), 1) < 64

    def step(i, carry):
        here = pl.ds(i, DUOS, stride=ROWS)
        there = pl.ds(i + ROWS // 2, DUOS, stride=ROWS)
        tail_a, tail_b = tail[here, :], tail[there, :]
        tail_first = jnp.where(low, tail_a, pltpu.roll(tail_b, 64, 1))
        tail_second = jnp.where(low, pltpu.roll(tail_a, 64, 1), tail_b)
        columns = jnp.concatenate(
            [
                jnp.concatenate([head0[here, :], head0[there, :], tail_first], axis=1),
                jnp.concatenate([head1[here, :], head1[there, :], tail_second], axis=1),
            ],
            axis=0,
        ).astype(BF16)
        spectrum = (kernel[i] * dot(x_table[...], columns)).astype(BF16)
        back = dot(x_back[...], spectrum)
        head0[here, :] = back[:DUOS, :128]
        head1[here, :] = back[DUOS:, :128]
        head0[there, :] = back[:DUOS, 128:256]
        head1[there, :] = back[DUOS:, 128:256]
        first, second = back[:DUOS, 256:], back[DUOS:, 256:]
        tail[here, :] = jnp.where(low, first, pltpu.roll(second, 64, 1))
        tail[there, :] = jnp.where(low, pltpu.roll(first, 64, 1), second)
        return carry

    lax.fori_loop(0, ROWS // 2, step, 0, unroll=6)
    for part in range(PARTS):
        for tile, lot in enumerate(lots):
            out[part, :, :, tile * 128 : (tile + 1) * 128] = (
                lot[part * block : (part + 1) * block].astype(BF16).reshape(QUADS, 2 * ROWS, 128)
            )


def middle(pieces, kernel):
    return pl.pallas_call(
        middle_body,
        in_specs=[VECTOR] * 4,
        out_specs=VECTOR,
        out_shape=jax.ShapeDtypeStruct(PIECES, BF16),
        scratch_shapes=[pltpu.VMEM((DUOS * ROWS, 128), F32)] * 3,
        compiler_params=pltpu.CompilerParams(vmem_limit_bytes=32 * 2**20),
        cost_estimate=pl.CostEstimate(flops=1400 * 10**6, bytes_accessed=7 * 10**6, transcendentals=0),
        name="middle_x",
    )(pieces, kernel, jnp.asarray(X_TABLE, BF16), jnp.asarray(X_BACK, BF16))


def backward_body(column, pieces, *refs):
    sources, refs = refs[:4], refs[4:]
    (total, y_table, z_tables, out), lots = ((None,) + refs[:3], refs[3:]) if len(refs) == 6 else (refs[:4], refs[4:])

    def planes(quad, carry):
        parts = [pieces[part, quad].astype(F32) for part in range(PARTS)]
        stacks = [
            jnp.concatenate([part[pair * ROWS : (pair + 1) * ROWS] for part in parts], axis=0) for pair in range(2)
        ]
        both = dot(y_table[...], jnp.concatenate(stacks, axis=1).astype(BF16)).astype(BF16)
        for pair in range(2):
            fields = both[:, pair * 384 : (pair + 1) * 384]
            for plane in range(2):
                lanes = fields[:, 128:] if plane else jnp.concatenate([fields[:, :128], fields[:, 256:]], axis=1)
                even = dot(lanes[:DUOS], z_tables[2 * plane])
                odd = dot(lanes[DUOS:], z_tables[2 * plane + 1])
                rows = pl.ds(pl.multiple_of((quad * 4 + pair * 2 + plane) * PITCH, 8), DUOS)
                lots[0][rows, :] = even[:, :128]
                lots[1][rows, :] = even[:, 128:] + odd[:, :128]
                lots[2][rows, :] = odd[:, 128:]
        return carry

    lax.fori_loop(0, QUADS, planes, 0, unroll=6)

    for slot, source in enumerate(sources):

        def gather(part, carry, source=source, slot=slot):
            duo = (column[0] ^ slot) * PER_CUT + part
            potential = tiles(lots, pl.ds(duo, ROWS, stride=PITCH))
            here = pl.ds(pl.multiple_of(duo * 384, 128), 384)
            right = source[:, pl.ds(pl.multiple_of(part * 384, 128), 384)].astype(F32)
            term = potential * right
            out[:, here] = -term if total is None else total[:, here] - term
            return carry

        lax.fori_loop(0, PER_CUT, gather, 0, unroll=12)


def backward(column, pieces, sources, total):
    return pl.pallas_call(
        backward_body,
        in_specs=[SCALAR] + [VECTOR] * (7 + (total is not None)),
        out_specs=VECTOR,
        out_shape=jax.ShapeDtypeStruct((ROWS, CELLS), F32),
        scratch_shapes=[pltpu.VMEM((ROWS * PITCH, 128), F32)] * 3,
        compiler_params=pltpu.CompilerParams(vmem_limit_bytes=32 * 2**20),
        cost_estimate=pl.CostEstimate(flops=1400 * 10**6, bytes_accessed=7 * 10**6, transcendentals=0),
        name="backward_yz",
    )(column, pieces, *sources, *([] if total is None else [total]), jnp.asarray(Y_BACK, BF16), jnp.asarray(Z_BACKS, BF16))


BOTH = ("band", "grid")
CHIPS = [(x, y, z) for x in range(4) for y in range(4) for z in range(8)]


def place(x, y, z, core):
    return ((z % 8 // 2) * 8 + x * 2 + core) * PARTS + y * 2 + z % 2


def exchange_groups():
    groups = [[place(x, y, 2 * k + low, 0) for y in range(4) for low in range(2)] for x in range(4) for k in range(4)]
    for y in range(4):
        for k in range(4):
            groups.append([place(slab ^ y, y, 2 * k + 2 - low, 1) for slab in range(4) for low in range(2)])
    return groups


def exchange(pieces):
    return lax.all_to_all(pieces, BOTH, 0, 0, axis_index_groups=exchange_groups(), tiled=True)


def turned(x, y, z, which):
    step = (2 if z % 2 == 0 else 0) if which == 0 else (-2 if z % 2 else 0)
    return x ^ y, x, (z + step) % 8


def move(array, pairs):
    return lax.ppermute(array, BOTH, pairs)


def after(array, *others):
    return lax.optimization_barrier((array, *others))[0]


SLABS = [(y, low) for y in range(4) for low in range(2)]


def scatter(orbital):
    cut = CELLS // 4
    return sum(
        move(
            orbital[:, step * cut : (step + 1) * cut],
            [(place(0, y, z + low, 0), place(step, y, z + low, z // 4)) for z in (0, 4) for y, low in SLABS],
        )
        for step in range(4)
    )


def along_z(mine, is_root):
    away = sum(
        move(
            mine,
            [(place(x, y, 4 * c + low, c), place(x, y, 4 * c + low + up, c)) for c in range(2) for x in range(4) for y, low in SLABS],
        )
        for up in (2, 6, 4)
    )
    return jnp.where(is_root, mine, away)


def gather_x(mine):
    got = []
    for step in range(4):
        pairs = [(place(x, y, z, 0), place(x ^ step, y, z, 0)) for x, y, z in CHIPS]
        pairs += [(place(x, y, z, 1), place(x ^ step, y ^ x ^ step, z, 1)) for x, y, z in CHIPS]
        got.append(move(mine, pairs))
    return got


def returned(array, which):
    first, second = [], []
    for x, y, z in CHIPS:
        across, row, level = turned(x, y, z, which)
        first.append((place(across, row, level, 1), place(across, y, level, 1)))
        second.append((place(across, y, level, 1), place(x, y, z, which)))
    return move(move(array, first), second)


def local(orbitals):
    band, grid = lax.axis_index("band"), lax.axis_index("grid")
    z_hi, x, core = band // 8, (band // 2) % 4, band % 2
    y, low = grid // 2, grid % 2
    column = x[None].astype(jnp.int32)
    kernel = coulomb(2 * jnp.where(core == 0, y, x ^ y) + low)
    own = orbitals[0]
    is_root = z_hi == 2 * core

    cut_0 = scatter(orbitals[0])
    out_a = [(place(x, y, z, 0), place(*turned(x, y, z, 0), 1)) for x, y, z in CHIPS]
    target_a = jnp.where(core == 0, own, move(own, out_a))
    spread_0 = along_z(cut_0, is_root)
    own_b = after(own, cut_0)
    out_b = [(place(x, y, z, 1), place(*turned(x, y, z, 1), 1)) for x, y, z in CHIPS]
    swap = [(place(x, y, z, 1), place(x, y, z, 0)) for x, y, z in CHIPS]
    target_b = move(own_b, swap) + move(own_b, out_b)
    cut_1 = scatter(after(orbitals[1], cut_0))
    source_0 = gather_x(spread_0)
    spread_1 = along_z(after(cut_1, spread_0), is_root)
    source_1 = gather_x(after(spread_1, *source_0))
    sources, targets = [source_0, source_1], [target_a, target_b]

    there = {}
    for p in range(2):
        for t in range(2):
            there[p, t] = exchange(forward(column, targets[t], sources[p]))
    sums = []
    for t in range(2):
        total = None
        for p in range(2):
            total = backward(column, exchange(middle(there[p, t], kernel)), sources[p], total)
        sums.append(total)
    sum_a, sum_b = sums
    back_a = returned(sum_a.astype(BF16), 0)
    swapped = move(sum_b, [(b, a) for a, b in swap])
    base = jnp.where(core == 0, sum_a + back_a.astype(F32), swapped)
    narrow = sum_b.astype(BF16)
    half = CELLS // 2
    back_b = jnp.concatenate([returned(narrow[:, :half], 1), returned(narrow[:, half:], 1)], axis=1)
    return (base + back_b.astype(F32))[None]


def solution(mesh):
    return jax.shard_map(
        local,
        mesh=mesh,
        in_specs=(P("band", "grid", None),),
        out_specs=P("band", "grid", None),
        check_vma=False,
    )
```

```python
import jax
import jax.numpy as jnp
import numpy as np
from jax import lax
from jax.experimental import pallas as pl
from jax.experimental.pallas import tpu as pltpu
from jax.sharding import PartitionSpec as P

SIDE = 192
PARTS = 8
ROWS = SIDE // PARTS
QUADS = ROWS // 4
DUOS = SIDE // 2
CELLS = SIDE * SIDE
COUL = 160.0
PITCH = 104
PER_CUT = DUOS // 4
PIECE = (QUADS, 2 * ROWS, 384)
VECTOR = pl.BlockSpec(memory_space=pltpu.VMEM)
SCALAR = pl.BlockSpec(memory_space=pltpu.SMEM)
F32 = jnp.float32
BF16 = jnp.bfloat16


def cas_matrix():
    index = np.arange(SIDE, dtype=np.int32)
    phases = (index[:, None] * index[None, :] % SIDE).astype(np.float32) * np.float32(2.0 * np.pi / SIDE)
    return np.cos(phases) + np.sin(phases)


CAS = cas_matrix()
BY_PARITY = np.concatenate([np.arange(0, SIDE, 2), np.arange(1, SIDE, 2)])
Y_TABLE = CAS[:, BY_PARITY]
X_TABLE = CAS[:, BY_PARITY]
X_BACK = CAS[BY_PARITY, :]


def z_tables():
    gap = np.zeros((64, 256), np.float32)
    space = np.zeros((SIDE, 64), np.float32)
    first = np.concatenate([CAS, space], axis=1)
    second = np.concatenate([CAS[:, :128], space, CAS[:, 128:]], axis=1)
    return np.stack([np.concatenate(part, axis=0) for table in (first, second) for part in ((table, gap), (gap, table))])


Z_TABLES = z_tables()
Z_BACKS = np.swapaxes(Z_TABLES, 1, 2)


def wave(index):
    return jnp.where(index < SIDE // 2, index, index - SIDE).astype(F32)


def coulomb(me):
    shape = (ROWS // 2, SIDE, 384)
    pair = lax.broadcasted_iota(jnp.int32, shape, 0)
    row = lax.broadcasted_iota(jnp.int32, shape, 1)
    col = lax.broadcasted_iota(jnp.int32, shape, 2)
    late = jnp.where(col < 256, col >= 128, col >= 320)
    kz = jnp.where(col < 256, col % 128, 128 + col % 64)
    ky = me * ROWS + pair + jnp.where(late, ROWS // 2, 0)
    mx, my, mz = wave(row), wave(ky), wave(kz)
    norm_sq = mx * mx + my * my + mz * mz
    bounded = jnp.maximum(norm_sq, 1.0)
    return jnp.where(norm_sq > 0.5, COUL / bounded, 0.0) / float(SIDE) ** 3


def dot(left, right):
    return jnp.dot(left, right, preferred_element_type=F32)


def tiles(lots, rows):
    return jnp.concatenate([lot[rows, :] for lot in lots], axis=1)


def forward_body(column, target, *refs):
    sources, (z_tables, y_table), outs, lots = refs[:-13], refs[-13:-11], refs[-11:-3], refs[-3:]
    for which in range(len(sources) // 4):
        for slot in range(4):
            source = sources[which * 4 + slot]

            def form(part, carry, source=source, slot=slot):
                duo = (column[0] ^ slot) * PER_CUT + part
                left = target[:, pl.ds(pl.multiple_of(duo * 384, 128), 384)].astype(F32)
                right = source[:, pl.ds(pl.multiple_of(part * 384, 128), 384)].astype(F32)
                density = left * right
                for tile, lot in enumerate(lots):
                    lot[pl.ds(duo, ROWS, stride=PITCH), :] = density[:, tile * 128 : (tile + 1) * 128]
                return carry

            lax.fori_loop(0, PER_CUT, form, 0, unroll=12)

        def planes(quad, carry, which=which):
            along_z = []
            for pair in range(2):
                halves = []
                for plane in range(2):
                    rows = pl.ds(pl.multiple_of((quad * 4 + pair * 2 + plane) * PITCH, 8), DUOS)
                    density = tiles(lots, rows).astype(BF16)
                    even = dot(density[:, :256], z_tables[2 * plane])
                    odd = dot(density[:, 128:], z_tables[2 * plane + 1])
                    halves.append(jnp.concatenate([even, odd], axis=0))
                low, high = halves
                along_z += [low[:, :128], high[:, :128], low[:, 128:] + high[:, 128:]]
            along_y = dot(y_table[...], jnp.concatenate(along_z, axis=1).astype(BF16))
            for part, out in enumerate(outs):
                rows = slice(part * ROWS, (part + 1) * ROWS)
                out[which, quad] = jnp.concatenate([along_y[rows, :384], along_y[rows, 384:]], axis=0).astype(BF16)
            return carry

        lax.fori_loop(0, QUADS, planes, 0, unroll=6)


def cost(pairs):
    return pl.CostEstimate(flops=pairs * 1400 * 10**6, bytes_accessed=pairs * 7 * 10**6, transcendentals=0)


def forward(column, target, sources, y_table):
    cuts = [cut for source in sources for cut in source]
    return pl.pallas_call(
        forward_body,
        in_specs=[SCALAR] + [VECTOR] * (len(cuts) + 3),
        out_specs=[VECTOR] * PARTS,
        out_shape=[jax.ShapeDtypeStruct((len(sources), *PIECE), BF16)] * PARTS,
        scratch_shapes=[pltpu.VMEM((ROWS * PITCH, 128), F32)] * 3,
        compiler_params=pltpu.CompilerParams(vmem_limit_bytes=32 * 2**20),
        cost_estimate=cost(len(sources)),
        name="forward_zy",
    )(column, target, *cuts, jnp.asarray(Z_TABLES, BF16), y_table)


def middle_body(member, *refs):
    pieces, (kernel, x_table, x_back), outs, (head0, head1, tail) = refs[:8], refs[8:11], refs[11:19], refs[19:]
    lots = (head0, head1, tail)
    block = QUADS * 2 * ROWS
    places = [pl.ds(pl.multiple_of((member[0] ^ part) * block, 8), block) for part in range(PARTS)]
    low = lax.broadcasted_iota(jnp.int32, (DUOS, 128), 1) < 64

    def step(i, carry):
        here = pl.ds(i, DUOS, stride=ROWS)
        there = pl.ds(i + ROWS // 2, DUOS, stride=ROWS)
        tail_a, tail_b = tail[here, :], tail[there, :]
        tail_first = jnp.where(low, tail_a, pltpu.roll(tail_b, 64, 1))
        tail_second = jnp.where(low, pltpu.roll(tail_a, 64, 1), tail_b)
        columns = jnp.concatenate(
            [
                jnp.concatenate([head0[here, :], head0[there, :], tail_first], axis=1),
                jnp.concatenate([head1[here, :], head1[there, :], tail_second], axis=1),
            ],
            axis=0,
        ).astype(BF16)
        spectrum = (kernel[i] * dot(x_table[...], columns)).astype(BF16)
        back = dot(x_back[...], spectrum)
        head0[here, :] = back[:DUOS, :128]
        head1[here, :] = back[DUOS:, :128]
        head0[there, :] = back[:DUOS, 128:256]
        head1[there, :] = back[DUOS:, 128:256]
        first, second = back[:DUOS, 256:], back[DUOS:, 256:]
        tail[here, :] = jnp.where(low, first, pltpu.roll(second, 64, 1))
        tail[there, :] = jnp.where(low, pltpu.roll(first, 64, 1), second)
        return carry

    for which in range(pieces[0].shape[0]):
        for place, piece in zip(places, pieces):
            for tile, lot in enumerate(lots):
                lot[place, :] = piece[which, :, :, tile * 128 : (tile + 1) * 128].astype(F32).reshape(block, 128)
        lax.fori_loop(0, ROWS // 2, step, 0, unroll=6)
        for place, out in zip(places, outs):
            for tile, lot in enumerate(lots):
                out[which, :, :, tile * 128 : (tile + 1) * 128] = lot[place, :].astype(BF16).reshape(QUADS, 2 * ROWS, 128)


def middle(member, pieces, kernel):
    return pl.pallas_call(
        middle_body,
        in_specs=[SCALAR] + [VECTOR] * (PARTS + 3),
        out_specs=[VECTOR] * PARTS,
        out_shape=[jax.ShapeDtypeStruct(pieces[0].shape, BF16)] * PARTS,
        scratch_shapes=[pltpu.VMEM((DUOS * ROWS, 128), F32)] * 3,
        compiler_params=pltpu.CompilerParams(vmem_limit_bytes=32 * 2**20),
        cost_estimate=cost(pieces[0].shape[0]),
        name="middle_x",
    )(member, *pieces, kernel, jnp.asarray(X_TABLE, BF16), jnp.asarray(X_BACK, BF16))


def backward_body(column, *refs):
    pieces, refs = refs[:8], refs[8:]
    pairs = pieces[0].shape[0]
    sources, refs = refs[: 4 * pairs], refs[4 * pairs :]
    (total, y_table, z_tables, out), lots = ((None,) + refs[:3], refs[3:]) if len(refs) == 6 else (refs[:4], refs[4:])

    for which in range(pairs):

        def planes(quad, carry, which=which):
            parts = [piece[which, quad].astype(F32) for piece in pieces]
            stacks = [
                jnp.concatenate([part[pair * ROWS : (pair + 1) * ROWS] for part in parts], axis=0) for pair in range(2)
            ]
            both = dot(y_table[...], jnp.concatenate(stacks, axis=1).astype(BF16)).astype(BF16)
            for pair in range(2):
                fields = both[:, pair * 384 : (pair + 1) * 384]
                for plane in range(2):
                    lanes = fields[:, 128:] if plane else jnp.concatenate([fields[:, :128], fields[:, 256:]], axis=1)
                    even = dot(lanes[:DUOS], z_tables[2 * plane])
                    odd = dot(lanes[DUOS:], z_tables[2 * plane + 1])
                    rows = pl.ds(pl.multiple_of((quad * 4 + pair * 2 + plane) * PITCH, 8), DUOS)
                    lots[0][rows, :] = even[:, :128]
                    lots[1][rows, :] = even[:, 128:] + odd[:, :128]
                    lots[2][rows, :] = odd[:, 128:]
            return carry

        lax.fori_loop(0, QUADS, planes, 0, unroll=3)
        base = total if which == 0 else out

        for slot in range(4):
            source = sources[which * 4 + slot]

            def gather(part, carry, source=source, slot=slot, base=base):
                duo = (column[0] ^ slot) * PER_CUT + part
                potential = tiles(lots, pl.ds(duo, ROWS, stride=PITCH))
                here = pl.ds(pl.multiple_of(duo * 384, 128), 384)
                right = source[:, pl.ds(pl.multiple_of(part * 384, 128), 384)].astype(F32)
                term = potential * right
                out[:, here] = -term if base is None else base[:, here] - term
                return carry

            lax.fori_loop(0, PER_CUT, gather, 0, unroll=12)


def backward(column, pieces, sources, total, y_table):
    cuts = [cut for source in sources for cut in source]
    return pl.pallas_call(
        backward_body,
        in_specs=[SCALAR] + [VECTOR] * (PARTS + len(cuts) + 2 + (total is not None)),
        out_specs=VECTOR,
        out_shape=jax.ShapeDtypeStruct((ROWS, CELLS), F32),
        scratch_shapes=[pltpu.VMEM((ROWS * PITCH, 128), F32)] * 3,
        compiler_params=pltpu.CompilerParams(vmem_limit_bytes=32 * 2**20),
        cost_estimate=cost(len(sources)),
        name="backward_yz",
    )(column, *pieces, *cuts, *([] if total is None else [total]), y_table, jnp.asarray(Z_BACKS, BF16))


def exchange(pieces):
    return [pieces[0]] + [
        lax.ppermute(pieces[d], "grid", [(i, i ^ d) for i in range(PARTS)]) for d in range(1, PARTS)
    ]


def band_of(z_hi, x, core):
    return z_hi % 4 * 8 + x * 2 + core


def move(array, pairs):
    return lax.ppermute(array, "band", pairs)


def after(array, *others):
    return lax.optimization_barrier((array, *others))[0]


def scatter(orbital, x):
    cut = CELLS // 4
    mine = jnp.where(x == 0, orbital[:, :cut], jnp.zeros((), BF16))
    for step in range(1, 4):
        pairs = [(band_of(z, 0, 0), band_of(z, step, 0)) for z in (0, 2)]
        mine = mine + move(orbital[:, step * cut : (step + 1) * cut], pairs)
    return mine


def along_z(mine, root, z_hi):
    away = sum(move(mine, [(band_of(root, x, 0), band_of(root + up, x, 0)) for x in range(4)]) for up in (1, 3, 2))
    return jnp.where(z_hi == root, mine, away)


def gather_x(mine, core):
    other = move(mine, [(band_of(z, x, 0), band_of(z, x, 1)) for z in range(4) for x in range(4)])
    mine = jnp.where(core == 0, mine, other)
    return [mine] + [
        move(mine, [(band_of(z, x, c), band_of(z, x ^ step, c)) for z in range(4) for x in range(4) for c in range(2)])
        for step in range(1, 4)
    ]


def local(orbitals):
    band, grid = lax.axis_index("band"), lax.axis_index("grid")
    z_hi, x, core = band // 8, (band // 2) % 4, band % 2
    column, member = x[None].astype(jnp.int32), grid[None].astype(jnp.int32)
    by_partner = ((grid ^ jnp.arange(PARTS))[:, None] * ROWS + jnp.arange(ROWS)).reshape(-1)
    y_table = jnp.asarray(Y_TABLE, BF16)[by_partner]
    y_back = y_table.T
    kernel = coulomb(grid)
    target = orbitals[0]

    cut_0 = scatter(orbitals[0], x)
    spread_0 = along_z(cut_0, 0, z_hi)
    source_0 = gather_x(spread_0, core)
    cut_0 = after(cut_0, spread_0)
    spread_2 = along_z(cut_0, 2, z_hi)
    source_2 = gather_x(after(spread_2, *source_0), core)
    cut_1 = scatter(after(orbitals[1], spread_0), x)
    spread_1 = along_z(after(cut_1, spread_2), 0, z_hi)
    source_1 = gather_x(after(spread_1, *source_2), core)
    spread_3 = along_z(after(cut_1, spread_1), 2, z_hi)
    source_3 = gather_x(after(spread_3, *source_1), core)

    batches = [[source_0], [source_2, source_1], [source_3]]
    there = [exchange(forward(column, target, batch, y_table)) for batch in batches]
    backs = [exchange(middle(member, pieces, kernel)) for pieces in there]
    total = None
    for pieces, batch in zip(backs, batches):
        total = backward(column, pieces, batch, total, y_back)
    return total[None]


def solution(mesh):
    return jax.shard_map(
        local,
        mesh=mesh,
        in_specs=(P("band", "grid", None),),
        out_specs=P("band", "grid", None),
        check_vma=False,
    )
```

```python
import jax
import jax.numpy as jnp
import numpy as np
from jax import lax
from jax.experimental import pallas as pl
from jax.experimental.pallas import tpu as pltpu
from jax.sharding import PartitionSpec as P

SIDE = 192
PARTS = 8
ROWS = SIDE // PARTS
QUADS = ROWS // 4
DUOS = SIDE // 2
CELLS = SIDE * SIDE
COUL = 160.0
PITCH = 104
PER_CUT = DUOS // 4
PIECE = (QUADS, 2 * ROWS, 384)
VECTOR = pl.BlockSpec(memory_space=pltpu.VMEM)
SCALAR = pl.BlockSpec(memory_space=pltpu.SMEM)
F32 = jnp.float32
BF16 = jnp.bfloat16


def cas_matrix():
    index = np.arange(SIDE, dtype=np.int32)
    phases = (index[:, None] * index[None, :] % SIDE).astype(np.float32) * np.float32(2.0 * np.pi / SIDE)
    return np.cos(phases) + np.sin(phases)


CAS = cas_matrix()
BY_PARITY = np.concatenate([np.arange(0, SIDE, 2), np.arange(1, SIDE, 2)])
Y_TABLE = CAS[:, BY_PARITY]
Y_BACK = CAS[BY_PARITY, :]
X_TABLE = CAS[:, BY_PARITY]
X_BACK = CAS[BY_PARITY, :]


def z_tables():
    gap = np.zeros((64, 256), np.float32)
    space = np.zeros((SIDE, 64), np.float32)
    first = np.concatenate([CAS, space], axis=1)
    second = np.concatenate([CAS[:, :128], space, CAS[:, 128:]], axis=1)
    return np.stack([np.concatenate(part, axis=0) for table in (first, second) for part in ((table, gap), (gap, table))])


Z_TABLES = z_tables()
Z_BACKS = np.swapaxes(Z_TABLES, 1, 2)


def wave(index):
    return jnp.where(index < SIDE // 2, index, index - SIDE).astype(F32)


def coulomb(me):
    shape = (ROWS // 2, SIDE, 384)
    pair = lax.broadcasted_iota(jnp.int32, shape, 0)
    row = lax.broadcasted_iota(jnp.int32, shape, 1)
    col = lax.broadcasted_iota(jnp.int32, shape, 2)
    late = jnp.where(col < 256, col >= 128, col >= 320)
    kz = jnp.where(col < 256, col % 128, 128 + col % 64)
    ky = me * ROWS + pair + jnp.where(late, ROWS // 2, 0)
    mx, my, mz = wave(row), wave(ky), wave(kz)
    norm_sq = mx * mx + my * my + mz * mz
    bounded = jnp.maximum(norm_sq, 1.0)
    return jnp.where(norm_sq > 0.5, COUL / bounded, 0.0) / float(SIDE) ** 3


def dot(left, right):
    return jnp.dot(left, right, preferred_element_type=F32)


def tiles(lots, rows):
    return jnp.concatenate([lot[rows, :] for lot in lots], axis=1)


def forward_body(column, target, *refs):
    sources, (z_tables, y_table, out), lots = refs[:-6], refs[-6:-3], refs[-3:]
    for which in range(len(sources) // 4):
        for slot in range(4):
            source = sources[which * 4 + slot]

            def form(part, carry, source=source, slot=slot):
                duo = (column[0] ^ slot) * PER_CUT + part
                left = target[:, pl.ds(pl.multiple_of(duo * 384, 128), 384)].astype(F32)
                right = source[:, pl.ds(pl.multiple_of(part * 384, 128), 384)].astype(F32)
                density = left * right
                for tile, lot in enumerate(lots):
                    lot[pl.ds(duo, ROWS, stride=PITCH), :] = density[:, tile * 128 : (tile + 1) * 128]
                return carry

            lax.fori_loop(0, PER_CUT, form, 0, unroll=12)

        def planes(quad, carry, which=which):
            along_z = []
            for pair in range(2):
                halves = []
                for plane in range(2):
                    rows = pl.ds(pl.multiple_of((quad * 4 + pair * 2 + plane) * PITCH, 8), DUOS)
                    density = tiles(lots, rows).astype(BF16)
                    even = dot(density[:, :256], z_tables[2 * plane])
                    odd = dot(density[:, 128:], z_tables[2 * plane + 1])
                    halves.append(jnp.concatenate([even, odd], axis=0))
                low, high = halves
                along_z += [low[:, :128], high[:, :128], low[:, 128:] + high[:, 128:]]
            along_y = dot(y_table[...], jnp.concatenate(along_z, axis=1).astype(BF16))
            for part in range(PARTS):
                rows = slice(part * ROWS, (part + 1) * ROWS)
                out[part, which, quad] = jnp.concatenate([along_y[rows, :384], along_y[rows, 384:]], axis=0).astype(BF16)
            return carry

        lax.fori_loop(0, QUADS, planes, 0, unroll=6)


def cost(pairs):
    return pl.CostEstimate(flops=pairs * 1400 * 10**6, bytes_accessed=pairs * 7 * 10**6, transcendentals=0)


def forward(column, target, sources):
    cuts = [cut for source in sources for cut in source]
    return pl.pallas_call(
        forward_body,
        in_specs=[SCALAR] + [VECTOR] * (len(cuts) + 3),
        out_specs=VECTOR,
        out_shape=jax.ShapeDtypeStruct((PARTS, len(sources), *PIECE), BF16),
        scratch_shapes=[pltpu.VMEM((ROWS * PITCH, 128), F32)] * 3,
        compiler_params=pltpu.CompilerParams(vmem_limit_bytes=32 * 2**20),
        cost_estimate=cost(len(sources)),
        name="forward_zy",
    )(column, target, *cuts, jnp.asarray(Z_TABLES, BF16), jnp.asarray(Y_TABLE, BF16))


def middle_body(pieces, kernel, x_table, x_back, out, head0, head1, tail):
    lots = (head0, head1, tail)
    block = QUADS * 2 * ROWS
    low = lax.broadcasted_iota(jnp.int32, (DUOS, 128), 1) < 64

    def step(i, carry):
        here = pl.ds(i, DUOS, stride=ROWS)
        there = pl.ds(i + ROWS // 2, DUOS, stride=ROWS)
        tail_a, tail_b = tail[here, :], tail[there, :]
        tail_first = jnp.where(low, tail_a, pltpu.roll(tail_b, 64, 1))
        tail_second = jnp.where(low, pltpu.roll(tail_a, 64, 1), tail_b)
        columns = jnp.concatenate(
            [
                jnp.concatenate([head0[here, :], head0[there, :], tail_first], axis=1),
                jnp.concatenate([head1[here, :], head1[there, :], tail_second], axis=1),
            ],
            axis=0,
        ).astype(BF16)
        spectrum = (kernel[i] * dot(x_table[...], columns)).astype(BF16)
        back = dot(x_back[...], spectrum)
        head0[here, :] = back[:DUOS, :128]
        head1[here, :] = back[DUOS:, :128]
        head0[there, :] = back[:DUOS, 128:256]
        head1[there, :] = back[DUOS:, 128:256]
        first, second = back[:DUOS, 256:], back[DUOS:, 256:]
        tail[here, :] = jnp.where(low, first, pltpu.roll(second, 64, 1))
        tail[there, :] = jnp.where(low, pltpu.roll(first, 64, 1), second)
        return carry

    for which in range(pieces.shape[1]):
        for part in range(PARTS):
            for tile, lot in enumerate(lots):
                lot[part * block : (part + 1) * block] = (
                    pieces[part, which, :, :, tile * 128 : (tile + 1) * 128].astype(F32).reshape(block, 128)
                )
        lax.fori_loop(0, ROWS // 2, step, 0, unroll=6)
        for part in range(PARTS):
            for tile, lot in enumerate(lots):
                out[part, which, :, :, tile * 128 : (tile + 1) * 128] = (
                    lot[part * block : (part + 1) * block].astype(BF16).reshape(QUADS, 2 * ROWS, 128)
                )


def middle(pieces, kernel):
    return pl.pallas_call(
        middle_body,
        in_specs=[VECTOR] * 4,
        out_specs=VECTOR,
        out_shape=jax.ShapeDtypeStruct(pieces.shape, BF16),
        scratch_shapes=[pltpu.VMEM((DUOS * ROWS, 128), F32)] * 3,
        compiler_params=pltpu.CompilerParams(vmem_limit_bytes=32 * 2**20),
        cost_estimate=cost(pieces.shape[1]),
        name="middle_x",
    )(pieces, kernel, jnp.asarray(X_TABLE, BF16), jnp.asarray(X_BACK, BF16))


def backward_body(column, pieces, *refs):
    pairs = pieces.shape[1]
    sources, refs = refs[: 4 * pairs], refs[4 * pairs :]
    (total, y_table, z_tables, out), lots = ((None,) + refs[:3], refs[3:]) if len(refs) == 6 else (refs[:4], refs[4:])

    for which in range(pairs):

        def planes(quad, carry, which=which):
            parts = [pieces[part, which, quad].astype(F32) for part in range(PARTS)]
            stacks = [
                jnp.concatenate([part[pair * ROWS : (pair + 1) * ROWS] for part in parts], axis=0) for pair in range(2)
            ]
            both = dot(y_table[...], jnp.concatenate(stacks, axis=1).astype(BF16)).astype(BF16)
            for pair in range(2):
                fields = both[:, pair * 384 : (pair + 1) * 384]
                for plane in range(2):
                    lanes = fields[:, 128:] if plane else jnp.concatenate([fields[:, :128], fields[:, 256:]], axis=1)
                    even = dot(lanes[:DUOS], z_tables[2 * plane])
                    odd = dot(lanes[DUOS:], z_tables[2 * plane + 1])
                    rows = pl.ds(pl.multiple_of((quad * 4 + pair * 2 + plane) * PITCH, 8), DUOS)
                    lots[0][rows, :] = even[:, :128]
                    lots[1][rows, :] = even[:, 128:] + odd[:, :128]
                    lots[2][rows, :] = odd[:, 128:]
            return carry

        lax.fori_loop(0, QUADS, planes, 0, unroll=3)
        base = total if which == 0 else out

        for slot in range(4):
            source = sources[which * 4 + slot]

            def gather(part, carry, source=source, slot=slot, base=base):
                duo = (column[0] ^ slot) * PER_CUT + part
                potential = tiles(lots, pl.ds(duo, ROWS, stride=PITCH))
                here = pl.ds(pl.multiple_of(duo * 384, 128), 384)
                right = source[:, pl.ds(pl.multiple_of(part * 384, 128), 384)].astype(F32)
                term = potential * right
                out[:, here] = -term if base is None else base[:, here] - term
                return carry

            lax.fori_loop(0, PER_CUT, gather, 0, unroll=12)


def backward(column, pieces, sources, total):
    cuts = [cut for source in sources for cut in source]
    return pl.pallas_call(
        backward_body,
        in_specs=[SCALAR] + [VECTOR] * (1 + len(cuts) + 2 + (total is not None)),
        out_specs=VECTOR,
        out_shape=jax.ShapeDtypeStruct((ROWS, CELLS), F32),
        scratch_shapes=[pltpu.VMEM((ROWS * PITCH, 128), F32)] * 3,
        compiler_params=pltpu.CompilerParams(vmem_limit_bytes=32 * 2**20),
        cost_estimate=cost(len(sources)),
        name="backward_yz",
    )(column, pieces, *cuts, *([] if total is None else [total]), jnp.asarray(Y_BACK, BF16), jnp.asarray(Z_BACKS, BF16))


def exchange(pieces):
    return lax.all_to_all(pieces, "grid", 0, 0, tiled=True)


def band_of(z_hi, x, core):
    return z_hi % 4 * 8 + x * 2 + core


def move(array, pairs):
    return lax.ppermute(array, "band", pairs)


def after(array, *others):
    return lax.optimization_barrier((array, *others))[0]


def scatter(orbital):
    cut = CELLS // 4
    return sum(
        move(
            orbital[:, step * cut : (step + 1) * cut],
            [(band_of(2 * root, 0, 0), band_of(2 * root, step, root)) for root in range(2)],
        )
        for step in range(4)
    )


def beside(mine, is_root):
    away = sum(
        move(mine, [(band_of(2 * c, x, c), band_of(2 * c + up, x, c)) for c in range(2) for x in range(4)]) for up in (1, 3)
    )
    return jnp.where(is_root, mine, away)


def beyond(mine):
    half = mine.shape[1] // 2
    parts = [
        move(part, [(band_of(2 * c + up, x, c), band_of(2 * c + 2, x, c)) for c in range(2) for x in range(4)])
        for up, part in ((1, mine[:, :half]), (3, mine[:, half:]))
    ]
    return mine + jnp.concatenate(parts, axis=1)


def gather_x(mine):
    return [mine] + [
        move(mine, [(band_of(z, x, c), band_of(z, x ^ step, c)) for z in range(4) for x in range(4) for c in range(2)])
        for step in range(1, 4)
    ]


def other_core(source):
    pairs = [(band_of(z, x, c), band_of(z, x, 1 - c)) for z in range(4) for x in range(4) for c in range(2)]
    return [move(cut, pairs) for cut in source]


def local(orbitals):
    band = lax.axis_index("band")
    z_hi, x, core = band // 8, (band // 2) % 4, band % 2
    column = x[None].astype(jnp.int32)
    kernel = coulomb(lax.axis_index("grid"))
    target = orbitals[0]
    is_root = z_hi == 2 * core

    cut_0 = scatter(orbitals[0])
    near_0 = beside(cut_0, is_root)
    cut_1 = scatter(after(orbitals[1], near_0))
    full_0 = beyond(near_0)
    mine_0 = gather_x(full_0)
    near_1 = beside(after(cut_1, full_0), is_root)
    full_1 = beyond(near_1)
    mine_1 = gather_x(after(full_1, *mine_0))

    batches = [[mine_0], [other_core(mine_0), mine_1], [other_core(mine_1)]]
    there = [exchange(forward(column, target, batch)) for batch in batches]
    backs = [exchange(middle(pieces, kernel)) for pieces in there]
    total = None
    for pieces, batch in zip(backs, batches):
        total = backward(column, pieces, batch, total)
    return total[None]


def solution(mesh):
    return jax.shard_map(
        local,
        mesh=mesh,
        in_specs=(P("band", "grid", None),),
        out_specs=P("band", "grid", None),
        check_vma=False,
    )
```

```python
import jax
import jax.numpy as jnp
import numpy as np
from jax import lax
from jax.experimental import pallas as pl
from jax.experimental.pallas import tpu as pltpu
from jax.sharding import PartitionSpec as P

SIDE = 192
PARTS = 8
ROWS = SIDE // PARTS
QUADS = ROWS // 4
DUOS = SIDE // 2
CELLS = SIDE * SIDE
COUL = 160.0
PITCH = 104
PER_CUT = DUOS // 4
PIECE = (QUADS, 2 * ROWS, 384)
VECTOR = pl.BlockSpec(memory_space=pltpu.VMEM)
SCALAR = pl.BlockSpec(memory_space=pltpu.SMEM)
F32 = jnp.float32
BF16 = jnp.bfloat16


def cas_matrix():
    index = np.arange(SIDE, dtype=np.int32)
    phases = (index[:, None] * index[None, :] % SIDE).astype(np.float32) * np.float32(2.0 * np.pi / SIDE)
    return np.cos(phases) + np.sin(phases)


CAS = cas_matrix()
BY_PARITY = np.concatenate([np.arange(0, SIDE, 2), np.arange(1, SIDE, 2)])
Y_TABLE = CAS[:, BY_PARITY]
Y_BACK = CAS[BY_PARITY, :]
X_TABLE = CAS[:, BY_PARITY]
X_BACK = CAS[BY_PARITY, :]


def z_tables():
    gap = np.zeros((64, 256), np.float32)
    space = np.zeros((SIDE, 64), np.float32)
    first = np.concatenate([CAS, space], axis=1)
    second = np.concatenate([CAS[:, :128], space, CAS[:, 128:]], axis=1)
    return np.stack([np.concatenate(part, axis=0) for table in (first, second) for part in ((table, gap), (gap, table))])


Z_TABLES = z_tables()
Z_BACKS = np.swapaxes(Z_TABLES, 1, 2)


def wave(index):
    return jnp.where(index < SIDE // 2, index, index - SIDE).astype(F32)


def coulomb(me):
    shape = (ROWS // 2, SIDE, 384)
    pair = lax.broadcasted_iota(jnp.int32, shape, 0)
    row = lax.broadcasted_iota(jnp.int32, shape, 1)
    col = lax.broadcasted_iota(jnp.int32, shape, 2)
    late = jnp.where(col < 256, col >= 128, col >= 320)
    kz = jnp.where(col < 256, col % 128, 128 + col % 64)
    ky = me * ROWS + pair + jnp.where(late, ROWS // 2, 0)
    mx, my, mz = wave(row), wave(ky), wave(kz)
    norm_sq = mx * mx + my * my + mz * mz
    bounded = jnp.maximum(norm_sq, 1.0)
    return jnp.where(norm_sq > 0.5, COUL / bounded, 0.0) / float(SIDE) ** 3


def dot(left, right):
    return jnp.dot(left, right, preferred_element_type=F32)


def tiles(lots, rows):
    return jnp.concatenate([lot[rows, :] for lot in lots], axis=1)


def forward_body(column, target, *refs):
    sources, (z_tables, y_table, out), lots = refs[:-6], refs[-6:-3], refs[-3:]
    for which in range(len(sources) // 4):
        for slot in range(4):
            source = sources[which * 4 + slot]

            def form(part, carry, source=source, slot=slot):
                duo = (column[0] ^ slot) * PER_CUT + part
                left = target[:, pl.ds(pl.multiple_of(duo * 384, 128), 384)].astype(F32)
                right = source[:, pl.ds(pl.multiple_of(part * 384, 128), 384)].astype(F32)
                density = left * right
                for tile, lot in enumerate(lots):
                    lot[pl.ds(duo, ROWS, stride=PITCH), :] = density[:, tile * 128 : (tile + 1) * 128]
                return carry

            lax.fori_loop(0, PER_CUT, form, 0, unroll=12)

        def planes(quad, carry, which=which):
            along_z = []
            for pair in range(2):
                halves = []
                for plane in range(2):
                    rows = pl.ds(pl.multiple_of((quad * 4 + pair * 2 + plane) * PITCH, 8), DUOS)
                    density = tiles(lots, rows).astype(BF16)
                    even = dot(density[:, :256], z_tables[2 * plane])
                    odd = dot(density[:, 128:], z_tables[2 * plane + 1])
                    halves.append(jnp.concatenate([even, odd], axis=0))
                low, high = halves
                along_z += [low[:, :128], high[:, :128], low[:, 128:] + high[:, 128:]]
            along_y = dot(y_table[...], jnp.concatenate(along_z, axis=1).astype(BF16))
            for part in range(PARTS):
                rows = slice(part * ROWS, (part + 1) * ROWS)
                out[part, which, quad] = jnp.concatenate([along_y[rows, :384], along_y[rows, 384:]], axis=0).astype(BF16)
            return carry

        lax.fori_loop(0, QUADS, planes, 0, unroll=6)


def cost(pairs):
    return pl.CostEstimate(flops=pairs * 1400 * 10**6, bytes_accessed=pairs * 7 * 10**6, transcendentals=0)


def forward(column, target, sources):
    cuts = [cut for source in sources for cut in source]
    return pl.pallas_call(
        forward_body,
        in_specs=[SCALAR] + [VECTOR] * (len(cuts) + 3),
        out_specs=VECTOR,
        out_shape=jax.ShapeDtypeStruct((PARTS, len(sources), *PIECE), BF16),
        scratch_shapes=[pltpu.VMEM((ROWS * PITCH, 128), F32)] * 3,
        compiler_params=pltpu.CompilerParams(vmem_limit_bytes=16 * 2**20),
        cost_estimate=cost(len(sources)),
        name="forward_zy",
    )(column, target, *cuts, jnp.asarray(Z_TABLES, BF16), jnp.asarray(Y_TABLE, BF16))


def middle_body(pieces, kernel, x_table, x_back, out, head0, head1, tail):
    lots = (head0, head1, tail)
    block = QUADS * 2 * ROWS
    low = lax.broadcasted_iota(jnp.int32, (DUOS, 128), 1) < 64

    def step(i, carry):
        here = pl.ds(i, DUOS, stride=ROWS)
        there = pl.ds(i + ROWS // 2, DUOS, stride=ROWS)
        tail_a, tail_b = tail[here, :], tail[there, :]
        tail_first = jnp.where(low, tail_a, pltpu.roll(tail_b, 64, 1))
        tail_second = jnp.where(low, pltpu.roll(tail_a, 64, 1), tail_b)
        columns = jnp.concatenate(
            [
                jnp.concatenate([head0[here, :], head0[there, :], tail_first], axis=1),
                jnp.concatenate([head1[here, :], head1[there, :], tail_second], axis=1),
            ],
            axis=0,
        ).astype(BF16)
        spectrum = (kernel[i] * dot(x_table[...], columns)).astype(BF16)
        back = dot(x_back[...], spectrum)
        head0[here, :] = back[:DUOS, :128]
        head1[here, :] = back[DUOS:, :128]
        head0[there, :] = back[:DUOS, 128:256]
        head1[there, :] = back[DUOS:, 128:256]
        first, second = back[:DUOS, 256:], back[DUOS:, 256:]
        tail[here, :] = jnp.where(low, first, pltpu.roll(second, 64, 1))
        tail[there, :] = jnp.where(low, pltpu.roll(first, 64, 1), second)
        return carry

    for which in range(pieces.shape[1]):
        for part in range(PARTS):
            for tile, lot in enumerate(lots):
                lot[part * block : (part + 1) * block] = (
                    pieces[part, which, :, :, tile * 128 : (tile + 1) * 128].astype(F32).reshape(block, 128)
                )
        lax.fori_loop(0, ROWS // 2, step, 0, unroll=6)
        for part in range(PARTS):
            for tile, lot in enumerate(lots):
                out[part, which, :, :, tile * 128 : (tile + 1) * 128] = (
                    lot[part * block : (part + 1) * block].astype(BF16).reshape(QUADS, 2 * ROWS, 128)
                )


def middle(pieces, kernel):
    return pl.pallas_call(
        middle_body,
        in_specs=[VECTOR] * 4,
        out_specs=VECTOR,
        out_shape=jax.ShapeDtypeStruct(pieces.shape, BF16),
        scratch_shapes=[pltpu.VMEM((DUOS * ROWS, 128), F32)] * 3,
        compiler_params=pltpu.CompilerParams(vmem_limit_bytes=16 * 2**20),
        cost_estimate=cost(pieces.shape[1]),
        name="middle_x",
    )(pieces, kernel, jnp.asarray(X_TABLE, BF16), jnp.asarray(X_BACK, BF16))


def backward_body(column, pieces, *refs):
    pairs = pieces.shape[1]
    sources, refs = refs[: 4 * pairs], refs[4 * pairs :]
    (total, y_table, z_tables, out), lots = ((None,) + refs[:3], refs[3:]) if len(refs) == 6 else (refs[:4], refs[4:])

    for which in range(pairs):

        def planes(quad, carry, which=which):
            parts = [pieces[part, which, quad].astype(F32) for part in range(PARTS)]
            stacks = [
                jnp.concatenate([part[pair * ROWS : (pair + 1) * ROWS] for part in parts], axis=0) for pair in range(2)
            ]
            both = dot(y_table[...], jnp.concatenate(stacks, axis=1).astype(BF16)).astype(BF16)
            for pair in range(2):
                fields = both[:, pair * 384 : (pair + 1) * 384]
                for plane in range(2):
                    lanes = fields[:, 128:] if plane else jnp.concatenate([fields[:, :128], fields[:, 256:]], axis=1)
                    even = dot(lanes[:DUOS], z_tables[2 * plane])
                    odd = dot(lanes[DUOS:], z_tables[2 * plane + 1])
                    rows = pl.ds(pl.multiple_of((quad * 4 + pair * 2 + plane) * PITCH, 8), DUOS)
                    lots[0][rows, :] = even[:, :128]
                    lots[1][rows, :] = even[:, 128:] + odd[:, :128]
                    lots[2][rows, :] = odd[:, 128:]
            return carry

        lax.fori_loop(0, QUADS, planes, 0, unroll=3)
        base = total if which == 0 else out

        for slot in range(4):
            source = sources[which * 4 + slot]

            def gather(part, carry, source=source, slot=slot, base=base):
                duo = (column[0] ^ slot) * PER_CUT + part
                potential = tiles(lots, pl.ds(duo, ROWS, stride=PITCH))
                here = pl.ds(pl.multiple_of(duo * 384, 128), 384)
                right = source[:, pl.ds(pl.multiple_of(part * 384, 128), 384)].astype(F32)
                term = potential * right
                out[:, here] = -term if base is None else base[:, here] - term
                return carry

            lax.fori_loop(0, PER_CUT, gather, 0, unroll=12)


def backward(column, pieces, sources, total):
    cuts = [cut for source in sources for cut in source]
    return pl.pallas_call(
        backward_body,
        in_specs=[SCALAR] + [VECTOR] * (1 + len(cuts) + 2 + (total is not None)),
        out_specs=VECTOR,
        out_shape=jax.ShapeDtypeStruct((ROWS, CELLS), F32),
        scratch_shapes=[pltpu.VMEM((ROWS * PITCH, 128), F32)] * 3,
        compiler_params=pltpu.CompilerParams(vmem_limit_bytes=16 * 2**20),
        cost_estimate=cost(len(sources)),
        name="backward_yz",
    )(column, pieces, *cuts, *([] if total is None else [total]), jnp.asarray(Y_BACK, BF16), jnp.asarray(Z_BACKS, BF16))


def exchange(pieces):
    return lax.all_to_all(pieces, "grid", 0, 0, tiled=True)


def band_of(z_hi, x, core):
    return z_hi % 4 * 8 + x * 2 + core


def move(array, pairs):
    return lax.ppermute(array, "band", pairs)


def after(array, *others):
    return lax.optimization_barrier((array, *others))[0]


def scatter(orbital):
    cut = CELLS // 4
    return sum(
        move(
            orbital[:, step * cut : (step + 1) * cut],
            [(band_of(2 * root, 0, 0), band_of(2 * root, step, root)) for root in range(2)],
        )
        for step in range(4)
    )


def beside(mine, is_root):
    away = sum(
        move(mine, [(band_of(2 * c, x, c), band_of(2 * c + up, x, c)) for c in range(2) for x in range(4)]) for up in (1, 3)
    )
    return jnp.where(is_root, mine, away)


def beyond(mine):
    half = mine.shape[1] // 2
    parts = [
        move(part, [(band_of(2 * c + up, x, c), band_of(2 * c + 2, x, c)) for c in range(2) for x in range(4)])
        for up, part in ((1, mine[:, :half]), (3, mine[:, half:]))
    ]
    return mine + jnp.concatenate(parts, axis=1)


def gather_x(mine):
    return [mine] + [
        move(mine, [(band_of(z, x, c), band_of(z, x ^ step, c)) for z in range(4) for x in range(4) for c in range(2)])
        for step in range(1, 4)
    ]


def other_core(source):
    pairs = [(band_of(z, x, c), band_of(z, x, 1 - c)) for z in range(4) for x in range(4) for c in range(2)]
    return [move(cut, pairs) for cut in source]


def local(orbitals):
    band = lax.axis_index("band")
    z_hi, x, core = band // 8, (band // 2) % 4, band % 2
    column = x[None].astype(jnp.int32)
    kernel = coulomb(lax.axis_index("grid"))
    target = orbitals[0]
    is_root = z_hi == 2 * core

    cut_0 = scatter(orbitals[0])
    cut_1 = scatter(after(orbitals[1], cut_0))
    full_0 = beyond(beside(cut_0, is_root))
    mine_0 = gather_x(full_0)
    other_0 = other_core(mine_0)
    full_1 = beyond(beside(after(cut_1, full_0), is_root))
    mine_1 = gather_x(after(full_1, *mine_0))
    other_1 = other_core(mine_1)

    batches = [[mine_0], [other_0], [mine_1, other_1]]
    ready = [middle(exchange(forward(column, target, batch)), kernel) for batch in batches]
    back_0 = exchange(ready[0])
    back_2 = exchange(ready[2])
    back_1 = exchange(after(ready[1], back_2))
    total = backward(column, back_0, batches[0], None)
    total = backward(column, back_2, batches[2], total)
    total = backward(column, back_1, batches[1], total)
    return total[None]


def solution(mesh):
    return jax.shard_map(
        local,
        mesh=mesh,
        in_specs=(P("band", "grid", None),),
        out_specs=P("band", "grid", None),
        check_vma=False,
    )
```

```python
import jax
import jax.numpy as jnp
import numpy as np
from jax import lax
from jax.experimental import pallas as pl
from jax.experimental.pallas import tpu as pltpu
from jax.sharding import PartitionSpec as P

SIDE = 192
PARTS = 8
ROWS = SIDE // PARTS
QUADS = ROWS // 4
DUOS = SIDE // 2
CELLS = SIDE * SIDE
COUL = 160.0
PITCH = 104
PER_CUT = DUOS // 4
PIECE = (QUADS, 2 * ROWS, 384)
VECTOR = pl.BlockSpec(memory_space=pltpu.VMEM)
FAR = pl.BlockSpec(memory_space=pl.ANY)
SCALAR = pl.BlockSpec(memory_space=pltpu.SMEM)
F32 = jnp.float32
BF16 = jnp.bfloat16


def cas_matrix():
    index = np.arange(SIDE, dtype=np.int32)
    phases = (index[:, None] * index[None, :] % SIDE).astype(np.float32) * np.float32(2.0 * np.pi / SIDE)
    return np.cos(phases) + np.sin(phases)


CAS = cas_matrix()
BY_PARITY = np.concatenate([np.arange(0, SIDE, 2), np.arange(1, SIDE, 2)])
Y_TABLE = CAS[:, BY_PARITY]
Y_BACK = CAS[BY_PARITY, :]
X_TABLE = CAS[:, BY_PARITY]
X_BACK = CAS[BY_PARITY, :]


def z_tables():
    gap = np.zeros((64, 256), np.float32)
    space = np.zeros((SIDE, 64), np.float32)
    first = np.concatenate([CAS, space], axis=1)
    second = np.concatenate([CAS[:, :128], space, CAS[:, 128:]], axis=1)
    return np.stack([np.concatenate(part, axis=0) for table in (first, second) for part in ((table, gap), (gap, table))])


Z_TABLES = z_tables()
Z_BACKS = np.swapaxes(Z_TABLES, 1, 2)


def wave(index):
    return jnp.where(index < SIDE // 2, index, index - SIDE).astype(F32)


def coulomb(me):
    shape = (ROWS // 2, SIDE, 384)
    pair = lax.broadcasted_iota(jnp.int32, shape, 0)
    row = lax.broadcasted_iota(jnp.int32, shape, 1)
    col = lax.broadcasted_iota(jnp.int32, shape, 2)
    late = jnp.where(col < 256, col >= 128, col >= 320)
    kz = jnp.where(col < 256, col % 128, 128 + col % 64)
    ky = me * ROWS + pair + jnp.where(late, ROWS // 2, 0)
    mx, my, mz = wave(row), wave(ky), wave(kz)
    norm_sq = mx * mx + my * my + mz * mz
    bounded = jnp.maximum(norm_sq, 1.0)
    return jnp.where(norm_sq > 0.5, COUL / bounded, 0.0) / float(SIDE) ** 3


def dot(left, right):
    return jnp.dot(left, right, preferred_element_type=F32)


def tiles(lots, rows):
    return jnp.concatenate([lot[rows, :] for lot in lots], axis=1)


def forward_body(column, target, *refs):
    sources, (z_tables, y_table, out), lots = refs[:-6], refs[-6:-3], refs[-3:]
    for which in range(len(sources) // 4):
        for slot in range(4):
            source = sources[which * 4 + slot]

            def form(part, carry, source=source, slot=slot):
                duo = (column[0] ^ slot) * PER_CUT + part
                left = target[:, pl.ds(pl.multiple_of(duo * 384, 128), 384)].astype(F32)
                right = source[:, pl.ds(pl.multiple_of(part * 384, 128), 384)].astype(F32)
                density = left * right
                for tile, lot in enumerate(lots):
                    lot[pl.ds(duo, ROWS, stride=PITCH), :] = density[:, tile * 128 : (tile + 1) * 128]
                return carry

            lax.fori_loop(0, PER_CUT, form, 0, unroll=12)

        def planes(quad, carry, which=which):
            along_z = []
            for pair in range(2):
                halves = []
                for plane in range(2):
                    rows = pl.ds(pl.multiple_of((quad * 4 + pair * 2 + plane) * PITCH, 8), DUOS)
                    density = tiles(lots, rows).astype(BF16)
                    even = dot(density[:, :256], z_tables[2 * plane])
                    odd = dot(density[:, 128:], z_tables[2 * plane + 1])
                    halves.append(jnp.concatenate([even, odd], axis=0))
                low, high = halves
                along_z += [low[:, :128], high[:, :128], low[:, 128:] + high[:, 128:]]
            along_y = dot(y_table[...], jnp.concatenate(along_z, axis=1).astype(BF16))
            for part in range(PARTS):
                rows = slice(part * ROWS, (part + 1) * ROWS)
                out[part, which, quad] = jnp.concatenate([along_y[rows, :384], along_y[rows, 384:]], axis=0).astype(BF16)
            return carry

        lax.fori_loop(0, QUADS, planes, 0, unroll=6)


def cost(pairs):
    return pl.CostEstimate(flops=pairs * 1400 * 10**6, bytes_accessed=pairs * 7 * 10**6, transcendentals=0)


def forward(column, target, sources):
    cuts = [cut for source in sources for cut in source]
    return pl.pallas_call(
        forward_body,
        in_specs=[SCALAR] + [VECTOR] * (len(cuts) + 3),
        out_specs=VECTOR,
        out_shape=jax.ShapeDtypeStruct((PARTS, len(sources), *PIECE), BF16),
        scratch_shapes=[pltpu.VMEM((ROWS * PITCH, 128), F32)] * 3,
        compiler_params=pltpu.CompilerParams(vmem_limit_bytes=16 * 2**20),
        cost_estimate=cost(len(sources)),
        name="forward_zy",
    )(column, target, *cuts, jnp.asarray(Z_TABLES, BF16), jnp.asarray(Y_TABLE, BF16))


def middle_body(pieces, kernel, x_table, x_back, out, head0, head1, tail):
    lots = (head0, head1, tail)
    block = QUADS * 2 * ROWS
    low = lax.broadcasted_iota(jnp.int32, (DUOS, 128), 1) < 64

    def step(i, carry):
        here = pl.ds(i, DUOS, stride=ROWS)
        there = pl.ds(i + ROWS // 2, DUOS, stride=ROWS)
        tail_a, tail_b = tail[here, :], tail[there, :]
        tail_first = jnp.where(low, tail_a, pltpu.roll(tail_b, 64, 1))
        tail_second = jnp.where(low, pltpu.roll(tail_a, 64, 1), tail_b)
        columns = jnp.concatenate(
            [
                jnp.concatenate([head0[here, :], head0[there, :], tail_first], axis=1),
                jnp.concatenate([head1[here, :], head1[there, :], tail_second], axis=1),
            ],
            axis=0,
        ).astype(BF16)
        spectrum = (kernel[i] * dot(x_table[...], columns)).astype(BF16)
        back = dot(x_back[...], spectrum)
        head0[here, :] = back[:DUOS, :128]
        head1[here, :] = back[DUOS:, :128]
        head0[there, :] = back[:DUOS, 128:256]
        head1[there, :] = back[DUOS:, 128:256]
        first, second = back[:DUOS, 256:], back[DUOS:, 256:]
        tail[here, :] = jnp.where(low, first, pltpu.roll(second, 64, 1))
        tail[there, :] = jnp.where(low, pltpu.roll(first, 64, 1), second)
        return carry

    for which in range(pieces.shape[1]):
        for part in range(PARTS):
            for tile, lot in enumerate(lots):
                lot[part * block : (part + 1) * block] = (
                    pieces[part, which, :, :, tile * 128 : (tile + 1) * 128].astype(F32).reshape(block, 128)
                )
        lax.fori_loop(0, ROWS // 2, step, 0, unroll=6)
        for part in range(PARTS):
            for tile, lot in enumerate(lots):
                out[part, which, :, :, tile * 128 : (tile + 1) * 128] = (
                    lot[part * block : (part + 1) * block].astype(BF16).reshape(QUADS, 2 * ROWS, 128)
                )


def middle(pieces, kernel):
    return pl.pallas_call(
        middle_body,
        in_specs=[VECTOR] * 4,
        out_specs=VECTOR,
        out_shape=jax.ShapeDtypeStruct(pieces.shape, BF16),
        scratch_shapes=[pltpu.VMEM((DUOS * ROWS, 128), F32)] * 3,
        compiler_params=pltpu.CompilerParams(vmem_limit_bytes=16 * 2**20),
        cost_estimate=cost(pieces.shape[1]),
        name="middle_x",
    )(pieces, kernel, jnp.asarray(X_TABLE, BF16), jnp.asarray(X_BACK, BF16))


def backward_body(column, far_pieces, *refs):
    pairs = far_pieces.shape[1]
    far_sources, refs = refs[: 4 * pairs], refs[4 * pairs :]
    total = refs[0] if len(refs) == 9 + 4 * pairs else None
    y_table, z_tables, out, *refs = refs[total is not None :]
    lots, (pieces, arrived), sources = refs[:3], refs[3:5], refs[5:]
    copies = [pltpu.make_async_copy(far_pieces, pieces, arrived.at[0])]
    copies += [
        pltpu.make_async_copy(far, near, arrived.at[1 + i]) for i, (far, near) in enumerate(zip(far_sources, sources))
    ]
    for copy in copies:
        copy.start()
    copies[0].wait()

    for which in range(pairs):

        def planes(quad, carry, which=which):
            parts = [pieces[part, which, quad].astype(F32) for part in range(PARTS)]
            stacks = [
                jnp.concatenate([part[pair * ROWS : (pair + 1) * ROWS] for part in parts], axis=0) for pair in range(2)
            ]
            both = dot(y_table[...], jnp.concatenate(stacks, axis=1).astype(BF16)).astype(BF16)
            for pair in range(2):
                fields = both[:, pair * 384 : (pair + 1) * 384]
                for plane in range(2):
                    lanes = fields[:, 128:] if plane else jnp.concatenate([fields[:, :128], fields[:, 256:]], axis=1)
                    even = dot(lanes[:DUOS], z_tables[2 * plane])
                    odd = dot(lanes[DUOS:], z_tables[2 * plane + 1])
                    rows = pl.ds(pl.multiple_of((quad * 4 + pair * 2 + plane) * PITCH, 8), DUOS)
                    lots[0][rows, :] = even[:, :128]
                    lots[1][rows, :] = even[:, 128:] + odd[:, :128]
                    lots[2][rows, :] = odd[:, 128:]
            return carry

        lax.fori_loop(0, QUADS, planes, 0, unroll=3)
        base = total if which == 0 else out

        for slot in range(4):
            source = sources[which * 4 + slot]
            copies[1 + which * 4 + slot].wait()

            def gather(part, carry, source=source, slot=slot, base=base):
                duo = (column[0] ^ slot) * PER_CUT + part
                potential = tiles(lots, pl.ds(duo, ROWS, stride=PITCH))
                here = pl.ds(pl.multiple_of(duo * 384, 128), 384)
                right = source[:, pl.ds(pl.multiple_of(part * 384, 128), 384)].astype(F32)
                term = potential * right
                out[:, here] = -term if base is None else base[:, here] - term
                return carry

            lax.fori_loop(0, PER_CUT, gather, 0, unroll=12)


def backward(column, pieces, sources, total):
    cuts = [cut for source in sources for cut in source]
    return pl.pallas_call(
        backward_body,
        in_specs=[SCALAR] + [FAR] * (1 + len(cuts)) + [VECTOR] * (2 + (total is not None)),
        out_specs=VECTOR,
        out_shape=jax.ShapeDtypeStruct((ROWS, CELLS), F32),
        scratch_shapes=[pltpu.VMEM((ROWS * PITCH, 128), F32)] * 3
        + [pltpu.VMEM(pieces.shape, BF16), pltpu.SemaphoreType.DMA((1 + len(cuts),))]
        + [pltpu.VMEM(cut.shape, BF16) for cut in cuts],
        compiler_params=pltpu.CompilerParams(vmem_limit_bytes=24 * 2**20),
        cost_estimate=cost(len(sources)),
        name="backward_yz",
    )(column, pieces, *cuts, *([] if total is None else [total]), jnp.asarray(Y_BACK, BF16), jnp.asarray(Z_BACKS, BF16))


def exchange(pieces):
    return lax.all_to_all(pieces, "grid", 0, 0, tiled=True)


def band_of(z_hi, x, core):
    return z_hi % 4 * 8 + x * 2 + core


def move(array, pairs):
    return lax.ppermute(array, "band", pairs)


def after(array, *others):
    return lax.optimization_barrier((array, *others))[0]


def scatter(orbital):
    cut = CELLS // 4
    return sum(
        move(
            orbital[:, step * cut : (step + 1) * cut],
            [(band_of(2 * root, 0, 0), band_of(2 * root, step, root)) for root in range(2)],
        )
        for step in range(4)
    )


def beside(mine, is_root):
    away = sum(
        move(mine, [(band_of(2 * c, x, c), band_of(2 * c + up, x, c)) for c in range(2) for x in range(4)]) for up in (1, 3)
    )
    return jnp.where(is_root, mine, away)


def beyond(mine):
    half = mine.shape[1] // 2
    parts = [
        move(part, [(band_of(2 * c + up, x, c), band_of(2 * c + 2, x, c)) for c in range(2) for x in range(4)])
        for up, part in ((1, mine[:, :half]), (3, mine[:, half:]))
    ]
    return mine + jnp.concatenate(parts, axis=1)


def gather_x(mine):
    return [mine] + [
        move(mine, [(band_of(z, x, c), band_of(z, x ^ step, c)) for z in range(4) for x in range(4) for c in range(2)])
        for step in range(1, 4)
    ]


def other_core(source):
    pairs = [(band_of(z, x, c), band_of(z, x, 1 - c)) for z in range(4) for x in range(4) for c in range(2)]
    return [move(cut, pairs) for cut in source]


def local(orbitals):
    band = lax.axis_index("band")
    z_hi, x, core = band // 8, (band // 2) % 4, band % 2
    column = x[None].astype(jnp.int32)
    kernel = coulomb(lax.axis_index("grid"))
    target = orbitals[0]
    is_root = z_hi == 2 * core

    cut_0 = scatter(orbitals[0])
    cut_1 = scatter(after(orbitals[1], cut_0))
    mine_0 = gather_x(beyond(beside(cut_0, is_root)))
    batch_0 = [mine_0, other_core(mine_0)]
    pieces_0 = forward(column, target, batch_0)
    mine_1 = gather_x(beyond(beside(after(cut_1, pieces_0), is_root)))
    batch_1 = [mine_1, other_core(mine_1)]
    pieces_1 = forward(column, target, batch_1)
    back_0 = exchange(middle(exchange(pieces_0), kernel))
    back_1 = exchange(middle(exchange(pieces_1), kernel))
    total = backward(column, back_0, batch_0, None)
    return backward(column, back_1, batch_1, total)[None]


def solution(mesh):
    return jax.shard_map(
        local,
        mesh=mesh,
        in_specs=(P("band", "grid", None),),
        out_specs=P("band", "grid", None),
        check_vma=False,
    )
```

```python
import jax
import jax.numpy as jnp
import numpy as np
from jax import lax
from jax.experimental import pallas as pl
from jax.experimental.pallas import tpu as pltpu
from jax.sharding import PartitionSpec as P

SIDE = 192
PARTS = 8
ROWS = SIDE // PARTS
QUADS = ROWS // 4
DUOS = SIDE // 2
CELLS = SIDE * SIDE
COUL = 160.0
PITCH = 104
PER_CUT = DUOS // 4
PIECE = (QUADS, 2 * ROWS, 384)
VECTOR = pl.BlockSpec(memory_space=pltpu.VMEM)
FAR = pl.BlockSpec(memory_space=pltpu.HBM)
SCALAR = pl.BlockSpec(memory_space=pltpu.SMEM)
F32 = jnp.float32
BF16 = jnp.bfloat16


def cas_matrix():
    index = np.arange(SIDE, dtype=np.int32)
    phases = (index[:, None] * index[None, :] % SIDE).astype(np.float32) * np.float32(2.0 * np.pi / SIDE)
    return np.cos(phases) + np.sin(phases)


CAS = cas_matrix()
BY_PARITY = np.concatenate([np.arange(0, SIDE, 2), np.arange(1, SIDE, 2)])
Y_TABLE = CAS[:, BY_PARITY]
Y_BACK = CAS[BY_PARITY, :]
X_TABLE = CAS[:, BY_PARITY]
X_BACK = CAS[BY_PARITY, :]


def z_tables():
    gap = np.zeros((64, 256), np.float32)
    space = np.zeros((SIDE, 64), np.float32)
    first = np.concatenate([CAS, space], axis=1)
    second = np.concatenate([CAS[:, :128], space, CAS[:, 128:]], axis=1)
    return np.stack([np.concatenate(part, axis=0) for table in (first, second) for part in ((table, gap), (gap, table))])


Z_TABLES = z_tables()
Z_BACKS = np.swapaxes(Z_TABLES, 1, 2)


def wave(index):
    return jnp.where(index < SIDE // 2, index, index - SIDE).astype(F32)


def coulomb(me):
    shape = (ROWS // 2, SIDE, 384)
    pair = lax.broadcasted_iota(jnp.int32, shape, 0)
    row = lax.broadcasted_iota(jnp.int32, shape, 1)
    col = lax.broadcasted_iota(jnp.int32, shape, 2)
    late = jnp.where(col < 256, col >= 128, col >= 320)
    kz = jnp.where(col < 256, col % 128, 128 + col % 64)
    ky = me * ROWS + pair + jnp.where(late, ROWS // 2, 0)
    mx, my, mz = wave(row), wave(ky), wave(kz)
    norm_sq = mx * mx + my * my + mz * mz
    bounded = jnp.maximum(norm_sq, 1.0)
    return jnp.where(norm_sq > 0.5, COUL / bounded, 0.0) / float(SIDE) ** 3


def dot(left, right):
    return jnp.dot(left, right, preferred_element_type=F32)


def tiles(lots, rows):
    return jnp.concatenate([lot[rows, :] for lot in lots], axis=1)


def started(pairs, semaphores):
    copies = [pltpu.make_async_copy(a, b, semaphores.at[i]) for i, (a, b) in enumerate(pairs)]
    for copy in copies:
        copy.start()
    return copies


def forward_body(column, far_target, *refs):
    pairs = (len(refs) - 9) // 9
    far_sources, (z_tables, y_table, far_out), refs = refs[: 4 * pairs], refs[4 * pairs : 4 * pairs + 3], refs[4 * pairs + 3 :]
    lots, (arrived, left, target), sources, outs = refs[:3], refs[3:6], refs[6 : 6 + 4 * pairs], refs[6 + 4 * pairs :]
    copies = started([(far_target, target), *zip(far_sources, sources)], arrived)
    copies[0].wait()
    results = []
    for which in range(pairs):
        out = outs[which]
        for slot in range(4):
            source = sources[which * 4 + slot]
            copies[1 + which * 4 + slot].wait()

            def form(part, carry, source=source, slot=slot):
                duo = (column[0] ^ slot) * PER_CUT + part
                left = target[:, pl.ds(pl.multiple_of(duo * 384, 128), 384)].astype(F32)
                right = source[:, pl.ds(pl.multiple_of(part * 384, 128), 384)].astype(F32)
                density = left * right
                for tile, lot in enumerate(lots):
                    lot[pl.ds(duo, ROWS, stride=PITCH), :] = density[:, tile * 128 : (tile + 1) * 128]
                return carry

            lax.fori_loop(0, PER_CUT, form, 0, unroll=12)

        def planes(quad, carry, out=out):
            along_z = []
            for pair in range(2):
                halves = []
                for plane in range(2):
                    rows = pl.ds(pl.multiple_of((quad * 4 + pair * 2 + plane) * PITCH, 8), DUOS)
                    density = tiles(lots, rows).astype(BF16)
                    even = dot(density[:, :256], z_tables[2 * plane])
                    odd = dot(density[:, 128:], z_tables[2 * plane + 1])
                    halves.append(jnp.concatenate([even, odd], axis=0))
                low, high = halves
                along_z += [low[:, :128], high[:, :128], low[:, 128:] + high[:, 128:]]
            along_y = dot(y_table[...], jnp.concatenate(along_z, axis=1).astype(BF16))
            for part in range(PARTS):
                rows = slice(part * ROWS, (part + 1) * ROWS)
                out[part, quad] = jnp.concatenate([along_y[rows, :384], along_y[rows, 384:]], axis=0).astype(BF16)
            return carry

        lax.fori_loop(0, QUADS, planes, 0, unroll=6)
        results.append(pltpu.make_async_copy(out, far_out.at[:, which], left.at[which]))
        results[-1].start()
    for copy in results:
        copy.wait()


def cost(pairs):
    return pl.CostEstimate(flops=pairs * 1400 * 10**6, bytes_accessed=pairs * 7 * 10**6, transcendentals=0)


def forward(column, target, sources):
    cuts = [cut for source in sources for cut in source]
    pairs = len(sources)
    return pl.pallas_call(
        forward_body,
        in_specs=[SCALAR] + [FAR] * (1 + len(cuts)) + [VECTOR] * 2,
        out_specs=FAR,
        out_shape=jax.ShapeDtypeStruct((PARTS, pairs, *PIECE), BF16),
        scratch_shapes=[pltpu.VMEM((ROWS * PITCH, 128), F32)] * 3
        + [pltpu.SemaphoreType.DMA((1 + len(cuts),)), pltpu.SemaphoreType.DMA((pairs,)), pltpu.VMEM(target.shape, BF16)]
        + [pltpu.VMEM(cut.shape, BF16) for cut in cuts]
        + [pltpu.VMEM((PARTS, *PIECE), BF16)] * pairs,
        compiler_params=pltpu.CompilerParams(vmem_limit_bytes=32 * 2**20),
        cost_estimate=cost(pairs),
        name="forward_zy",
    )(column, target, *cuts, jnp.asarray(Z_TABLES, BF16), jnp.asarray(Y_TABLE, BF16))


def middle_body(far_pieces, far_kernel, x_table, x_back, far_out, head0, head1, tail, arrived, left, kernel, *pieces):
    lots = (head0, head1, tail)
    copies = started([(far_pieces.at[:, 0], pieces[0]), (far_kernel, kernel)], arrived)
    copies += [
        pltpu.make_async_copy(far_pieces.at[:, i], piece, arrived.at[1 + i]) for i, piece in enumerate(pieces) if i
    ]
    for copy in copies[2:]:
        copy.start()
    block = QUADS * 2 * ROWS
    low = lax.broadcasted_iota(jnp.int32, (DUOS, 128), 1) < 64

    def step(i, carry):
        here = pl.ds(i, DUOS, stride=ROWS)
        there = pl.ds(i + ROWS // 2, DUOS, stride=ROWS)
        tail_a, tail_b = tail[here, :], tail[there, :]
        tail_first = jnp.where(low, tail_a, pltpu.roll(tail_b, 64, 1))
        tail_second = jnp.where(low, pltpu.roll(tail_a, 64, 1), tail_b)
        columns = jnp.concatenate(
            [
                jnp.concatenate([head0[here, :], head0[there, :], tail_first], axis=1),
                jnp.concatenate([head1[here, :], head1[there, :], tail_second], axis=1),
            ],
            axis=0,
        ).astype(BF16)
        spectrum = (kernel[i] * dot(x_table[...], columns)).astype(BF16)
        back = dot(x_back[...], spectrum)
        head0[here, :] = back[:DUOS, :128]
        head1[here, :] = back[DUOS:, :128]
        head0[there, :] = back[:DUOS, 128:256]
        head1[there, :] = back[DUOS:, 128:256]
        first, second = back[:DUOS, 256:], back[DUOS:, 256:]
        tail[here, :] = jnp.where(low, first, pltpu.roll(second, 64, 1))
        tail[there, :] = jnp.where(low, pltpu.roll(first, 64, 1), second)
        return carry

    results = []
    for which, piece in enumerate(pieces):
        copies[which and 1 + which].wait()
        for part in range(PARTS):
            for tile, lot in enumerate(lots):
                lot[part * block : (part + 1) * block] = (
                    piece[part, :, :, tile * 128 : (tile + 1) * 128].astype(F32).reshape(block, 128)
                )
        if which == 0:
            copies[1].wait()
        lax.fori_loop(0, ROWS // 2, step, 0, unroll=6)
        for part in range(PARTS):
            for tile, lot in enumerate(lots):
                piece[part, :, :, tile * 128 : (tile + 1) * 128] = (
                    lot[part * block : (part + 1) * block].astype(BF16).reshape(QUADS, 2 * ROWS, 128)
                )
        results.append(pltpu.make_async_copy(piece, far_out.at[:, which], left.at[which]))
        results[-1].start()
    for copy in results:
        copy.wait()


def middle(pieces, kernel):
    pairs = pieces.shape[1]
    return pl.pallas_call(
        middle_body,
        in_specs=[FAR, FAR, VECTOR, VECTOR],
        out_specs=FAR,
        out_shape=jax.ShapeDtypeStruct(pieces.shape, BF16),
        scratch_shapes=[pltpu.VMEM((DUOS * ROWS, 128), F32)] * 3
        + [pltpu.SemaphoreType.DMA((1 + pairs,)), pltpu.SemaphoreType.DMA((pairs,)), pltpu.VMEM(kernel.shape, F32)]
        + [pltpu.VMEM((PARTS, *PIECE), BF16)] * pairs,
        compiler_params=pltpu.CompilerParams(vmem_limit_bytes=32 * 2**20),
        cost_estimate=cost(pairs),
        name="middle_x",
    )(pieces, kernel, jnp.asarray(X_TABLE, BF16), jnp.asarray(X_BACK, BF16))


def backward_body(column, far_pieces, *refs):
    pairs = far_pieces.shape[1]
    far_sources, refs = refs[: 4 * pairs], refs[4 * pairs :]
    far_total = refs[0] if len(refs) == 11 + 4 * pairs else None
    y_table, z_tables, far_out, *refs = refs[far_total is not None :]
    lots, (pieces, out, arrived, left), sources = refs[:3], refs[3:7], refs[7:]
    total = None if far_total is None else out
    copies = started([(far_pieces, pieces), *zip(far_sources, sources)], arrived)
    if total is not None:
        copies.append(pltpu.make_async_copy(far_total, out, arrived.at[1 + 4 * pairs]))
        copies[-1].start()
    copies[0].wait()
    results = []

    for which in range(pairs):

        def planes(quad, carry, which=which):
            parts = [pieces[part, which, quad].astype(F32) for part in range(PARTS)]
            stacks = [
                jnp.concatenate([part[pair * ROWS : (pair + 1) * ROWS] for part in parts], axis=0) for pair in range(2)
            ]
            both = dot(y_table[...], jnp.concatenate(stacks, axis=1).astype(BF16)).astype(BF16)
            for pair in range(2):
                fields = both[:, pair * 384 : (pair + 1) * 384]
                for plane in range(2):
                    lanes = fields[:, 128:] if plane else jnp.concatenate([fields[:, :128], fields[:, 256:]], axis=1)
                    even = dot(lanes[:DUOS], z_tables[2 * plane])
                    odd = dot(lanes[DUOS:], z_tables[2 * plane + 1])
                    rows = pl.ds(pl.multiple_of((quad * 4 + pair * 2 + plane) * PITCH, 8), DUOS)
                    lots[0][rows, :] = even[:, :128]
                    lots[1][rows, :] = even[:, 128:] + odd[:, :128]
                    lots[2][rows, :] = odd[:, 128:]
            return carry

        lax.fori_loop(0, QUADS, planes, 0, unroll=3)
        base = total if which == 0 else out

        for slot in range(4):
            source = sources[which * 4 + slot]
            copies[1 + which * 4 + slot].wait()
            if which == 0 and slot == 0 and total is not None:
                copies[-1].wait()

            def gather(part, carry, source=source, slot=slot, base=base):
                duo = (column[0] ^ slot) * PER_CUT + part
                potential = tiles(lots, pl.ds(duo, ROWS, stride=PITCH))
                here = pl.ds(pl.multiple_of(duo * 384, 128), 384)
                right = source[:, pl.ds(pl.multiple_of(part * 384, 128), 384)].astype(F32)
                term = potential * right
                out[:, here] = -term if base is None else base[:, here] - term
                return carry

            lax.fori_loop(0, PER_CUT, gather, 0, unroll=12)
            if which == pairs - 1:
                here = pl.ds(pl.multiple_of((column[0] ^ slot) * (CELLS // 4), 128), CELLS // 4)
                results.append(pltpu.make_async_copy(out.at[:, here], far_out.at[:, here], left.at[slot]))
                results[-1].start()
    for copy in results:
        copy.wait()


def backward(column, pieces, sources, total):
    cuts = [cut for source in sources for cut in source]
    return pl.pallas_call(
        backward_body,
        in_specs=[SCALAR] + [FAR] * (1 + len(cuts) + (total is not None)) + [VECTOR] * 2,
        out_specs=FAR,
        out_shape=jax.ShapeDtypeStruct((ROWS, CELLS), F32),
        scratch_shapes=[pltpu.VMEM((ROWS * PITCH, 128), F32)] * 3
        + [pltpu.VMEM(pieces.shape, BF16), pltpu.VMEM((ROWS, CELLS), F32)]
        + [pltpu.SemaphoreType.DMA((2 + len(cuts),)), pltpu.SemaphoreType.DMA((4,))]
        + [pltpu.VMEM(cut.shape, BF16) for cut in cuts],
        compiler_params=pltpu.CompilerParams(vmem_limit_bytes=32 * 2**20),
        cost_estimate=cost(len(sources)),
        name="backward_yz",
    )(column, pieces, *cuts, *([] if total is None else [total]), jnp.asarray(Y_BACK, BF16), jnp.asarray(Z_BACKS, BF16))


def exchange(pieces):
    return lax.all_to_all(pieces, "grid", 0, 0, tiled=True)


def band_of(z_hi, x, core):
    return z_hi % 4 * 8 + x * 2 + core


def move(array, pairs):
    return lax.ppermute(array, "band", pairs)


def after(array, *others):
    return lax.optimization_barrier((array, *others))[0]


def scatter(orbital):
    cut = CELLS // 4
    return sum(
        move(
            orbital[:, step * cut : (step + 1) * cut],
            [(band_of(2 * root, 0, 0), band_of(2 * root, step, root)) for root in range(2)],
        )
        for step in range(4)
    )


def beside(mine, is_root):
    away = sum(
        move(mine, [(band_of(2 * c, x, c), band_of(2 * c + up, x, c)) for c in range(2) for x in range(4)]) for up in (1, 3)
    )
    return jnp.where(is_root, mine, away)


def beyond(mine):
    half = mine.shape[1] // 2
    parts = [
        move(part, [(band_of(2 * c + up, x, c), band_of(2 * c + 2, x, c)) for c in range(2) for x in range(4)])
        for up, part in ((1, mine[:, :half]), (3, mine[:, half:]))
    ]
    return mine + jnp.concatenate(parts, axis=1)


def gather_x(mine):
    return [mine] + [
        move(mine, [(band_of(z, x, c), band_of(z, x ^ step, c)) for z in range(4) for x in range(4) for c in range(2)])
        for step in range(1, 4)
    ]


def other_core(source):
    pairs = [(band_of(z, x, c), band_of(z, x, 1 - c)) for z in range(4) for x in range(4) for c in range(2)]
    return [move(cut, pairs) for cut in source]


def local(orbitals):
    band = lax.axis_index("band")
    z_hi, x, core = band // 8, (band // 2) % 4, band % 2
    column = x[None].astype(jnp.int32)
    kernel = coulomb(lax.axis_index("grid"))
    target = orbitals[0]
    is_root = z_hi == 2 * core

    cut_0 = scatter(orbitals[0])
    cut_1 = scatter(after(orbitals[1], cut_0))
    full_0 = beyond(beside(cut_0, is_root))
    mine_0 = gather_x(full_0)
    full_1 = beyond(beside(after(cut_1, full_0), is_root))
    batch_0 = [mine_0, other_core(mine_0)]
    pieces_0 = forward(column, after(target, full_1), batch_0)
    mine_1 = gather_x(after(full_1, *mine_0))
    batch_1 = [mine_1, other_core(mine_1)]
    pieces_1 = forward(column, target, batch_1)
    back_0 = exchange(middle(exchange(pieces_0), kernel))
    back_1 = exchange(middle(exchange(pieces_1), kernel))
    total = backward(column, back_0, batch_0, None)
    return backward(column, back_1, batch_1, total)[None]


def solution(mesh):
    return jax.shard_map(
        local,
        mesh=mesh,
        in_specs=(P("band", "grid", None),),
        out_specs=P("band", "grid", None),
        check_vma=False,
    )
```

```python
import jax
import jax.numpy as jnp
import numpy as np
from jax import lax
from jax.experimental import pallas as pl
from jax.experimental.pallas import tpu as pltpu
from jax.sharding import PartitionSpec as P

SIDE = 192
PARTS = 8
ROWS = SIDE // PARTS
QUADS = ROWS // 4
DUOS = SIDE // 2
CELLS = SIDE * SIDE
COUL = 160.0
PITCH = 104
PER_CUT = DUOS // 4
PIECE = (QUADS, 2 * ROWS, 384)
VECTOR = pl.BlockSpec(memory_space=pltpu.VMEM)
FAR = pl.BlockSpec(memory_space=pltpu.HBM)
SCALAR = pl.BlockSpec(memory_space=pltpu.SMEM)
F32 = jnp.float32
BF16 = jnp.bfloat16


def cas_matrix():
    index = np.arange(SIDE, dtype=np.int32)
    phases = (index[:, None] * index[None, :] % SIDE).astype(np.float32) * np.float32(2.0 * np.pi / SIDE)
    return np.cos(phases) + np.sin(phases)


CAS = cas_matrix()
BY_PARITY = np.concatenate([np.arange(0, SIDE, 2), np.arange(1, SIDE, 2)])
Y_TABLE = CAS[:, BY_PARITY]
Y_BACK = CAS[BY_PARITY, :]
X_TABLE = CAS[:, BY_PARITY]
X_BACK = CAS[BY_PARITY, :]


def z_tables():
    gap = np.zeros((64, 256), np.float32)
    space = np.zeros((SIDE, 64), np.float32)
    first = np.concatenate([CAS, space], axis=1)
    second = np.concatenate([CAS[:, :128], space, CAS[:, 128:]], axis=1)
    return np.stack([np.concatenate(part, axis=0) for table in (first, second) for part in ((table, gap), (gap, table))])


Z_TABLES = z_tables()
Z_BACKS = np.swapaxes(Z_TABLES, 1, 2)


def wave(index):
    return jnp.where(index < SIDE // 2, index, index - SIDE).astype(F32)


def coulomb(me):
    shape = (ROWS // 2, SIDE, 384)
    pair = lax.broadcasted_iota(jnp.int32, shape, 0)
    row = lax.broadcasted_iota(jnp.int32, shape, 1)
    col = lax.broadcasted_iota(jnp.int32, shape, 2)
    late = jnp.where(col < 256, col >= 128, col >= 320)
    kz = jnp.where(col < 256, col % 128, 128 + col % 64)
    ky = me * ROWS + pair + jnp.where(late, ROWS // 2, 0)
    mx, my, mz = wave(row), wave(ky), wave(kz)
    norm_sq = mx * mx + my * my + mz * mz
    bounded = jnp.maximum(norm_sq, 1.0)
    return jnp.where(norm_sq > 0.5, COUL / bounded, 0.0) / float(SIDE) ** 3


def dot(left, right):
    return jnp.dot(left, right, preferred_element_type=F32)


def tiles(lots, rows):
    return jnp.concatenate([lot[rows, :] for lot in lots], axis=1)


def started(pairs, semaphores):
    copies = [pltpu.make_async_copy(a, b, semaphores.at[i]) for i, (a, b) in enumerate(pairs)]
    for copy in copies:
        copy.start()
    return copies


def forward_body(column, far_target, *refs):
    pairs = (len(refs) - 9) // 9
    far_sources, (z_tables, y_table, far_out), refs = refs[: 4 * pairs], refs[4 * pairs : 4 * pairs + 3], refs[4 * pairs + 3 :]
    lots, (arrived, left, target), sources, outs = refs[:3], refs[3:6], refs[6 : 6 + 4 * pairs], refs[6 + 4 * pairs :]
    copies = started([(far_target, target), *zip(far_sources, sources)], arrived)
    copies[0].wait()
    results = []
    for which in range(pairs):
        out = outs[which]
        for slot in range(4):
            source = sources[which * 4 + slot]
            copies[1 + which * 4 + slot].wait()

            def form(part, carry, source=source, slot=slot):
                duo = (column[0] ^ slot) * PER_CUT + part
                left = target[:, pl.ds(pl.multiple_of(duo * 384, 128), 384)].astype(F32)
                right = source[:, pl.ds(pl.multiple_of(part * 384, 128), 384)].astype(F32)
                density = left * right
                for tile, lot in enumerate(lots):
                    lot[pl.ds(duo, ROWS, stride=PITCH), :] = density[:, tile * 128 : (tile + 1) * 128]
                return carry

            lax.fori_loop(0, PER_CUT, form, 0, unroll=12)

        def planes(quad, carry, out=out):
            along_z = []
            for pair in range(2):
                halves = []
                for plane in range(2):
                    rows = pl.ds(pl.multiple_of((quad * 4 + pair * 2 + plane) * PITCH, 8), DUOS)
                    density = tiles(lots, rows).astype(BF16)
                    even = dot(density[:, :256], z_tables[2 * plane])
                    odd = dot(density[:, 128:], z_tables[2 * plane + 1])
                    halves.append(jnp.concatenate([even, odd], axis=0))
                low, high = halves
                along_z += [low[:, :128], high[:, :128], low[:, 128:] + high[:, 128:]]
            along_y = dot(y_table[...], jnp.concatenate(along_z, axis=1).astype(BF16))
            for part in range(PARTS):
                rows = slice(part * ROWS, (part + 1) * ROWS)
                out[part, quad] = jnp.concatenate([along_y[rows, :384], along_y[rows, 384:]], axis=0).astype(BF16)
            return carry

        lax.fori_loop(0, QUADS, planes, 0, unroll=6)
        results.append(pltpu.make_async_copy(out, far_out.at[:, which], left.at[which]))
        results[-1].start()
    for copy in results:
        copy.wait()


def cost(pairs):
    return pl.CostEstimate(flops=pairs * 1400 * 10**6, bytes_accessed=pairs * 7 * 10**6, transcendentals=0)


def forward(column, target, sources):
    cuts = [cut for source in sources for cut in source]
    pairs = len(sources)
    return pl.pallas_call(
        forward_body,
        in_specs=[SCALAR] + [FAR] * (1 + len(cuts)) + [VECTOR] * 2,
        out_specs=FAR,
        out_shape=jax.ShapeDtypeStruct((PARTS, pairs, *PIECE), BF16),
        scratch_shapes=[pltpu.VMEM((ROWS * PITCH, 128), F32)] * 3
        + [pltpu.SemaphoreType.DMA((1 + len(cuts),)), pltpu.SemaphoreType.DMA((pairs,)), pltpu.VMEM(target.shape, BF16)]
        + [pltpu.VMEM(cut.shape, BF16) for cut in cuts]
        + [pltpu.VMEM((PARTS, *PIECE), BF16)] * pairs,
        compiler_params=pltpu.CompilerParams(vmem_limit_bytes=62 * 2**20),
        cost_estimate=cost(pairs),
        name="forward_zy",
    )(column, target, *cuts, jnp.asarray(Z_TABLES, BF16), jnp.asarray(Y_TABLE, BF16))


def middle_body(far_pieces, far_kernel, x_table, x_back, far_out, head0, head1, tail, arrived, left, kernel, *pieces):
    lots = (head0, head1, tail)
    copies = started([(far_pieces.at[:, 0], pieces[0]), (far_kernel, kernel)], arrived)
    copies += [
        pltpu.make_async_copy(far_pieces.at[:, i], piece, arrived.at[1 + i]) for i, piece in enumerate(pieces) if i
    ]
    for copy in copies[2:]:
        copy.start()
    block = QUADS * 2 * ROWS
    low = lax.broadcasted_iota(jnp.int32, (DUOS, 128), 1) < 64

    def step(i, carry):
        here = pl.ds(i, DUOS, stride=ROWS)
        there = pl.ds(i + ROWS // 2, DUOS, stride=ROWS)
        tail_a, tail_b = tail[here, :], tail[there, :]
        tail_first = jnp.where(low, tail_a, pltpu.roll(tail_b, 64, 1))
        tail_second = jnp.where(low, pltpu.roll(tail_a, 64, 1), tail_b)
        columns = jnp.concatenate(
            [
                jnp.concatenate([head0[here, :], head0[there, :], tail_first], axis=1),
                jnp.concatenate([head1[here, :], head1[there, :], tail_second], axis=1),
            ],
            axis=0,
        ).astype(BF16)
        spectrum = (kernel[i] * dot(x_table[...], columns)).astype(BF16)
        back = dot(x_back[...], spectrum)
        head0[here, :] = back[:DUOS, :128]
        head1[here, :] = back[DUOS:, :128]
        head0[there, :] = back[:DUOS, 128:256]
        head1[there, :] = back[DUOS:, 128:256]
        first, second = back[:DUOS, 256:], back[DUOS:, 256:]
        tail[here, :] = jnp.where(low, first, pltpu.roll(second, 64, 1))
        tail[there, :] = jnp.where(low, pltpu.roll(first, 64, 1), second)
        return carry

    results = []
    for which, piece in enumerate(pieces):
        copies[which and 1 + which].wait()
        for part in range(PARTS):
            for tile, lot in enumerate(lots):
                lot[part * block : (part + 1) * block] = (
                    piece[part, :, :, tile * 128 : (tile + 1) * 128].astype(F32).reshape(block, 128)
                )
        if which == 0:
            copies[1].wait()
        lax.fori_loop(0, ROWS // 2, step, 0, unroll=6)
        for part in range(PARTS):
            for tile, lot in enumerate(lots):
                piece[part, :, :, tile * 128 : (tile + 1) * 128] = (
                    lot[part * block : (part + 1) * block].astype(BF16).reshape(QUADS, 2 * ROWS, 128)
                )
        results.append(pltpu.make_async_copy(piece, far_out.at[:, which], left.at[which]))
        results[-1].start()
    for copy in results:
        copy.wait()


def middle(pieces, kernel):
    pairs = pieces.shape[1]
    return pl.pallas_call(
        middle_body,
        in_specs=[FAR, FAR, VECTOR, VECTOR],
        out_specs=FAR,
        out_shape=jax.ShapeDtypeStruct(pieces.shape, BF16),
        scratch_shapes=[pltpu.VMEM((DUOS * ROWS, 128), F32)] * 3
        + [pltpu.SemaphoreType.DMA((1 + pairs,)), pltpu.SemaphoreType.DMA((pairs,)), pltpu.VMEM(kernel.shape, F32)]
        + [pltpu.VMEM((PARTS, *PIECE), BF16)] * pairs,
        compiler_params=pltpu.CompilerParams(vmem_limit_bytes=62 * 2**20),
        cost_estimate=cost(pairs),
        name="middle_x",
    )(pieces, kernel, jnp.asarray(X_TABLE, BF16), jnp.asarray(X_BACK, BF16))


def backward_body(column, far_pieces, *refs):
    pairs = far_pieces.shape[1]
    far_sources, refs = refs[: 4 * pairs], refs[4 * pairs :]
    far_total = refs[0] if len(refs) == 11 + 4 * pairs else None
    y_table, z_tables, far_out, *refs = refs[far_total is not None :]
    lots, (pieces, out, arrived, left), sources = refs[:3], refs[3:7], refs[7:]
    total = None if far_total is None else out
    copies = started([(far_pieces, pieces), *zip(far_sources, sources)], arrived)
    if total is not None:
        copies.append(pltpu.make_async_copy(far_total, out, arrived.at[1 + 4 * pairs]))
        copies[-1].start()
    copies[0].wait()
    results = []

    for which in range(pairs):

        def planes(quad, carry, which=which):
            parts = [pieces[part, which, quad].astype(F32) for part in range(PARTS)]
            stacks = [
                jnp.concatenate([part[pair * ROWS : (pair + 1) * ROWS] for part in parts], axis=0) for pair in range(2)
            ]
            both = dot(y_table[...], jnp.concatenate(stacks, axis=1).astype(BF16)).astype(BF16)
            for pair in range(2):
                fields = both[:, pair * 384 : (pair + 1) * 384]
                for plane in range(2):
                    lanes = fields[:, 128:] if plane else jnp.concatenate([fields[:, :128], fields[:, 256:]], axis=1)
                    even = dot(lanes[:DUOS], z_tables[2 * plane])
                    odd = dot(lanes[DUOS:], z_tables[2 * plane + 1])
                    rows = pl.ds(pl.multiple_of((quad * 4 + pair * 2 + plane) * PITCH, 8), DUOS)
                    lots[0][rows, :] = even[:, :128]
                    lots[1][rows, :] = even[:, 128:] + odd[:, :128]
                    lots[2][rows, :] = odd[:, 128:]
            return carry

        lax.fori_loop(0, QUADS, planes, 0, unroll=3)
        base = total if which == 0 else out

        for slot in range(4):
            source = sources[which * 4 + slot]
            copies[1 + which * 4 + slot].wait()
            if which == 0 and slot == 0 and total is not None:
                copies[-1].wait()

            def gather(part, carry, source=source, slot=slot, base=base):
                duo = (column[0] ^ slot) * PER_CUT + part
                potential = tiles(lots, pl.ds(duo, ROWS, stride=PITCH))
                here = pl.ds(pl.multiple_of(duo * 384, 128), 384)
                right = source[:, pl.ds(pl.multiple_of(part * 384, 128), 384)].astype(F32)
                term = potential * right
                out[:, here] = -term if base is None else base[:, here] - term
                return carry

            lax.fori_loop(0, PER_CUT, gather, 0, unroll=12)
            if which == pairs - 1:
                here = pl.ds(pl.multiple_of((column[0] ^ slot) * (CELLS // 4), 128), CELLS // 4)
                results.append(pltpu.make_async_copy(out.at[:, here], far_out.at[:, here], left.at[slot]))
                results[-1].start()
    for copy in results:
        copy.wait()


def backward(column, pieces, sources, total):
    cuts = [cut for source in sources for cut in source]
    return pl.pallas_call(
        backward_body,
        in_specs=[SCALAR] + [FAR] * (1 + len(cuts) + (total is not None)) + [VECTOR] * 2,
        out_specs=FAR,
        out_shape=jax.ShapeDtypeStruct((ROWS, CELLS), F32),
        scratch_shapes=[pltpu.VMEM((ROWS * PITCH, 128), F32)] * 3
        + [pltpu.VMEM(pieces.shape, BF16), pltpu.VMEM((ROWS, CELLS), F32)]
        + [pltpu.SemaphoreType.DMA((2 + len(cuts),)), pltpu.SemaphoreType.DMA((4,))]
        + [pltpu.VMEM(cut.shape, BF16) for cut in cuts],
        compiler_params=pltpu.CompilerParams(vmem_limit_bytes=62 * 2**20),
        cost_estimate=cost(len(sources)),
        name="backward_yz",
    )(column, pieces, *cuts, *([] if total is None else [total]), jnp.asarray(Y_BACK, BF16), jnp.asarray(Z_BACKS, BF16))


def exchange(pieces):
    return lax.all_to_all(pieces, "grid", 0, 0, tiled=True)


def band_of(z_hi, x, core):
    return z_hi % 4 * 8 + x * 2 + core


def move(array, pairs):
    return lax.ppermute(array, "band", pairs)


def after(array, *others):
    return lax.optimization_barrier((array, *others))[0]


def scatter(orbital):
    cut = CELLS // 4
    return sum(
        move(
            orbital[:, step * cut : (step + 1) * cut],
            [(band_of(2 * root, 0, 0), band_of(2 * root, step, root)) for root in range(2)],
        )
        for step in range(4)
    )


def beside(mine, is_root):
    away = sum(
        move(mine, [(band_of(2 * c, x, c), band_of(2 * c + up, x, c)) for c in range(2) for x in range(4)]) for up in (1, 3)
    )
    return jnp.where(is_root, mine, away)


def beyond(mine):
    half = mine.shape[1] // 2
    parts = [
        move(part, [(band_of(2 * c + up, x, c), band_of(2 * c + 2, x, c)) for c in range(2) for x in range(4)])
        for up, part in ((1, mine[:, :half]), (3, mine[:, half:]))
    ]
    return mine + jnp.concatenate(parts, axis=1)


def gather_x(mine):
    return [mine] + [
        move(mine, [(band_of(z, x, c), band_of(z, x ^ step, c)) for z in range(4) for x in range(4) for c in range(2)])
        for step in range(1, 4)
    ]


def other_core(source):
    pairs = [(band_of(z, x, c), band_of(z, x, 1 - c)) for z in range(4) for x in range(4) for c in range(2)]
    return [move(cut, pairs) for cut in source]


def local(orbitals):
    band = lax.axis_index("band")
    z_hi, x, core = band // 8, (band // 2) % 4, band % 2
    column = x[None].astype(jnp.int32)
    kernel = coulomb(lax.axis_index("grid"))
    target = orbitals[0]
    is_root = z_hi == 2 * core

    cut_0 = scatter(orbitals[0])
    cut_1 = scatter(after(orbitals[1], cut_0))
    full_0 = beyond(beside(cut_0, is_root))
    mine_0 = gather_x(full_0)
    full_1 = beyond(beside(after(cut_1, full_0), is_root))
    batch_0 = [mine_0, other_core(mine_0)]
    pieces_0 = forward(column, after(target, full_1), batch_0)
    mine_1 = gather_x(after(full_1, *mine_0))
    batch_1 = [mine_1, other_core(mine_1)]
    pieces_1 = forward(column, target, batch_1)
    back_0 = exchange(middle(exchange(pieces_0), kernel))
    back_1 = exchange(middle(exchange(pieces_1), kernel))
    total = backward(column, back_0, batch_0, None)
    return backward(column, back_1, batch_1, total)[None]


def solution(mesh):
    return jax.shard_map(
        local,
        mesh=mesh,
        in_specs=(P("band", "grid", None),),
        out_specs=P("band", "grid", None),
        check_vma=False,
    )
```

```python
import jax
import jax.numpy as jnp
import numpy as np
from jax import lax
from jax.experimental import pallas as pl
from jax.experimental.pallas import tpu as pltpu
from jax.sharding import PartitionSpec as P

SIDE = 192
PARTS = 8
ROWS = SIDE // PARTS
QUADS = ROWS // 4
DUOS = SIDE // 2
CELLS = SIDE * SIDE
COUL = 160.0
PITCH = 104
PER_CUT = DUOS // 4
PIECE = (QUADS, 2 * ROWS, 384)
VECTOR = pl.BlockSpec(memory_space=pltpu.VMEM)
FAR = pl.BlockSpec(memory_space=pltpu.HBM)
SCALAR = pl.BlockSpec(memory_space=pltpu.SMEM)
F32 = jnp.float32
BF16 = jnp.bfloat16


def cas_matrix():
    index = np.arange(SIDE, dtype=np.int32)
    phases = (index[:, None] * index[None, :] % SIDE).astype(np.float32) * np.float32(2.0 * np.pi / SIDE)
    return np.cos(phases) + np.sin(phases)


CAS = cas_matrix()
BY_PARITY = np.concatenate([np.arange(0, SIDE, 2), np.arange(1, SIDE, 2)])
Y_TABLE = CAS[:, BY_PARITY]
Y_BACK = CAS[BY_PARITY, :]
X_TABLE = CAS[:, BY_PARITY]
X_BACK = CAS[BY_PARITY, :]


def z_tables():
    gap = np.zeros((64, 256), np.float32)
    space = np.zeros((SIDE, 64), np.float32)
    first = np.concatenate([CAS, space], axis=1)
    second = np.concatenate([CAS[:, :128], space, CAS[:, 128:]], axis=1)
    return np.stack([np.concatenate(part, axis=0) for table in (first, second) for part in ((table, gap), (gap, table))])


Z_TABLES = z_tables()
Z_BACKS = np.swapaxes(Z_TABLES, 1, 2)


def wave(index):
    return jnp.where(index < SIDE // 2, index, index - SIDE).astype(F32)


def coulomb(me):
    shape = (ROWS // 2, SIDE, 384)
    pair = lax.broadcasted_iota(jnp.int32, shape, 0)
    row = lax.broadcasted_iota(jnp.int32, shape, 1)
    col = lax.broadcasted_iota(jnp.int32, shape, 2)
    late = jnp.where(col < 256, col >= 128, col >= 320)
    kz = jnp.where(col < 256, col % 128, 128 + col % 64)
    ky = me * ROWS + pair + jnp.where(late, ROWS // 2, 0)
    mx, my, mz = wave(row), wave(ky), wave(kz)
    norm_sq = mx * mx + my * my + mz * mz
    bounded = jnp.maximum(norm_sq, 1.0)
    return jnp.where(norm_sq > 0.5, COUL / bounded, 0.0) / float(SIDE) ** 3


def dot(left, right):
    return jnp.dot(left, right, preferred_element_type=F32)


def tiles(lots, rows):
    return jnp.concatenate([lot[rows, :] for lot in lots], axis=1)


def started(pairs, semaphores):
    copies = [pltpu.make_async_copy(a, b, semaphores.at[i]) for i, (a, b) in enumerate(pairs)]
    for copy in copies:
        copy.start()
    return copies


def forward_body(column, far_target, *refs):
    pairs = (len(refs) - 9) // 9
    far_sources, (z_tables, y_table, far_out), refs = refs[: 4 * pairs], refs[4 * pairs : 4 * pairs + 3], refs[4 * pairs + 3 :]
    lots, (arrived, left, target), sources, outs = refs[:3], refs[3:6], refs[6 : 6 + 4 * pairs], refs[6 + 4 * pairs :]
    copies = started([(far_target, target), *zip(far_sources, sources)], arrived)
    copies[0].wait()
    results = []
    for which in range(pairs):
        out = outs[which]
        for slot in range(4):
            source = sources[which * 4 + slot]
            copies[1 + which * 4 + slot].wait()

            def form(part, carry, source=source, slot=slot):
                duo = (column[0] ^ slot) * PER_CUT + part
                left = target[:, pl.ds(pl.multiple_of(duo * 384, 128), 384)].astype(F32)
                right = source[:, pl.ds(pl.multiple_of(part * 384, 128), 384)].astype(F32)
                density = left * right
                for tile, lot in enumerate(lots):
                    lot[pl.ds(duo, ROWS, stride=PITCH), :] = density[:, tile * 128 : (tile + 1) * 128]
                return carry

            lax.fori_loop(0, PER_CUT, form, 0, unroll=12)

        def planes(quad, carry, out=out):
            along_z = []
            for pair in range(2):
                halves = []
                for plane in range(2):
                    rows = pl.ds(pl.multiple_of((quad * 4 + pair * 2 + plane) * PITCH, 8), DUOS)
                    density = tiles(lots, rows).astype(BF16)
                    even = dot(density[:, :256], z_tables[2 * plane])
                    odd = dot(density[:, 128:], z_tables[2 * plane + 1])
                    halves.append(jnp.concatenate([even, odd], axis=0))
                low, high = halves
                along_z += [low[:, :128], high[:, :128], low[:, 128:] + high[:, 128:]]
            along_y = dot(y_table[...], jnp.concatenate(along_z, axis=1).astype(BF16))
            for part in range(PARTS):
                rows = slice(part * ROWS, (part + 1) * ROWS)
                out[part, quad] = jnp.concatenate([along_y[rows, :384], along_y[rows, 384:]], axis=0).astype(BF16)
            return carry

        lax.fori_loop(0, QUADS, planes, 0, unroll=6)
        results.append(pltpu.make_async_copy(out, far_out.at[:, which], left.at[which]))
        results[-1].start()
    for copy in results:
        copy.wait()


def cost(pairs):
    return pl.CostEstimate(flops=pairs * 1400 * 10**6, bytes_accessed=pairs * 7 * 10**6, transcendentals=0)


def forward(column, target, sources):
    cuts = [cut for source in sources for cut in source]
    pairs = len(sources)
    return pl.pallas_call(
        forward_body,
        in_specs=[SCALAR] + [FAR] * (1 + len(cuts)) + [VECTOR] * 2,
        out_specs=FAR,
        out_shape=jax.ShapeDtypeStruct((PARTS, pairs, *PIECE), BF16),
        scratch_shapes=[pltpu.VMEM((ROWS * PITCH, 128), F32)] * 3
        + [pltpu.SemaphoreType.DMA((1 + len(cuts),)), pltpu.SemaphoreType.DMA((pairs,)), pltpu.VMEM(target.shape, BF16)]
        + [pltpu.VMEM(cut.shape, BF16) for cut in cuts]
        + [pltpu.VMEM((PARTS, *PIECE), BF16)] * pairs,
        compiler_params=pltpu.CompilerParams(vmem_limit_bytes=62 * 2**20),
        cost_estimate=cost(pairs),
        name="forward_zy",
    )(column, target, *cuts, jnp.asarray(Z_TABLES, BF16), jnp.asarray(Y_TABLE, BF16))


def middle_body(far_pieces, far_kernel, x_table, x_back, far_out, head0, head1, tail, arrived, left, kernel, *pieces):
    lots = (head0, head1, tail)
    copies = started([(far_pieces.at[:, 0], pieces[0]), (far_kernel, kernel)], arrived)
    copies += [
        pltpu.make_async_copy(far_pieces.at[:, i], piece, arrived.at[1 + i]) for i, piece in enumerate(pieces) if i
    ]
    for copy in copies[2:]:
        copy.start()
    block = QUADS * 2 * ROWS
    low = lax.broadcasted_iota(jnp.int32, (DUOS, 128), 1) < 64

    def step(i, carry):
        here = pl.ds(i, DUOS, stride=ROWS)
        there = pl.ds(i + ROWS // 2, DUOS, stride=ROWS)
        tail_a, tail_b = tail[here, :], tail[there, :]
        tail_first = jnp.where(low, tail_a, pltpu.roll(tail_b, 64, 1))
        tail_second = jnp.where(low, pltpu.roll(tail_a, 64, 1), tail_b)
        columns = jnp.concatenate(
            [
                jnp.concatenate([head0[here, :], head0[there, :], tail_first], axis=1),
                jnp.concatenate([head1[here, :], head1[there, :], tail_second], axis=1),
            ],
            axis=0,
        ).astype(BF16)
        spectrum = (kernel[i] * dot(x_table[...], columns)).astype(BF16)
        back = dot(x_back[...], spectrum)
        head0[here, :] = back[:DUOS, :128]
        head1[here, :] = back[DUOS:, :128]
        head0[there, :] = back[:DUOS, 128:256]
        head1[there, :] = back[DUOS:, 128:256]
        first, second = back[:DUOS, 256:], back[DUOS:, 256:]
        tail[here, :] = jnp.where(low, first, pltpu.roll(second, 64, 1))
        tail[there, :] = jnp.where(low, pltpu.roll(first, 64, 1), second)
        return carry

    results = []
    for which, piece in enumerate(pieces):
        copies[which and 1 + which].wait()
        for part in range(PARTS):
            for tile, lot in enumerate(lots):
                lot[part * block : (part + 1) * block] = (
                    piece[part, :, :, tile * 128 : (tile + 1) * 128].astype(F32).reshape(block, 128)
                )
        if which == 0:
            copies[1].wait()
        lax.fori_loop(0, ROWS // 2, step, 0, unroll=6)
        for part in range(PARTS):
            for tile, lot in enumerate(lots):
                piece[part, :, :, tile * 128 : (tile + 1) * 128] = (
                    lot[part * block : (part + 1) * block].astype(BF16).reshape(QUADS, 2 * ROWS, 128)
                )
        results.append(pltpu.make_async_copy(piece, far_out.at[:, which], left.at[which]))
        results[-1].start()
    for copy in results:
        copy.wait()


def middle(pieces, kernel):
    pairs = pieces.shape[1]
    return pl.pallas_call(
        middle_body,
        in_specs=[FAR, FAR, VECTOR, VECTOR],
        out_specs=FAR,
        out_shape=jax.ShapeDtypeStruct(pieces.shape, BF16),
        scratch_shapes=[pltpu.VMEM((DUOS * ROWS, 128), F32)] * 3
        + [pltpu.SemaphoreType.DMA((1 + pairs,)), pltpu.SemaphoreType.DMA((pairs,)), pltpu.VMEM(kernel.shape, F32)]
        + [pltpu.VMEM((PARTS, *PIECE), BF16)] * pairs,
        compiler_params=pltpu.CompilerParams(vmem_limit_bytes=62 * 2**20),
        cost_estimate=cost(pairs),
        name="middle_x",
    )(pieces, kernel, jnp.asarray(X_TABLE, BF16), jnp.asarray(X_BACK, BF16))


def backward_body(column, far_pieces, *refs):
    pairs = far_pieces.shape[1]
    far_sources, refs = refs[: 4 * pairs], refs[4 * pairs :]
    far_total = refs[0] if len(refs) == 10 + 5 * pairs else None
    y_table, z_tables, far_out, *refs = refs[far_total is not None :]
    lots, (out, arrived, left), pieces, sources = refs[:3], refs[3:6], refs[6 : 6 + pairs], refs[6 + pairs :]
    total = None if far_total is None else out
    brought = [(far_pieces.at[:, i], piece) for i, piece in enumerate(pieces)] + list(zip(far_sources, sources))
    copies = started(brought + ([] if total is None else [(far_total, out)]), arrived)
    results = []

    for which in range(pairs):
        copies[which].wait()

        def planes(quad, carry, which=which):
            parts = [pieces[which][part, quad].astype(F32) for part in range(PARTS)]
            stacks = [
                jnp.concatenate([part[pair * ROWS : (pair + 1) * ROWS] for part in parts], axis=0) for pair in range(2)
            ]
            both = dot(y_table[...], jnp.concatenate(stacks, axis=1).astype(BF16)).astype(BF16)
            for pair in range(2):
                fields = both[:, pair * 384 : (pair + 1) * 384]
                for plane in range(2):
                    lanes = fields[:, 128:] if plane else jnp.concatenate([fields[:, :128], fields[:, 256:]], axis=1)
                    even = dot(lanes[:DUOS], z_tables[2 * plane])
                    odd = dot(lanes[DUOS:], z_tables[2 * plane + 1])
                    rows = pl.ds(pl.multiple_of((quad * 4 + pair * 2 + plane) * PITCH, 8), DUOS)
                    lots[0][rows, :] = even[:, :128]
                    lots[1][rows, :] = even[:, 128:] + odd[:, :128]
                    lots[2][rows, :] = odd[:, 128:]
            return carry

        lax.fori_loop(0, QUADS, planes, 0, unroll=6)
        base = total if which == 0 else out

        for slot in range(4):
            source = sources[which * 4 + slot]
            copies[pairs + which * 4 + slot].wait()
            if which == 0 and slot == 0 and total is not None:
                copies[-1].wait()

            def gather(part, carry, source=source, slot=slot, base=base):
                duo = (column[0] ^ slot) * PER_CUT + part
                potential = tiles(lots, pl.ds(duo, ROWS, stride=PITCH))
                here = pl.ds(pl.multiple_of(duo * 384, 128), 384)
                right = source[:, pl.ds(pl.multiple_of(part * 384, 128), 384)].astype(F32)
                term = potential * right
                out[:, here] = -term if base is None else base[:, here] - term
                return carry

            lax.fori_loop(0, PER_CUT, gather, 0, unroll=12)
            if which == pairs - 1:
                here = pl.ds(pl.multiple_of((column[0] ^ slot) * (CELLS // 4), 128), CELLS // 4)
                results.append(pltpu.make_async_copy(out.at[:, here], far_out.at[:, here], left.at[slot]))
                results[-1].start()
    for copy in results:
        copy.wait()


def backward(column, pieces, sources, total):
    cuts = [cut for source in sources for cut in source]
    return pl.pallas_call(
        backward_body,
        in_specs=[SCALAR] + [FAR] * (1 + len(cuts) + (total is not None)) + [VECTOR] * 2,
        out_specs=FAR,
        out_shape=jax.ShapeDtypeStruct((ROWS, CELLS), F32),
        scratch_shapes=[pltpu.VMEM((ROWS * PITCH, 128), F32)] * 3
        + [pltpu.VMEM((ROWS, CELLS), F32), pltpu.SemaphoreType.DMA((6 * len(sources),)), pltpu.SemaphoreType.DMA((4,))]
        + [pltpu.VMEM((PARTS, *PIECE), BF16)] * len(sources)
        + [pltpu.VMEM(cut.shape, BF16) for cut in cuts],
        compiler_params=pltpu.CompilerParams(vmem_limit_bytes=62 * 2**20),
        cost_estimate=cost(len(sources)),
        name="backward_yz",
    )(column, pieces, *cuts, *([] if total is None else [total]), jnp.asarray(Y_BACK, BF16), jnp.asarray(Z_BACKS, BF16))


def exchange(pieces):
    return lax.all_to_all(pieces, "grid", 0, 0, tiled=True)


def band_of(z_hi, x, core):
    return z_hi % 4 * 8 + x * 2 + core


def move(array, pairs):
    return lax.ppermute(array, "band", pairs)


def after(array, *others):
    return lax.optimization_barrier((array, *others))[0]


def scatter(orbital):
    cut = CELLS // 4
    return sum(
        move(
            orbital[:, step * cut : (step + 1) * cut],
            [(band_of(2 * root, 0, 0), band_of(2 * root, step, root)) for root in range(2)],
        )
        for step in range(4)
    )


def beside(mine, is_root):
    away = sum(
        move(mine, [(band_of(2 * c, x, c), band_of(2 * c + up, x, c)) for c in range(2) for x in range(4)]) for up in (1, 3)
    )
    return jnp.where(is_root, mine, away)


def beyond(mine):
    half = mine.shape[1] // 2
    parts = [
        move(part, [(band_of(2 * c + up, x, c), band_of(2 * c + 2, x, c)) for c in range(2) for x in range(4)])
        for up, part in ((1, mine[:, :half]), (3, mine[:, half:]))
    ]
    return mine + jnp.concatenate(parts, axis=1)


def gather_x(mine):
    return [mine] + [
        move(mine, [(band_of(z, x, c), band_of(z, x ^ step, c)) for z in range(4) for x in range(4) for c in range(2)])
        for step in range(1, 4)
    ]


def other_core(source):
    pairs = [(band_of(z, x, c), band_of(z, x, 1 - c)) for z in range(4) for x in range(4) for c in range(2)]
    return [move(cut, pairs) for cut in source]


def local(orbitals):
    band = lax.axis_index("band")
    z_hi, x, core = band // 8, (band // 2) % 4, band % 2
    column = x[None].astype(jnp.int32)
    kernel = coulomb(lax.axis_index("grid"))
    target = orbitals[0]
    is_root = z_hi == 2 * core

    cut_0 = scatter(orbitals[0])
    cut_1 = scatter(after(orbitals[1], cut_0))
    full_0 = beyond(after(beside(cut_0, is_root), cut_1))
    mine_0 = gather_x(full_0)
    batch_0 = [mine_0, other_core(mine_0)]
    full_1 = beyond(beside(after(cut_1, batch_0[1][0]), is_root))
    pieces_0 = after(forward(column, target, batch_0), full_1)
    mine_1 = gather_x(after(full_1, *mine_0))
    batch_1 = [mine_1, other_core(mine_1)]
    pieces_1 = forward(column, target, batch_1)
    back_0 = exchange(middle(exchange(pieces_0), kernel))
    back_1 = exchange(middle(exchange(pieces_1), kernel))
    total = backward(column, back_0, batch_0, None)
    return backward(column, back_1, batch_1, total)[None]


def solution(mesh):
    return jax.shard_map(
        local,
        mesh=mesh,
        in_specs=(P("band", "grid", None),),
        out_specs=P("band", "grid", None),
        check_vma=False,
    )
```

```python
import functools

import jax
import jax.numpy as jnp
import numpy as np
from jax import lax
from jax.experimental import pallas as pl
from jax.experimental.pallas import tpu as pltpu
from jax.sharding import PartitionSpec as P

SIDE = 192
PARTS = 8
ROWS = SIDE // PARTS
QUADS = ROWS // 4
DUOS = SIDE // 2
CELLS = SIDE * SIDE
COUL = 160.0
PITCH = 104
CUT = CELLS // 4
PER_CUT = DUOS // 4
PIECE = (QUADS, 2 * ROWS, 384)
VECTOR = pl.BlockSpec(memory_space=pltpu.VMEM)
FAR = pl.BlockSpec(memory_space=pltpu.HBM)
SCALAR = pl.BlockSpec(memory_space=pltpu.SMEM)
F32 = jnp.float32
BF16 = jnp.bfloat16


def cas_matrix():
    index = np.arange(SIDE, dtype=np.int32)
    phases = (index[:, None] * index[None, :] % SIDE).astype(np.float32) * np.float32(2.0 * np.pi / SIDE)
    return np.cos(phases) + np.sin(phases)


CAS = cas_matrix()
BY_PARITY = np.concatenate([np.arange(0, SIDE, 2), np.arange(1, SIDE, 2)])
Y_TABLE = CAS[:, BY_PARITY]
Y_BACK = CAS[BY_PARITY, :]
X_TABLE = CAS[:, BY_PARITY]
X_BACK = CAS[BY_PARITY, :]


def z_tables():
    gap = np.zeros((64, 256), np.float32)
    space = np.zeros((SIDE, 64), np.float32)
    first = np.concatenate([CAS, space], axis=1)
    second = np.concatenate([CAS[:, :128], space, CAS[:, 128:]], axis=1)
    return np.stack([np.concatenate(part, axis=0) for table in (first, second) for part in ((table, gap), (gap, table))])


Z_TABLES = z_tables()
Z_BACKS = np.swapaxes(Z_TABLES, 1, 2)


def wave(index):
    return jnp.where(index < SIDE // 2, index, index - SIDE).astype(F32)


def coulomb(me):
    shape = (ROWS // 2, SIDE, 384)
    pair = lax.broadcasted_iota(jnp.int32, shape, 0)
    row = lax.broadcasted_iota(jnp.int32, shape, 1)
    col = lax.broadcasted_iota(jnp.int32, shape, 2)
    late = jnp.where(col < 256, col >= 128, col >= 320)
    kz = jnp.where(col < 256, col % 128, 128 + col % 64)
    ky = me * ROWS + pair + jnp.where(late, ROWS // 2, 0)
    mx, my, mz = wave(row), wave(ky), wave(kz)
    norm_sq = mx * mx + my * my + mz * mz
    bounded = jnp.maximum(norm_sq, 1.0)
    return jnp.where(norm_sq > 0.5, COUL / bounded, 0.0) / float(SIDE) ** 3


def dot(left, right):
    return jnp.dot(left, right, preferred_element_type=F32)


def tiles(lots, rows):
    return jnp.concatenate([lot[rows, :] for lot in lots], axis=1)


def started(pairs, semaphores):
    copies = [pltpu.make_async_copy(a, b, semaphores.at[i]) for i, (a, b) in enumerate(pairs)]
    for copy in copies:
        copy.start()
    return copies


def forward_body(which, column, far_orbitals, *refs):
    far_sources, (z_tables, y_table), far_out, refs = refs[:4], refs[4:6], refs[-15], refs[-14:]
    lots, (arrived, left), targets, sources, out = refs[:3], refs[3:5], refs[5:9], refs[9:13], refs[13]
    brought = []
    for slot in range(4):
        here = pl.ds(pl.multiple_of((column[0] ^ slot) * CUT, 128), CUT)
        brought += [(far_orbitals.at[0, :, here], targets[slot]), (far_sources[slot], sources[slot])]
    copies = started(brought, arrived)
    for slot in range(4):
        target, source = targets[slot], sources[slot]
        copies[2 * slot].wait()
        copies[2 * slot + 1].wait()

        def form(part, carry, target=target, source=source, slot=slot):
            duo = (column[0] ^ slot) * PER_CUT + part
            here = pl.ds(pl.multiple_of(part * 384, 128), 384)
            density = target[:, here].astype(F32) * source[:, here].astype(F32)
            for tile, lot in enumerate(lots):
                lot[pl.ds(duo, ROWS, stride=PITCH), :] = density[:, tile * 128 : (tile + 1) * 128]
            return carry

        lax.fori_loop(0, PER_CUT, form, 0, unroll=12)

    results = []
    for quad in range(QUADS):
        along_z = []
        for pair in range(2):
            halves = []
            for plane in range(2):
                row = (quad * 4 + pair * 2 + plane) * PITCH
                density = tiles(lots, slice(row, row + DUOS)).astype(BF16)
                even = dot(density[:, :256], z_tables[2 * plane])
                odd = dot(density[:, 128:], z_tables[2 * plane + 1])
                halves.append(jnp.concatenate([even, odd], axis=0))
            low, high = halves
            along_z += [low[:, :128], high[:, :128], low[:, 128:] + high[:, 128:]]
        along_y = dot(y_table[...], jnp.concatenate(along_z, axis=1).astype(BF16))
        for part in range(PARTS):
            rows = slice(part * ROWS, (part + 1) * ROWS)
            out[part, quad] = jnp.concatenate([along_y[rows, :384], along_y[rows, 384:]], axis=0).astype(BF16)
        results.append(pltpu.make_async_copy(out.at[:, quad], far_out.at[:, which, quad], left.at[quad]))
        results[-1].start()
    for copy in results:
        copy.wait()


def cost(pairs):
    return pl.CostEstimate(flops=pairs * 1400 * 10**6, bytes_accessed=pairs * 7 * 10**6, transcendentals=0)


def forward(column, orbitals, source, which, pieces):
    return pl.pallas_call(
        functools.partial(forward_body, which),
        in_specs=[SCALAR] + [FAR] * 5 + [VECTOR] * 2 + [FAR] * (pieces is not None),
        out_specs=FAR,
        out_shape=jax.ShapeDtypeStruct((PARTS, 2, *PIECE), BF16),
        input_output_aliases={} if pieces is None else {8: 0},
        scratch_shapes=[pltpu.VMEM((ROWS * PITCH, 128), F32)] * 3
        + [pltpu.SemaphoreType.DMA((8,)), pltpu.SemaphoreType.DMA((QUADS,))]
        + [pltpu.VMEM((ROWS, CUT), BF16)] * 8
        + [pltpu.VMEM((PARTS, *PIECE), BF16)],
        compiler_params=pltpu.CompilerParams(vmem_limit_bytes=62 * 2**20),
        cost_estimate=cost(1),
        name="forward_zy",
    )(
        column,
        orbitals,
        *source,
        jnp.asarray(Z_TABLES, BF16),
        jnp.asarray(Y_TABLE, BF16),
        *([] if pieces is None else [pieces]),
    )


def middle_body(far_pieces, far_kernel, x_table, x_back, far_out, head0, head1, tail, arrived, left, kernel, *pieces):
    lots = (head0, head1, tail)
    copies = started([(far_pieces.at[:, 0], pieces[0]), (far_kernel, kernel)], arrived)
    copies += [
        pltpu.make_async_copy(far_pieces.at[:, i], piece, arrived.at[1 + i]) for i, piece in enumerate(pieces) if i
    ]
    for copy in copies[2:]:
        copy.start()
    block = QUADS * 2 * ROWS
    low = lax.broadcasted_iota(jnp.int32, (DUOS, 128), 1) < 64

    def step(i, carry):
        here = pl.ds(i, DUOS, stride=ROWS)
        there = pl.ds(i + ROWS // 2, DUOS, stride=ROWS)
        tail_a, tail_b = tail[here, :], tail[there, :]
        tail_first = jnp.where(low, tail_a, pltpu.roll(tail_b, 64, 1))
        tail_second = jnp.where(low, pltpu.roll(tail_a, 64, 1), tail_b)
        columns = jnp.concatenate(
            [
                jnp.concatenate([head0[here, :], head0[there, :], tail_first], axis=1),
                jnp.concatenate([head1[here, :], head1[there, :], tail_second], axis=1),
            ],
            axis=0,
        ).astype(BF16)
        spectrum = (kernel[i] * dot(x_table[...], columns)).astype(BF16)
        back = dot(x_back[...], spectrum)
        head0[here, :] = back[:DUOS, :128]
        head1[here, :] = back[DUOS:, :128]
        head0[there, :] = back[:DUOS, 128:256]
        head1[there, :] = back[DUOS:, 128:256]
        first, second = back[:DUOS, 256:], back[DUOS:, 256:]
        tail[here, :] = jnp.where(low, first, pltpu.roll(second, 64, 1))
        tail[there, :] = jnp.where(low, pltpu.roll(first, 64, 1), second)
        return carry

    results = []
    for which, piece in enumerate(pieces):
        copies[which and 1 + which].wait()
        for part in range(PARTS):
            for tile, lot in enumerate(lots):
                lot[part * block : (part + 1) * block] = (
                    piece[part, :, :, tile * 128 : (tile + 1) * 128].astype(F32).reshape(block, 128)
                )
        if which == 0:
            copies[1].wait()
        lax.fori_loop(0, ROWS // 2, step, 0, unroll=6)
        for part in range(PARTS):
            for tile, lot in enumerate(lots):
                piece[part, :, :, tile * 128 : (tile + 1) * 128] = (
                    lot[part * block : (part + 1) * block].astype(BF16).reshape(QUADS, 2 * ROWS, 128)
                )
        results.append(pltpu.make_async_copy(piece, far_out.at[:, which], left.at[which]))
        results[-1].start()
    for copy in results:
        copy.wait()


def middle(pieces, kernel):
    pairs = pieces.shape[1]
    return pl.pallas_call(
        middle_body,
        in_specs=[FAR, FAR, VECTOR, VECTOR],
        out_specs=FAR,
        out_shape=jax.ShapeDtypeStruct(pieces.shape, BF16),
        scratch_shapes=[pltpu.VMEM((DUOS * ROWS, 128), F32)] * 3
        + [pltpu.SemaphoreType.DMA((1 + pairs,)), pltpu.SemaphoreType.DMA((pairs,)), pltpu.VMEM(kernel.shape, F32)]
        + [pltpu.VMEM((PARTS, *PIECE), BF16)] * pairs,
        compiler_params=pltpu.CompilerParams(vmem_limit_bytes=62 * 2**20),
        cost_estimate=cost(pairs),
        name="middle_x",
    )(pieces, kernel, jnp.asarray(X_TABLE, BF16), jnp.asarray(X_BACK, BF16))


def backward_body(column, far_pieces, *refs):
    pairs = far_pieces.shape[1]
    far_sources, refs = refs[: 4 * pairs], refs[4 * pairs :]
    far_total = refs[0] if len(refs) == 7 + 8 * pairs else None
    y_table, z_tables, far_out, *refs = refs[far_total is not None :]
    (out, arrived, left), refs = refs[:3], refs[3:]
    lots = [refs[3 * i : 3 * i + 3] for i in range(pairs)]
    pieces, sources = refs[3 * pairs : 4 * pairs], refs[4 * pairs :]
    brought = [(far_pieces.at[:, i], piece) for i, piece in enumerate(pieces)] + list(zip(far_sources, sources))
    copies = started(brought + ([] if far_total is None else [(far_total, out)]), arrived)

    for which in range(pairs):
        copies[which].wait()

        def planes(quad, carry, which=which):
            parts = [pieces[which][part, quad].astype(F32) for part in range(PARTS)]
            stacks = [
                jnp.concatenate([part[pair * ROWS : (pair + 1) * ROWS] for part in parts], axis=0) for pair in range(2)
            ]
            both = dot(y_table[...], jnp.concatenate(stacks, axis=1).astype(BF16)).astype(BF16)
            for pair in range(2):
                fields = both[:, pair * 384 : (pair + 1) * 384]
                for plane in range(2):
                    lanes = fields[:, 128:] if plane else jnp.concatenate([fields[:, :128], fields[:, 256:]], axis=1)
                    even = dot(lanes[:DUOS], z_tables[2 * plane])
                    odd = dot(lanes[DUOS:], z_tables[2 * plane + 1])
                    rows = pl.ds(pl.multiple_of((quad * 4 + pair * 2 + plane) * PITCH, 8), DUOS)
                    lots[which][0][rows, :] = even[:, :128]
                    lots[which][1][rows, :] = even[:, 128:] + odd[:, :128]
                    lots[which][2][rows, :] = odd[:, 128:]
            return carry

        lax.fori_loop(0, QUADS, planes, 0, unroll=6)

    for copy in copies[pairs:]:
        copy.wait()
    results = []
    for slot in range(4):

        def gather(part, carry, slot=slot):
            duo = (column[0] ^ slot) * PER_CUT + part
            here = pl.ds(pl.multiple_of(duo * 384, 128), 384)
            there = pl.ds(pl.multiple_of(part * 384, 128), 384)
            term = 0.0 if far_total is None else out[:, here]
            for which in range(pairs):
                potential = tiles(lots[which], pl.ds(duo, ROWS, stride=PITCH))
                term = term - potential * sources[which * 4 + slot][:, there].astype(F32)
            out[:, here] = term
            return carry

        lax.fori_loop(0, PER_CUT, gather, 0, unroll=12)
        here = pl.ds(pl.multiple_of((column[0] ^ slot) * CUT, 128), CUT)
        results.append(pltpu.make_async_copy(out.at[:, here], far_out.at[:, here], left.at[slot]))
        results[-1].start()
    for copy in results:
        copy.wait()


def backward(column, pieces, sources, total):
    cuts = [cut for source in sources for cut in source]
    return pl.pallas_call(
        backward_body,
        in_specs=[SCALAR] + [FAR] * (1 + len(cuts) + (total is not None)) + [VECTOR] * 2,
        out_specs=FAR,
        out_shape=jax.ShapeDtypeStruct((ROWS, CELLS), F32),
        scratch_shapes=[pltpu.VMEM((ROWS, CELLS), F32)]
        + [pltpu.SemaphoreType.DMA((6 * len(sources),)), pltpu.SemaphoreType.DMA((4,))]
        + [pltpu.VMEM((ROWS * PITCH, 128), F32)] * (3 * len(sources))
        + [pltpu.VMEM((PARTS, *PIECE), BF16)] * len(sources)
        + [pltpu.VMEM(cut.shape, BF16) for cut in cuts],
        compiler_params=pltpu.CompilerParams(vmem_limit_bytes=62 * 2**20),
        cost_estimate=cost(len(sources)),
        name="backward_yz",
    )(column, pieces, *cuts, *([] if total is None else [total]), jnp.asarray(Y_BACK, BF16), jnp.asarray(Z_BACKS, BF16))


def exchange(pieces):
    return lax.all_to_all(pieces, "grid", 0, 0, tiled=True)


def band_of(z_hi, x, core):
    return z_hi % 4 * 8 + x * 2 + core


def move(array, pairs):
    return lax.ppermute(array, "band", pairs)


def after(array, *others):
    return lax.optimization_barrier((array, *others))[0]


def scatter(orbitals, which):
    return sum(
        move(
            orbitals[which, :, step * CUT : (step + 1) * CUT],
            [(band_of(2 * root, 0, 0), band_of(2 * root, step, root)) for root in range(2)],
        )
        for step in range(4)
    )


def beside(mine, is_root):
    away = sum(
        move(mine, [(band_of(2 * c, x, c), band_of(2 * c + up, x, c)) for c in range(2) for x in range(4)]) for up in (1, 3)
    )
    return jnp.where(is_root, mine, away)


def beyond(mine):
    half = mine.shape[1] // 2
    parts = [
        move(part, [(band_of(2 * c + up, x, c), band_of(2 * c + 2, x, c)) for c in range(2) for x in range(4)])
        for up, part in ((1, mine[:, :half]), (3, mine[:, half:]))
    ]
    return mine + jnp.concatenate(parts, axis=1)


def gather_x(mine):
    return [mine] + [
        move(mine, [(band_of(z, x, c), band_of(z, x ^ step, c)) for z in range(4) for x in range(4) for c in range(2)])
        for step in range(1, 4)
    ]


def other_core(source):
    pairs = [(band_of(z, x, c), band_of(z, x, 1 - c)) for z in range(4) for x in range(4) for c in range(2)]
    return [move(cut, pairs) for cut in source]


def local(orbitals):
    band = lax.axis_index("band")
    z_hi, x, core = band // 8, (band // 2) % 4, band % 2
    column = x[None].astype(jnp.int32)
    kernel = coulomb(lax.axis_index("grid"))
    is_root = z_hi == 2 * core

    cut_0 = scatter(orbitals, 0)
    cut_1 = scatter(after(orbitals, cut_0), 1)
    full_0 = beyond(beside(cut_0, is_root))
    mine_0 = gather_x(full_0)
    full_1 = beyond(beside(after(cut_1, full_0), is_root))
    batch_0 = [mine_0, other_core(mine_0)]
    pieces_0 = forward(column, orbitals, mine_0, 0, None)
    pieces_0 = after(forward(column, orbitals, batch_0[1], 1, pieces_0), full_1)
    mine_1 = gather_x(after(full_1, *mine_0))
    batch_1 = [mine_1, other_core(mine_1)]
    pieces_1 = forward(column, orbitals, mine_1, 0, None)
    pieces_1 = forward(column, orbitals, batch_1[1], 1, pieces_1)
    back_0 = exchange(middle(exchange(pieces_0), kernel))
    back_1 = exchange(middle(exchange(pieces_1), kernel))
    total = backward(column, back_0, batch_0, None)
    return backward(column, back_1, batch_1, total)[None]


def solution(mesh):
    return jax.shard_map(
        local,
        mesh=mesh,
        in_specs=(P("band", "grid", None),),
        out_specs=P("band", "grid", None),
        check_vma=False,
    )
```

```python
import jax
import jax.numpy as jnp
import numpy as np
from jax import lax
from jax.experimental import pallas as pl
from jax.experimental.pallas import tpu as pltpu
from jax.sharding import PartitionSpec as P

SIDE = 192
PARTS = 8
ROWS = SIDE // PARTS
QUADS = ROWS // 4
DUOS = SIDE // 2
CELLS = SIDE * SIDE
COUL = 160.0
PITCH = 104
CUT = CELLS // 4
PER_CUT = DUOS // 4
PIECE = (QUADS, 2 * ROWS, 384)
VECTOR = pl.BlockSpec(memory_space=pltpu.VMEM)
FAR = pl.BlockSpec(memory_space=pltpu.HBM)
SCALAR = pl.BlockSpec(memory_space=pltpu.SMEM)
F32 = jnp.float32
BF16 = jnp.bfloat16


def cas_matrix():
    index = np.arange(SIDE, dtype=np.int32)
    phases = (index[:, None] * index[None, :] % SIDE).astype(np.float32) * np.float32(2.0 * np.pi / SIDE)
    return np.cos(phases) + np.sin(phases)


CAS = cas_matrix()
BY_PARITY = np.concatenate([np.arange(0, SIDE, 2), np.arange(1, SIDE, 2)])
Y_TABLE = CAS[:, BY_PARITY]
Y_BACK = CAS[BY_PARITY, :]
X_TABLE = CAS[:, BY_PARITY]
X_BACK = CAS[BY_PARITY, :]


def z_tables():
    gap = np.zeros((64, 256), np.float32)
    space = np.zeros((SIDE, 64), np.float32)
    first = np.concatenate([CAS, space], axis=1)
    second = np.concatenate([CAS[:, :128], space, CAS[:, 128:]], axis=1)
    return np.stack([np.concatenate(part, axis=0) for table in (first, second) for part in ((table, gap), (gap, table))])


Z_TABLES = z_tables()
Z_BACKS = np.swapaxes(Z_TABLES, 1, 2)


def wave(index):
    return jnp.where(index < SIDE // 2, index, index - SIDE).astype(F32)


def coulomb(me):
    shape = (ROWS // 2, SIDE, 384)
    pair = lax.broadcasted_iota(jnp.int32, shape, 0)
    row = lax.broadcasted_iota(jnp.int32, shape, 1)
    col = lax.broadcasted_iota(jnp.int32, shape, 2)
    late = jnp.where(col < 256, col >= 128, col >= 320)
    kz = jnp.where(col < 256, col % 128, 128 + col % 64)
    ky = me * ROWS + pair + jnp.where(late, ROWS // 2, 0)
    mx, my, mz = wave(row), wave(ky), wave(kz)
    norm_sq = mx * mx + my * my + mz * mz
    bounded = jnp.maximum(norm_sq, 1.0)
    return jnp.where(norm_sq > 0.5, COUL / bounded, 0.0) / float(SIDE) ** 3


def dot(left, right):
    return jnp.dot(left, right, preferred_element_type=F32)


def tiles(lots, rows):
    return jnp.concatenate([lot[rows, :] for lot in lots], axis=1)


def started(pairs, semaphores):
    copies = [pltpu.make_async_copy(a, b, semaphores.at[i]) for i, (a, b) in enumerate(pairs)]
    for copy in copies:
        copy.start()
    return copies


def forward_body(column, far_orbitals, *refs):
    pairs = (len(refs) - 12) // 9
    far_sources, (z_tables, y_table, far_out), refs = refs[: 4 * pairs], refs[4 * pairs : 4 * pairs + 3], refs[4 * pairs + 3 :]
    lots, (arrived, left), targets, refs = refs[:3], refs[3:5], refs[5:9], refs[9:]
    sources, outs = refs[: 4 * pairs], refs[4 * pairs :]
    brought = []
    for slot in range(4):
        here = pl.ds(pl.multiple_of((column[0] ^ slot) * CUT, 128), CUT)
        brought += [(far_orbitals.at[0, :, here], targets[slot]), (far_sources[slot], sources[slot])]
    copies = started(brought + list(zip(far_sources[4:], sources[4:])), arrived)
    results = []
    for which, out in enumerate(outs):
        for slot in range(4):
            target, source = targets[slot], sources[4 * which + slot]
            for copy in copies[2 * slot : 2 * slot + 2] if which == 0 else copies[4 + 4 * which + slot :][:1]:
                copy.wait()

            def form(part, carry, target=target, source=source, slot=slot):
                duo = (column[0] ^ slot) * PER_CUT + part
                here = pl.ds(pl.multiple_of(part * 384, 128), 384)
                density = target[:, here].astype(F32) * source[:, here].astype(F32)
                for tile, lot in enumerate(lots):
                    lot[pl.ds(duo, ROWS, stride=PITCH), :] = density[:, tile * 128 : (tile + 1) * 128]
                return carry

            lax.fori_loop(0, PER_CUT, form, 0, unroll=12)

        def result(quad, which=which, out=out):
            return pltpu.make_async_copy(out.at[:, quad], far_out.at[:, which, quad], left.at[which, quad])

        def planes(quad, carry, out=out, result=result):
            along_z = []
            for pair in range(2):
                halves = []
                for plane in range(2):
                    rows = pl.ds(pl.multiple_of((quad * 4 + pair * 2 + plane) * PITCH, 8), DUOS)
                    density = tiles(lots, rows).astype(BF16)
                    even = dot(density[:, :256], z_tables[2 * plane])
                    odd = dot(density[:, 128:], z_tables[2 * plane + 1])
                    halves.append(jnp.concatenate([even, odd], axis=0))
                low, high = halves
                along_z += [low[:, :128], high[:, :128], low[:, 128:] + high[:, 128:]]
            along_y = dot(y_table[...], jnp.concatenate(along_z, axis=1).astype(BF16))
            for part in range(PARTS):
                rows = slice(part * ROWS, (part + 1) * ROWS)
                out[part, quad] = jnp.concatenate([along_y[rows, :384], along_y[rows, 384:]], axis=0).astype(BF16)
            result(quad).start()
            return carry

        lax.fori_loop(0, QUADS, planes, 0, unroll=3)
        results += [result(quad) for quad in range(QUADS)]
    for copy in results:
        copy.wait()


def cost(pairs):
    return pl.CostEstimate(flops=pairs * 1400 * 10**6, bytes_accessed=pairs * 7 * 10**6, transcendentals=0)


def forward(column, orbitals, sources):
    cuts = [cut for source in sources for cut in source]
    pairs = len(sources)
    return pl.pallas_call(
        forward_body,
        in_specs=[SCALAR] + [FAR] * (1 + len(cuts)) + [VECTOR] * 2,
        out_specs=FAR,
        out_shape=jax.ShapeDtypeStruct((PARTS, pairs, *PIECE), BF16),
        scratch_shapes=[pltpu.VMEM((ROWS * PITCH, 128), F32)] * 3
        + [pltpu.SemaphoreType.DMA((4 + len(cuts),)), pltpu.SemaphoreType.DMA((pairs, QUADS))]
        + [pltpu.VMEM((ROWS, CUT), BF16)] * (4 + len(cuts))
        + [pltpu.VMEM((PARTS, *PIECE), BF16)] * pairs,
        compiler_params=pltpu.CompilerParams(vmem_limit_bytes=62 * 2**20),
        cost_estimate=cost(pairs),
        name="forward_zy",
    )(column, orbitals, *cuts, jnp.asarray(Z_TABLES, BF16), jnp.asarray(Y_TABLE, BF16))


def middle_body(far_pieces, far_kernel, x_table, x_back, far_out, head0, head1, tail, arrived, left, kernel, *pieces):
    lots = (head0, head1, tail)
    copies = started([(far_pieces.at[:, 0], pieces[0]), (far_kernel, kernel)], arrived)
    copies += [
        pltpu.make_async_copy(far_pieces.at[:, i], piece, arrived.at[1 + i]) for i, piece in enumerate(pieces) if i
    ]
    for copy in copies[2:]:
        copy.start()
    block = QUADS * 2 * ROWS
    low = lax.broadcasted_iota(jnp.int32, (DUOS, 128), 1) < 64

    def step(i, carry):
        here = pl.ds(i, DUOS, stride=ROWS)
        there = pl.ds(i + ROWS // 2, DUOS, stride=ROWS)
        tail_a, tail_b = tail[here, :], tail[there, :]
        tail_first = jnp.where(low, tail_a, pltpu.roll(tail_b, 64, 1))
        tail_second = jnp.where(low, pltpu.roll(tail_a, 64, 1), tail_b)
        columns = jnp.concatenate(
            [
                jnp.concatenate([head0[here, :], head0[there, :], tail_first], axis=1),
                jnp.concatenate([head1[here, :], head1[there, :], tail_second], axis=1),
            ],
            axis=0,
        ).astype(BF16)
        spectrum = (kernel[i] * dot(x_table[...], columns)).astype(BF16)
        back = dot(x_back[...], spectrum)
        head0[here, :] = back[:DUOS, :128]
        head1[here, :] = back[DUOS:, :128]
        head0[there, :] = back[:DUOS, 128:256]
        head1[there, :] = back[DUOS:, 128:256]
        first, second = back[:DUOS, 256:], back[DUOS:, 256:]
        tail[here, :] = jnp.where(low, first, pltpu.roll(second, 64, 1))
        tail[there, :] = jnp.where(low, pltpu.roll(first, 64, 1), second)
        return carry

    results = []
    for which, piece in enumerate(pieces):
        copies[which and 1 + which].wait()
        for part in range(PARTS):
            for tile, lot in enumerate(lots):
                lot[part * block : (part + 1) * block] = (
                    piece[part, :, :, tile * 128 : (tile + 1) * 128].astype(F32).reshape(block, 128)
                )
        if which == 0:
            copies[1].wait()
        lax.fori_loop(0, ROWS // 2, step, 0, unroll=6)
        for part in range(PARTS):
            for tile, lot in enumerate(lots):
                piece[part, :, :, tile * 128 : (tile + 1) * 128] = (
                    lot[part * block : (part + 1) * block].astype(BF16).reshape(QUADS, 2 * ROWS, 128)
                )
        results.append(pltpu.make_async_copy(piece, far_out.at[:, which], left.at[which]))
        results[-1].start()
    for copy in results:
        copy.wait()


def middle(pieces, kernel):
    pairs = pieces.shape[1]
    return pl.pallas_call(
        middle_body,
        in_specs=[FAR, FAR, VECTOR, VECTOR],
        out_specs=FAR,
        out_shape=jax.ShapeDtypeStruct(pieces.shape, BF16),
        scratch_shapes=[pltpu.VMEM((DUOS * ROWS, 128), F32)] * 3
        + [pltpu.SemaphoreType.DMA((1 + pairs,)), pltpu.SemaphoreType.DMA((pairs,)), pltpu.VMEM(kernel.shape, F32)]
        + [pltpu.VMEM((PARTS, *PIECE), BF16)] * pairs,
        compiler_params=pltpu.CompilerParams(vmem_limit_bytes=62 * 2**20),
        cost_estimate=cost(pairs),
        name="middle_x",
    )(pieces, kernel, jnp.asarray(X_TABLE, BF16), jnp.asarray(X_BACK, BF16))


def backward_body(column, far_pieces, *refs):
    pairs = far_pieces.shape[1]
    far_sources, refs = refs[: 4 * pairs], refs[4 * pairs :]
    far_total = refs[0] if len(refs) == 7 + 8 * pairs else None
    y_table, z_tables, far_out, *refs = refs[far_total is not None :]
    (out, arrived, left), refs = refs[:3], refs[3:]
    lots = [refs[3 * i : 3 * i + 3] for i in range(pairs)]
    pieces, sources = refs[3 * pairs : 4 * pairs], refs[4 * pairs :]
    brought = [(far_pieces.at[:, i], piece) for i, piece in enumerate(pieces)] + list(zip(far_sources, sources))
    copies = started(brought + ([] if far_total is None else [(far_total, out)]), arrived)

    for which in range(pairs):
        copies[which].wait()

        def planes(quad, carry, which=which):
            parts = [pieces[which][part, quad].astype(F32) for part in range(PARTS)]
            stacks = [
                jnp.concatenate([part[pair * ROWS : (pair + 1) * ROWS] for part in parts], axis=0) for pair in range(2)
            ]
            both = dot(y_table[...], jnp.concatenate(stacks, axis=1).astype(BF16)).astype(BF16)
            for pair in range(2):
                fields = both[:, pair * 384 : (pair + 1) * 384]
                for plane in range(2):
                    lanes = fields[:, 128:] if plane else jnp.concatenate([fields[:, :128], fields[:, 256:]], axis=1)
                    even = dot(lanes[:DUOS], z_tables[2 * plane])
                    odd = dot(lanes[DUOS:], z_tables[2 * plane + 1])
                    rows = pl.ds(pl.multiple_of((quad * 4 + pair * 2 + plane) * PITCH, 8), DUOS)
                    lots[which][0][rows, :] = even[:, :128]
                    lots[which][1][rows, :] = even[:, 128:] + odd[:, :128]
                    lots[which][2][rows, :] = odd[:, 128:]
            return carry

        lax.fori_loop(0, QUADS, planes, 0, unroll=3)

    for copy in copies[pairs:]:
        copy.wait()
    results = []
    for slot in range(4):

        def gather(part, carry, slot=slot):
            duo = (column[0] ^ slot) * PER_CUT + part
            here = pl.ds(pl.multiple_of(duo * 384, 128), 384)
            there = pl.ds(pl.multiple_of(part * 384, 128), 384)
            term = 0.0 if far_total is None else out[:, here]
            for which in range(pairs):
                potential = tiles(lots[which], pl.ds(duo, ROWS, stride=PITCH))
                term = term - potential * sources[which * 4 + slot][:, there].astype(F32)
            out[:, here] = term
            return carry

        lax.fori_loop(0, PER_CUT, gather, 0, unroll=12)
        here = pl.ds(pl.multiple_of((column[0] ^ slot) * CUT, 128), CUT)
        results.append(pltpu.make_async_copy(out.at[:, here], far_out.at[:, here], left.at[slot]))
        results[-1].start()
    for copy in results:
        copy.wait()


def backward(column, pieces, sources, total):
    cuts = [cut for source in sources for cut in source]
    return pl.pallas_call(
        backward_body,
        in_specs=[SCALAR] + [FAR] * (1 + len(cuts) + (total is not None)) + [VECTOR] * 2,
        out_specs=FAR,
        out_shape=jax.ShapeDtypeStruct((ROWS, CELLS), F32),
        scratch_shapes=[pltpu.VMEM((ROWS, CELLS), F32)]
        + [pltpu.SemaphoreType.DMA((6 * len(sources),)), pltpu.SemaphoreType.DMA((4,))]
        + [pltpu.VMEM((ROWS * PITCH, 128), F32)] * (3 * len(sources))
        + [pltpu.VMEM((PARTS, *PIECE), BF16)] * len(sources)
        + [pltpu.VMEM(cut.shape, BF16) for cut in cuts],
        compiler_params=pltpu.CompilerParams(vmem_limit_bytes=62 * 2**20),
        cost_estimate=cost(len(sources)),
        name="backward_yz",
    )(column, pieces, *cuts, *([] if total is None else [total]), jnp.asarray(Y_BACK, BF16), jnp.asarray(Z_BACKS, BF16))


def exchange(pieces):
    return lax.all_to_all(pieces, "grid", 0, 0, tiled=True)


def band_of(z_hi, x, core):
    return z_hi % 4 * 8 + x * 2 + core


def move(array, pairs):
    return lax.ppermute(array, "band", pairs)


def after(array, *others):
    return lax.optimization_barrier((array, *others))[0]


def scatter(orbitals, which):
    return sum(
        move(
            orbitals[which, :, step * CUT : (step + 1) * CUT],
            [(band_of(2 * root, 0, 0), band_of(2 * root, step, root)) for root in range(2)],
        )
        for step in range(4)
    )


def beside(mine, is_root):
    away = sum(
        move(mine, [(band_of(2 * c, x, c), band_of(2 * c + up, x, c)) for c in range(2) for x in range(4)]) for up in (1, 3)
    )
    return jnp.where(is_root, mine, away)


def along_z(mine, is_root, *others):
    away = sum(
        move(mine, [(band_of(2 * c, x, c), band_of(2 * c + up, x, c)) for c in range(2) for x in range(4)])
        for up in (1, 3, 2)
    )
    return jnp.where(is_root, mine, away)


def beyond(mine):
    half = mine.shape[1] // 2
    parts = [
        move(part, [(band_of(2 * c + up, x, c), band_of(2 * c + 2, x, c)) for c in range(2) for x in range(4)])
        for up, part in ((1, mine[:, :half]), (3, mine[:, half:]))
    ]
    return mine + jnp.concatenate(parts, axis=1)


def gather_x(mine):
    return [mine] + [
        move(mine, [(band_of(z, x, c), band_of(z, x ^ step, c)) for z in range(4) for x in range(4) for c in range(2)])
        for step in range(1, 4)
    ]


def other_core(source):
    pairs = [(band_of(z, x, c), band_of(z, x, 1 - c)) for z in range(4) for x in range(4) for c in range(2)]
    return [move(cut, pairs) for cut in source]


def local(orbitals):
    band = lax.axis_index("band")
    z_hi, x, core = band // 8, (band // 2) % 4, band % 2
    column = x[None].astype(jnp.int32)
    kernel = coulomb(lax.axis_index("grid"))
    is_root = z_hi == 2 * core

    cut_0 = scatter(orbitals, 0)
    cut_1 = scatter(after(orbitals, cut_0), 1)
    near_0 = beside(cut_0, is_root)
    full_0 = beyond(near_0)
    mine_0 = gather_x(full_0)
    batch_0 = [mine_0, other_core(mine_0)]
    pieces_0 = forward(column, orbitals, batch_0)
    full_1 = along_z(after(cut_1, full_0), is_root, pieces_0)
    pieces_0 = after(pieces_0, full_1)
    mine_1 = gather_x(full_1)
    batch_1 = [mine_1, other_core(mine_1)]
    pieces_1 = forward(column, orbitals, batch_1)
    back_0 = exchange(middle(exchange(pieces_0), kernel))
    back_1 = exchange(middle(exchange(pieces_1), kernel))
    total = backward(column, back_0, batch_0, None)
    return backward(column, back_1, batch_1, total)[None]


def solution(mesh):
    return jax.shard_map(
        local,
        mesh=mesh,
        in_specs=(P("band", "grid", None),),
        out_specs=P("band", "grid", None),
        check_vma=False,
    )
```

```python
import jax
import jax.numpy as jnp
import numpy as np
from jax import lax
from jax.experimental import pallas as pl
from jax.experimental.pallas import tpu as pltpu
from jax.sharding import PartitionSpec as P

SIDE = 192
PARTS = 8
ROWS = SIDE // PARTS
QUADS = ROWS // 4
DUOS = SIDE // 2
CELLS = SIDE * SIDE
COUL = 160.0
PITCH = 104
CUT = CELLS // 4
PER_CUT = DUOS // 4
PIECE = (QUADS, 2 * ROWS, 384)
VECTOR = pl.BlockSpec(memory_space=pltpu.VMEM)
FAR = pl.BlockSpec(memory_space=pltpu.HBM)
SCALAR = pl.BlockSpec(memory_space=pltpu.SMEM)
F32 = jnp.float32
BF16 = jnp.bfloat16


def cas_matrix():
    index = np.arange(SIDE, dtype=np.int32)
    phases = (index[:, None] * index[None, :] % SIDE).astype(np.float32) * np.float32(2.0 * np.pi / SIDE)
    return np.cos(phases) + np.sin(phases)


CAS = cas_matrix()
BY_PARITY = np.concatenate([np.arange(0, SIDE, 2), np.arange(1, SIDE, 2)])
Y_TABLE = CAS[:, BY_PARITY]
Y_BACK = CAS[BY_PARITY, :]
X_TABLE = CAS[:, BY_PARITY]
X_BACK = CAS[BY_PARITY, :]


def z_tables():
    gap = np.zeros((64, 256), np.float32)
    space = np.zeros((SIDE, 64), np.float32)
    first = np.concatenate([CAS, space], axis=1)
    second = np.concatenate([CAS[:, :128], space, CAS[:, 128:]], axis=1)
    return np.stack([np.concatenate(part, axis=0) for table in (first, second) for part in ((table, gap), (gap, table))])


Z_TABLES = z_tables()
Z_BACKS = np.swapaxes(Z_TABLES, 1, 2)


def wave(index):
    return jnp.where(index < SIDE // 2, index, index - SIDE).astype(F32)


def coulomb(me):
    shape = (ROWS // 2, SIDE, 384)
    pair = lax.broadcasted_iota(jnp.int32, shape, 0)
    row = lax.broadcasted_iota(jnp.int32, shape, 1)
    col = lax.broadcasted_iota(jnp.int32, shape, 2)
    late = jnp.where(col < 256, col >= 128, col >= 320)
    kz = jnp.where(col < 256, col % 128, 128 + col % 64)
    ky = me * ROWS + pair + jnp.where(late, ROWS // 2, 0)
    mx, my, mz = wave(row), wave(ky), wave(kz)
    norm_sq = mx * mx + my * my + mz * mz
    bounded = jnp.maximum(norm_sq, 1.0)
    return jnp.where(norm_sq > 0.5, COUL / bounded, 0.0) / float(SIDE) ** 3


def dot(left, right):
    return jnp.dot(left, right, preferred_element_type=F32)


def tiles(lots, rows):
    return jnp.concatenate([lot[rows, :] for lot in lots], axis=1)


def started(pairs, semaphores):
    copies = [pltpu.make_async_copy(a, b, semaphores.at[i]) for i, (a, b) in enumerate(pairs)]
    for copy in copies:
        copy.start()
    return copies


def forward_body(column, far_orbitals, *refs):
    pairs = (len(refs) - 12) // 9
    far_sources, (z_tables, y_table, far_out), refs = refs[: 4 * pairs], refs[4 * pairs : 4 * pairs + 3], refs[4 * pairs + 3 :]
    lots, (arrived, left), targets, refs = refs[:3], refs[3:5], refs[5:9], refs[9:]
    sources, outs = refs[: 4 * pairs], refs[4 * pairs :]
    brought = []
    for slot in range(4):
        here = pl.ds(pl.multiple_of((column[0] ^ slot) * CUT, 128), CUT)
        brought += [(far_orbitals.at[0, :, here], targets[slot]), (far_sources[slot], sources[slot])]
    copies = started(brought + list(zip(far_sources[4:], sources[4:])), arrived)
    results = []
    for which, out in enumerate(outs):
        for slot in range(4):
            target, source = targets[slot], sources[4 * which + slot]
            for copy in copies[2 * slot : 2 * slot + 2] if which == 0 else copies[4 + 4 * which + slot :][:1]:
                copy.wait()

            def form(part, carry, target=target, source=source, slot=slot):
                duo = (column[0] ^ slot) * PER_CUT + part
                here = pl.ds(pl.multiple_of(part * 384, 128), 384)
                density = target[:, here].astype(F32) * source[:, here].astype(F32)
                for tile, lot in enumerate(lots):
                    lot[pl.ds(duo, ROWS, stride=PITCH), :] = density[:, tile * 128 : (tile + 1) * 128]
                return carry

            lax.fori_loop(0, PER_CUT, form, 0, unroll=12)

        def result(quad, which=which, out=out):
            return pltpu.make_async_copy(out.at[:, quad], far_out.at[:, which, quad], left.at[which, quad])

        def planes(quad, carry, out=out, result=result):
            along_z = []
            for pair in range(2):
                halves = []
                for plane in range(2):
                    rows = pl.ds(pl.multiple_of((quad * 4 + pair * 2 + plane) * PITCH, 8), DUOS)
                    density = tiles(lots, rows).astype(BF16)
                    even = dot(density[:, :256], z_tables[2 * plane])
                    odd = dot(density[:, 128:], z_tables[2 * plane + 1])
                    halves.append(jnp.concatenate([even, odd], axis=0))
                low, high = halves
                along_z += [low[:, :128], high[:, :128], low[:, 128:] + high[:, 128:]]
            along_y = dot(y_table[...], jnp.concatenate(along_z, axis=1).astype(BF16))
            for part in range(PARTS):
                rows = slice(part * ROWS, (part + 1) * ROWS)
                out[part, quad] = jnp.concatenate([along_y[rows, :384], along_y[rows, 384:]], axis=0).astype(BF16)
            result(quad).start()
            return carry

        lax.fori_loop(0, QUADS, planes, 0, unroll=3)
        results += [result(quad) for quad in range(QUADS)]
    for copy in results:
        copy.wait()


def cost(pairs):
    return pl.CostEstimate(flops=pairs * 1400 * 10**6, bytes_accessed=pairs * 7 * 10**6, transcendentals=0)


def forward(column, orbitals, sources):
    cuts = [cut for source in sources for cut in source]
    pairs = len(sources)
    return pl.pallas_call(
        forward_body,
        in_specs=[SCALAR] + [FAR] * (1 + len(cuts)) + [VECTOR] * 2,
        out_specs=FAR,
        out_shape=jax.ShapeDtypeStruct((PARTS, pairs, *PIECE), BF16),
        scratch_shapes=[pltpu.VMEM((ROWS * PITCH, 128), F32)] * 3
        + [pltpu.SemaphoreType.DMA((4 + len(cuts),)), pltpu.SemaphoreType.DMA((pairs, QUADS))]
        + [pltpu.VMEM((ROWS, CUT), BF16)] * (4 + len(cuts))
        + [pltpu.VMEM((PARTS, *PIECE), BF16)] * pairs,
        compiler_params=pltpu.CompilerParams(vmem_limit_bytes=62 * 2**20),
        cost_estimate=cost(pairs),
        name="forward_zy",
    )(column, orbitals, *cuts, jnp.asarray(Z_TABLES, BF16), jnp.asarray(Y_TABLE, BF16))


def middle_body(far_pieces, far_kernel, x_table, x_back, far_out, head0, head1, tail, arrived, left, kernel, *pieces):
    lots = (head0, head1, tail)
    copies = started([(far_pieces.at[:, 0], pieces[0]), (far_kernel, kernel)], arrived)
    copies += [
        pltpu.make_async_copy(far_pieces.at[:, i], piece, arrived.at[1 + i]) for i, piece in enumerate(pieces) if i
    ]
    for copy in copies[2:]:
        copy.start()
    block = QUADS * 2 * ROWS
    low = lax.broadcasted_iota(jnp.int32, (DUOS, 128), 1) < 64

    def step(i, carry):
        here = pl.ds(i, DUOS, stride=ROWS)
        there = pl.ds(i + ROWS // 2, DUOS, stride=ROWS)
        tail_a, tail_b = tail[here, :], tail[there, :]
        tail_first = jnp.where(low, tail_a, pltpu.roll(tail_b, 64, 1))
        tail_second = jnp.where(low, pltpu.roll(tail_a, 64, 1), tail_b)
        columns = jnp.concatenate(
            [
                jnp.concatenate([head0[here, :], head0[there, :], tail_first], axis=1),
                jnp.concatenate([head1[here, :], head1[there, :], tail_second], axis=1),
            ],
            axis=0,
        ).astype(BF16)
        spectrum = (kernel[i] * dot(x_table[...], columns)).astype(BF16)
        back = dot(x_back[...], spectrum)
        head0[here, :] = back[:DUOS, :128]
        head1[here, :] = back[DUOS:, :128]
        head0[there, :] = back[:DUOS, 128:256]
        head1[there, :] = back[DUOS:, 128:256]
        first, second = back[:DUOS, 256:], back[DUOS:, 256:]
        tail[here, :] = jnp.where(low, first, pltpu.roll(second, 64, 1))
        tail[there, :] = jnp.where(low, pltpu.roll(first, 64, 1), second)
        return carry

    results = []
    for which, piece in enumerate(pieces):
        copies[which and 1 + which].wait()
        for part in range(PARTS):
            for tile, lot in enumerate(lots):
                lot[part * block : (part + 1) * block] = (
                    piece[part, :, :, tile * 128 : (tile + 1) * 128].astype(F32).reshape(block, 128)
                )
        if which == 0:
            copies[1].wait()
        lax.fori_loop(0, ROWS // 2, step, 0, unroll=6)
        for part in range(PARTS):
            for tile, lot in enumerate(lots):
                piece[part, :, :, tile * 128 : (tile + 1) * 128] = (
                    lot[part * block : (part + 1) * block].astype(BF16).reshape(QUADS, 2 * ROWS, 128)
                )
        results.append(pltpu.make_async_copy(piece, far_out.at[:, which], left.at[which]))
        results[-1].start()
    for copy in results:
        copy.wait()


def middle(pieces, kernel):
    pairs = pieces.shape[1]
    return pl.pallas_call(
        middle_body,
        in_specs=[FAR, FAR, VECTOR, VECTOR],
        out_specs=FAR,
        out_shape=jax.ShapeDtypeStruct(pieces.shape, BF16),
        scratch_shapes=[pltpu.VMEM((DUOS * ROWS, 128), F32)] * 3
        + [pltpu.SemaphoreType.DMA((1 + pairs,)), pltpu.SemaphoreType.DMA((pairs,)), pltpu.VMEM(kernel.shape, F32)]
        + [pltpu.VMEM((PARTS, *PIECE), BF16)] * pairs,
        compiler_params=pltpu.CompilerParams(vmem_limit_bytes=62 * 2**20),
        cost_estimate=cost(pairs),
        name="middle_x",
    )(pieces, kernel, jnp.asarray(X_TABLE, BF16), jnp.asarray(X_BACK, BF16))


def backward_body(column, far_pieces, *refs):
    pairs = far_pieces.shape[1]
    far_sources, refs = refs[: 4 * pairs], refs[4 * pairs :]
    far_total = refs[0] if len(refs) == 7 + 8 * pairs else None
    y_table, z_tables, far_out, *refs = refs[far_total is not None :]
    (out, arrived, left), refs = refs[:3], refs[3:]
    lots = [refs[3 * i : 3 * i + 3] for i in range(pairs)]
    pieces, sources = refs[3 * pairs : 4 * pairs], refs[4 * pairs :]
    brought = [(far_pieces.at[:, i], piece) for i, piece in enumerate(pieces)] + list(zip(far_sources, sources))
    copies = started(brought + ([] if far_total is None else [(far_total, out)]), arrived)

    for which in range(pairs):
        copies[which].wait()

        def planes(quad, carry, which=which):
            parts = [pieces[which][part, quad].astype(F32) for part in range(PARTS)]
            stacks = [
                jnp.concatenate([part[pair * ROWS : (pair + 1) * ROWS] for part in parts], axis=0) for pair in range(2)
            ]
            both = dot(y_table[...], jnp.concatenate(stacks, axis=1).astype(BF16)).astype(BF16)
            for pair in range(2):
                fields = both[:, pair * 384 : (pair + 1) * 384]
                for plane in range(2):
                    lanes = fields[:, 128:] if plane else jnp.concatenate([fields[:, :128], fields[:, 256:]], axis=1)
                    even = dot(lanes[:DUOS], z_tables[2 * plane])
                    odd = dot(lanes[DUOS:], z_tables[2 * plane + 1])
                    rows = pl.ds(pl.multiple_of((quad * 4 + pair * 2 + plane) * PITCH, 8), DUOS)
                    lots[which][0][rows, :] = even[:, :128]
                    lots[which][1][rows, :] = even[:, 128:] + odd[:, :128]
                    lots[which][2][rows, :] = odd[:, 128:]
            return carry

        lax.fori_loop(0, QUADS, planes, 0, unroll=3)

    for copy in copies[pairs:]:
        copy.wait()
    results = []
    for slot in range(4):

        def gather(part, carry, slot=slot):
            duo = (column[0] ^ slot) * PER_CUT + part
            here = pl.ds(pl.multiple_of(duo * 384, 128), 384)
            there = pl.ds(pl.multiple_of(part * 384, 128), 384)
            term = 0.0 if far_total is None else out[:, here]
            for which in range(pairs):
                potential = tiles(lots[which], pl.ds(duo, ROWS, stride=PITCH))
                term = term - potential * sources[which * 4 + slot][:, there].astype(F32)
            out[:, here] = term
            return carry

        lax.fori_loop(0, PER_CUT, gather, 0, unroll=12)
        here = pl.ds(pl.multiple_of((column[0] ^ slot) * CUT, 128), CUT)
        results.append(pltpu.make_async_copy(out.at[:, here], far_out.at[:, here], left.at[slot]))
        results[-1].start()
    for copy in results:
        copy.wait()


def backward(column, pieces, sources, total):
    cuts = [cut for source in sources for cut in source]
    return pl.pallas_call(
        backward_body,
        in_specs=[SCALAR] + [FAR] * (1 + len(cuts) + (total is not None)) + [VECTOR] * 2,
        out_specs=FAR,
        out_shape=jax.ShapeDtypeStruct((ROWS, CELLS), F32),
        scratch_shapes=[pltpu.VMEM((ROWS, CELLS), F32)]
        + [pltpu.SemaphoreType.DMA((6 * len(sources),)), pltpu.SemaphoreType.DMA((4,))]
        + [pltpu.VMEM((ROWS * PITCH, 128), F32)] * (3 * len(sources))
        + [pltpu.VMEM((PARTS, *PIECE), BF16)] * len(sources)
        + [pltpu.VMEM(cut.shape, BF16) for cut in cuts],
        compiler_params=pltpu.CompilerParams(vmem_limit_bytes=62 * 2**20),
        cost_estimate=cost(len(sources)),
        name="backward_yz",
    )(column, pieces, *cuts, *([] if total is None else [total]), jnp.asarray(Y_BACK, BF16), jnp.asarray(Z_BACKS, BF16))


def exchange(pieces):
    return lax.all_to_all(pieces, "grid", 0, 0, tiled=True)


def band_of(z_hi, x, core):
    return z_hi % 4 * 8 + x * 2 + core


def move(array, pairs):
    return lax.ppermute(array, "band", pairs)


def after(array, *others):
    return lax.optimization_barrier((array, *others))[0]


def to_x(cut, step):
    return move(cut, [(band_of(2 * root, 0, 0), band_of(2 * root, step, root)) for root in range(2)])


def scatter(orbitals, which, first):
    return first + sum(to_x(orbitals[which, :, step * CUT : (step + 1) * CUT], step) for step in range(1, 4))


def beside(mine, is_root):
    away = sum(
        move(mine, [(band_of(2 * c, x, c), band_of(2 * c + up, x, c)) for c in range(2) for x in range(4)]) for up in (1, 3)
    )
    return jnp.where(is_root, mine, away)


def along_z(mine, is_root, *others):
    away = sum(
        move(mine, [(band_of(2 * c, x, c), band_of(2 * c + up, x, c)) for c in range(2) for x in range(4)])
        for up in (1, 3, 2)
    )
    return jnp.where(is_root, mine, away)


def beyond(mine):
    half = mine.shape[1] // 2
    parts = [
        move(part, [(band_of(2 * c + up, x, c), band_of(2 * c + 2, x, c)) for c in range(2) for x in range(4)])
        for up, part in ((1, mine[:, :half]), (3, mine[:, half:]))
    ]
    return mine + jnp.concatenate(parts, axis=1)


def gather_x(mine):
    return [mine] + [
        move(mine, [(band_of(z, x, c), band_of(z, x ^ step, c)) for z in range(4) for x in range(4) for c in range(2)])
        for step in range(1, 4)
    ]


def other_core(source):
    pairs = [(band_of(z, x, c), band_of(z, x, 1 - c)) for z in range(4) for x in range(4) for c in range(2)]
    return [move(cut, pairs) for cut in source]


def local(orbitals):
    band = lax.axis_index("band")
    z_hi, x, core = band // 8, (band // 2) % 4, band % 2
    column = x[None].astype(jnp.int32)
    kernel = coulomb(lax.axis_index("grid"))
    is_root = z_hi == 2 * core

    first = to_x(orbitals[:, :, :CUT], 0)
    cut_0 = scatter(orbitals, 0, first[0])
    cut_1 = scatter(after(orbitals, cut_0), 1, first[1])
    near_0 = beside(cut_0, is_root)
    full_0 = beyond(near_0)
    mine_0 = gather_x(full_0)
    batch_0 = [mine_0, other_core(mine_0)]
    pieces_0 = forward(column, orbitals, batch_0)
    full_1 = along_z(after(cut_1, full_0), is_root, pieces_0)
    pieces_0 = after(pieces_0, full_1)
    mine_1 = gather_x(full_1)
    batch_1 = [mine_1, other_core(mine_1)]
    pieces_1 = forward(column, orbitals, batch_1)
    back_0 = exchange(middle(exchange(pieces_0), kernel))
    back_1 = exchange(middle(exchange(pieces_1), kernel))
    total = backward(column, back_0, batch_0, None)
    return backward(column, back_1, batch_1, total)[None]


def solution(mesh):
    return jax.shard_map(
        local,
        mesh=mesh,
        in_specs=(P("band", "grid", None),),
        out_specs=P("band", "grid", None),
        check_vma=False,
    )
```

```python
import jax
import jax.numpy as jnp
import numpy as np
from jax import lax
from jax.experimental import pallas as pl
from jax.experimental.pallas import tpu as pltpu
from jax.sharding import PartitionSpec as P

SIDE = 192
PARTS = 8
ROWS = SIDE // PARTS
QUADS = ROWS // 4
DUOS = SIDE // 2
CELLS = SIDE * SIDE
COUL = 160.0
PITCH = 104
CUT = CELLS // 4
PER_CUT = DUOS // 4
PIECE = (QUADS, 2 * ROWS, 384)
VECTOR = pl.BlockSpec(memory_space=pltpu.VMEM)
FAR = pl.BlockSpec(memory_space=pltpu.HBM)
SCALAR = pl.BlockSpec(memory_space=pltpu.SMEM)
F32 = jnp.float32
BF16 = jnp.bfloat16


def cas_matrix():
    index = np.arange(SIDE, dtype=np.int32)
    phases = (index[:, None] * index[None, :] % SIDE).astype(np.float32) * np.float32(2.0 * np.pi / SIDE)
    return np.cos(phases) + np.sin(phases)


CAS = cas_matrix()
BY_PARITY = np.concatenate([np.arange(0, SIDE, 2), np.arange(1, SIDE, 2)])
Y_TABLE = CAS[:, BY_PARITY]
Y_BACK = CAS[BY_PARITY, :]
X_TABLE = CAS[:, BY_PARITY]
X_BACK = CAS[BY_PARITY, :]


def z_tables():
    gap = np.zeros((64, 256), np.float32)
    space = np.zeros((SIDE, 64), np.float32)
    first = np.concatenate([CAS, space], axis=1)
    second = np.concatenate([CAS[:, :128], space, CAS[:, 128:]], axis=1)
    return np.stack([np.concatenate(part, axis=0) for table in (first, second) for part in ((table, gap), (gap, table))])


Z_TABLES = z_tables()
Z_BACKS = np.swapaxes(Z_TABLES, 1, 2)


def wave(index):
    return jnp.where(index < SIDE // 2, index, index - SIDE).astype(F32)


def coulomb(me):
    shape = (ROWS // 2, SIDE, 384)
    pair = lax.broadcasted_iota(jnp.int32, shape, 0)
    row = lax.broadcasted_iota(jnp.int32, shape, 1)
    col = lax.broadcasted_iota(jnp.int32, shape, 2)
    late = jnp.where(col < 256, col >= 128, col >= 320)
    kz = jnp.where(col < 256, col % 128, 128 + col % 64)
    ky = me * ROWS + pair + jnp.where(late, ROWS // 2, 0)
    mx, my, mz = wave(row), wave(ky), wave(kz)
    norm_sq = mx * mx + my * my + mz * mz
    bounded = jnp.maximum(norm_sq, 1.0)
    return jnp.where(norm_sq > 0.5, COUL / bounded, 0.0) / float(SIDE) ** 3


def dot(left, right):
    return jnp.dot(left, right, preferred_element_type=F32)


def tiles(lots, rows):
    return jnp.concatenate([lot[rows, :] for lot in lots], axis=1)


def started(pairs, semaphores):
    copies = [pltpu.make_async_copy(a, b, semaphores.at[i]) for i, (a, b) in enumerate(pairs)]
    for copy in copies:
        copy.start()
    return copies


def forward_body(column, far_orbitals, *refs):
    pairs = (len(refs) - 12) // 9
    far_sources, (z_tables, y_table, far_out), refs = refs[: 4 * pairs], refs[4 * pairs : 4 * pairs + 3], refs[4 * pairs + 3 :]
    lots, (arrived, left), targets, refs = refs[:3], refs[3:5], refs[5:9], refs[9:]
    sources, outs = refs[: 4 * pairs], refs[4 * pairs :]
    brought = []
    for slot in range(4):
        here = pl.ds(pl.multiple_of((column[0] ^ slot) * CUT, 128), CUT)
        brought += [(far_orbitals.at[0, :, here], targets[slot]), (far_sources[slot], sources[slot])]
    copies = started(brought + list(zip(far_sources[4:], sources[4:])), arrived)
    results = []
    for which, out in enumerate(outs):
        for slot in range(4):
            target, source = targets[slot], sources[4 * which + slot]
            for copy in copies[2 * slot : 2 * slot + 2] if which == 0 else copies[4 + 4 * which + slot :][:1]:
                copy.wait()

            def form(part, carry, target=target, source=source, slot=slot):
                duo = (column[0] ^ slot) * PER_CUT + part
                here = pl.ds(pl.multiple_of(part * 384, 128), 384)
                density = target[:, here].astype(F32) * source[:, here].astype(F32)
                for tile, lot in enumerate(lots):
                    lot[pl.ds(duo, ROWS, stride=PITCH), :] = density[:, tile * 128 : (tile + 1) * 128]
                return carry

            lax.fori_loop(0, PER_CUT, form, 0, unroll=12)

        def result(quad, which=which, out=out):
            return pltpu.make_async_copy(out.at[:, quad], far_out.at[:, which, quad], left.at[which, quad])

        def planes(quad, carry, out=out, result=result):
            along_z = []
            for pair in range(2):
                halves = []
                for plane in range(2):
                    rows = pl.ds(pl.multiple_of((quad * 4 + pair * 2 + plane) * PITCH, 8), DUOS)
                    density = tiles(lots, rows).astype(BF16)
                    even = dot(density[:, :256], z_tables[2 * plane])
                    odd = dot(density[:, 128:], z_tables[2 * plane + 1])
                    halves.append(jnp.concatenate([even, odd], axis=0))
                low, high = halves
                along_z += [low[:, :128], high[:, :128], low[:, 128:] + high[:, 128:]]
            along_y = dot(y_table[...], jnp.concatenate(along_z, axis=1).astype(BF16))
            for part in range(PARTS):
                rows = slice(part * ROWS, (part + 1) * ROWS)
                out[part, quad] = jnp.concatenate([along_y[rows, :384], along_y[rows, 384:]], axis=0).astype(BF16)
            result(quad).start()
            return carry

        lax.fori_loop(0, QUADS, planes, 0, unroll=3)
        results += [result(quad) for quad in range(QUADS)]
    for copy in results:
        copy.wait()


def cost(pairs):
    return pl.CostEstimate(flops=pairs * 1400 * 10**6, bytes_accessed=pairs * 7 * 10**6, transcendentals=0)


def forward(column, orbitals, sources):
    cuts = [cut for source in sources for cut in source]
    pairs = len(sources)
    return pl.pallas_call(
        forward_body,
        in_specs=[SCALAR] + [FAR] * (1 + len(cuts)) + [VECTOR] * 2,
        out_specs=FAR,
        out_shape=jax.ShapeDtypeStruct((PARTS, pairs, *PIECE), BF16),
        scratch_shapes=[pltpu.VMEM((ROWS * PITCH, 128), F32)] * 3
        + [pltpu.SemaphoreType.DMA((4 + len(cuts),)), pltpu.SemaphoreType.DMA((pairs, QUADS))]
        + [pltpu.VMEM((ROWS, CUT), BF16)] * (4 + len(cuts))
        + [pltpu.VMEM((PARTS, *PIECE), BF16)] * pairs,
        compiler_params=pltpu.CompilerParams(vmem_limit_bytes=62 * 2**20),
        cost_estimate=cost(pairs),
        name="forward_zy",
    )(column, orbitals, *cuts, jnp.asarray(Z_TABLES, BF16), jnp.asarray(Y_TABLE, BF16))


def middle_body(far_pieces, far_kernel, x_table, x_back, far_out, head0, head1, tail, arrived, left, kernel, *pieces):
    lots = (head0, head1, tail)
    copies = started([(far_pieces.at[:, 0], pieces[0]), (far_kernel, kernel)], arrived)
    copies += [
        pltpu.make_async_copy(far_pieces.at[:, i], piece, arrived.at[1 + i]) for i, piece in enumerate(pieces) if i
    ]
    for copy in copies[2:]:
        copy.start()
    block = QUADS * 2 * ROWS
    low = lax.broadcasted_iota(jnp.int32, (DUOS, 128), 1) < 64

    def step(i, carry):
        here = pl.ds(i, DUOS, stride=ROWS)
        there = pl.ds(i + ROWS // 2, DUOS, stride=ROWS)
        tail_a, tail_b = tail[here, :], tail[there, :]
        tail_first = jnp.where(low, tail_a, pltpu.roll(tail_b, 64, 1))
        tail_second = jnp.where(low, pltpu.roll(tail_a, 64, 1), tail_b)
        columns = jnp.concatenate(
            [
                jnp.concatenate([head0[here, :], head0[there, :], tail_first], axis=1),
                jnp.concatenate([head1[here, :], head1[there, :], tail_second], axis=1),
            ],
            axis=0,
        ).astype(BF16)
        spectrum = (kernel[i] * dot(x_table[...], columns)).astype(BF16)
        back = dot(x_back[...], spectrum)
        head0[here, :] = back[:DUOS, :128]
        head1[here, :] = back[DUOS:, :128]
        head0[there, :] = back[:DUOS, 128:256]
        head1[there, :] = back[DUOS:, 128:256]
        first, second = back[:DUOS, 256:], back[DUOS:, 256:]
        tail[here, :] = jnp.where(low, first, pltpu.roll(second, 64, 1))
        tail[there, :] = jnp.where(low, pltpu.roll(first, 64, 1), second)
        return carry

    results = []
    for which, piece in enumerate(pieces):
        copies[which and 1 + which].wait()
        for part in range(PARTS):
            for tile, lot in enumerate(lots):
                lot[part * block : (part + 1) * block] = (
                    piece[part, :, :, tile * 128 : (tile + 1) * 128].astype(F32).reshape(block, 128)
                )
        if which == 0:
            copies[1].wait()
        lax.fori_loop(0, ROWS // 2, step, 0, unroll=6)
        for part in range(PARTS):
            for tile, lot in enumerate(lots):
                piece[part, :, :, tile * 128 : (tile + 1) * 128] = (
                    lot[part * block : (part + 1) * block].astype(BF16).reshape(QUADS, 2 * ROWS, 128)
                )
        results.append(pltpu.make_async_copy(piece, far_out.at[:, which], left.at[which]))
        results[-1].start()
    for copy in results:
        copy.wait()


def middle(pieces, kernel):
    pairs = pieces.shape[1]
    return pl.pallas_call(
        middle_body,
        in_specs=[FAR, FAR, VECTOR, VECTOR],
        out_specs=FAR,
        out_shape=jax.ShapeDtypeStruct(pieces.shape, BF16),
        scratch_shapes=[pltpu.VMEM((DUOS * ROWS, 128), F32)] * 3
        + [pltpu.SemaphoreType.DMA((1 + pairs,)), pltpu.SemaphoreType.DMA((pairs,)), pltpu.VMEM(kernel.shape, F32)]
        + [pltpu.VMEM((PARTS, *PIECE), BF16)] * pairs,
        compiler_params=pltpu.CompilerParams(vmem_limit_bytes=62 * 2**20),
        cost_estimate=cost(pairs),
        name="middle_x",
    )(pieces, kernel, jnp.asarray(X_TABLE, BF16), jnp.asarray(X_BACK, BF16))


def backward_body(column, far_pieces, *refs):
    pairs = far_pieces.shape[1]
    far_sources, refs = refs[: 4 * pairs], refs[4 * pairs :]
    far_total = refs[0] if len(refs) == 7 + 8 * pairs else None
    y_table, z_tables, far_out, *refs = refs[far_total is not None :]
    (out, arrived, left), refs = refs[:3], refs[3:]
    lots = [refs[3 * i : 3 * i + 3] for i in range(pairs)]
    pieces, sources = refs[3 * pairs : 4 * pairs], refs[4 * pairs :]
    brought = [(far_pieces.at[:, i], piece) for i, piece in enumerate(pieces)] + list(zip(far_sources, sources))
    copies = started(brought + ([] if far_total is None else [(far_total, out)]), arrived)

    for which in range(pairs):
        copies[which].wait()

        def planes(quad, carry, which=which):
            parts = [pieces[which][part, quad].astype(F32) for part in range(PARTS)]
            stacks = [
                jnp.concatenate([part[pair * ROWS : (pair + 1) * ROWS] for part in parts], axis=0) for pair in range(2)
            ]
            both = dot(y_table[...], jnp.concatenate(stacks, axis=1).astype(BF16)).astype(BF16)
            for pair in range(2):
                fields = both[:, pair * 384 : (pair + 1) * 384]
                for plane in range(2):
                    lanes = fields[:, 128:] if plane else jnp.concatenate([fields[:, :128], fields[:, 256:]], axis=1)
                    even = dot(lanes[:DUOS], z_tables[2 * plane])
                    odd = dot(lanes[DUOS:], z_tables[2 * plane + 1])
                    rows = pl.ds(pl.multiple_of((quad * 4 + pair * 2 + plane) * PITCH, 8), DUOS)
                    lots[which][0][rows, :] = even[:, :128]
                    lots[which][1][rows, :] = even[:, 128:] + odd[:, :128]
                    lots[which][2][rows, :] = odd[:, 128:]
            return carry

        lax.fori_loop(0, QUADS, planes, 0, unroll=3)

    for copy in copies[pairs:]:
        copy.wait()
    results = []
    for slot in range(4):

        def gather(part, carry, slot=slot):
            duo = (column[0] ^ slot) * PER_CUT + part
            here = pl.ds(pl.multiple_of(duo * 384, 128), 384)
            there = pl.ds(pl.multiple_of(part * 384, 128), 384)
            term = 0.0 if far_total is None else out[:, here]
            for which in range(pairs):
                potential = tiles(lots[which], pl.ds(duo, ROWS, stride=PITCH))
                term = term - potential * sources[which * 4 + slot][:, there].astype(F32)
            out[:, here] = term
            return carry

        lax.fori_loop(0, PER_CUT, gather, 0, unroll=12)
        here = pl.ds(pl.multiple_of((column[0] ^ slot) * CUT, 128), CUT)
        results.append(pltpu.make_async_copy(out.at[:, here], far_out.at[:, here], left.at[slot]))
        results[-1].start()
    for copy in results:
        copy.wait()


def backward(column, pieces, sources, total):
    cuts = [cut for source in sources for cut in source]
    return pl.pallas_call(
        backward_body,
        in_specs=[SCALAR] + [FAR] * (1 + len(cuts) + (total is not None)) + [VECTOR] * 2,
        out_specs=FAR,
        out_shape=jax.ShapeDtypeStruct((ROWS, CELLS), F32),
        scratch_shapes=[pltpu.VMEM((ROWS, CELLS), F32)]
        + [pltpu.SemaphoreType.DMA((6 * len(sources),)), pltpu.SemaphoreType.DMA((4,))]
        + [pltpu.VMEM((ROWS * PITCH, 128), F32)] * (3 * len(sources))
        + [pltpu.VMEM((PARTS, *PIECE), BF16)] * len(sources)
        + [pltpu.VMEM(cut.shape, BF16) for cut in cuts],
        compiler_params=pltpu.CompilerParams(vmem_limit_bytes=62 * 2**20),
        cost_estimate=cost(len(sources)),
        name="backward_yz",
    )(column, pieces, *cuts, *([] if total is None else [total]), jnp.asarray(Y_BACK, BF16), jnp.asarray(Z_BACKS, BF16))


def exchange(pieces):
    return lax.all_to_all(pieces, "grid", 0, 0, tiled=True)


def band_of(z_hi, x, core):
    return z_hi % 4 * 8 + x * 2 + core


def move(array, pairs):
    return lax.ppermute(array, "band", pairs)


def after(array, *others):
    return lax.optimization_barrier((array, *others))[0]


def to_x(cut, step):
    return move(cut, [(band_of(2 * root, 0, 0), band_of(2 * root, step, root)) for root in range(2)])


def scatter(orbitals, which, first):
    return first + sum(to_x(orbitals[which, :, step * CUT : (step + 1) * CUT], step) for step in range(1, 4))


def along_z(mine, is_root):
    away = sum(
        move(mine, [(band_of(2 * c, x, c), band_of(2 * c + up, x, c)) for c in range(2) for x in range(4)])
        for up in (1, 3, 2)
    )
    return jnp.where(is_root, mine, away)


def beyond(mine):
    half = mine.shape[1] // 2
    parts = [
        move(part, [(band_of(2 * c + up, x, c), band_of(2 * c + 2, x, c)) for c in range(2) for x in range(4)])
        for up, part in ((1, mine[:, :half]), (3, mine[:, half:]))
    ]
    return mine + jnp.concatenate(parts, axis=1)


def gather_x(mine):
    return [mine] + [
        move(mine, [(band_of(z, x, c), band_of(z, x ^ step, c)) for z in range(4) for x in range(4) for c in range(2)])
        for step in range(1, 4)
    ]


def other_core(source):
    pairs = [(band_of(z, x, c), band_of(z, x, 1 - c)) for z in range(4) for x in range(4) for c in range(2)]
    return [move(cut, pairs) for cut in source]


def local(orbitals):
    band = lax.axis_index("band")
    z_hi, x, core = band // 8, (band // 2) % 4, band % 2
    column = x[None].astype(jnp.int32)
    kernel = coulomb(lax.axis_index("grid"))
    is_root = z_hi == 2 * core

    first = to_x(orbitals[:, :, :CUT], 0)
    cut_0 = scatter(orbitals, 0, first[0])
    cut_1 = scatter(after(orbitals, cut_0), 1, first[1])
    full_0 = along_z(cut_0, is_root)
    mine_0 = gather_x(full_0)
    batch_0 = [mine_0, other_core(mine_0)]
    pieces_0 = forward(column, orbitals, batch_0)
    full_1 = along_z(after(cut_1, full_0), is_root)
    pieces_0 = after(pieces_0, full_1)
    mine_1 = gather_x(full_1)
    batch_1 = [mine_1, other_core(mine_1)]
    pieces_1 = forward(column, orbitals, batch_1)
    back_0 = exchange(middle(exchange(pieces_0), kernel))
    back_1 = exchange(middle(exchange(pieces_1), kernel))
    total = backward(column, back_0, batch_0, None)
    return backward(column, back_1, batch_1, total)[None]


def solution(mesh):
    return jax.shard_map(
        local,
        mesh=mesh,
        in_specs=(P("band", "grid", None),),
        out_specs=P("band", "grid", None),
        check_vma=False,
    )
```
